256 devices in a mesh: sec: 32 (over z, x), tile: 8 (over y, core).
Axes of the slice: x: 4, y: 4, z: 8, core: 2. Of those that a mesh axis runs over, the one named last changes fastest.
Arguments:
- ov_first: int32 [32768], P(('sec', 'tile')), may hold values from 0 to 8191, as said below
- ov_second: int32 [32768], P(('sec', 'tile')), may hold values from 0 to 8191, as said below
- match_count: int32 [32768], P(('sec', 'tile')), may hold values from 1 to 32, as said below
- cell_first: int32 [32, 32768], P(None, ('sec', 'tile')), may hold values from 0 to 48
- cell_second: int32 [32, 32768], P(None, ('sec', 'tile')), may hold values from 0 to 48
- frac_first: float32 [2, 32, 32768], P(None, None, ('sec', 'tile')), may hold values from 0 to 1
- frac_second: float32 [2, 32, 32768], P(None, None, ('sec', 'tile')), may hold values from 0 to 1
- target: float32 [2, 32, 32768], P(None, None, ('sec', 'tile')), may hold values from -6 to 6
- stiffness: float32 [256, 32], P('tile', 'sec'), may hold values from 0.3 to 3
Outputs:
- solution_field: float32 [256, 32, 128], P('tile', 'sec')
- residual: float32 [256, 32, 128], P('tile', 'sec')
The draws below stay inside these ranges and needn't reach their ends.
Inputs may be any that keep to these rules, and one draw needn't show every extreme that they name: `ov_first`: the first tile of each correlation among one device's 128 rows is a tile of that device (tile numbers are tile * 32 + section). `ov_second`: the second tile differs from the first and lies in the same section or in the section numbered one less. `match_count`: the first correlation among each device's rows has all 32 matches live. `cell_first`: cell row * 7 + column of the 7 x 7 cells of a tile's node grid. `cell_second`: cell row * 7 + column of the 7 x 7 cells of a tile's node grid.
All inputs are finite; a program needn't handle non-finite values.
Results may differ from the reference program's by a relative error of at most 0.00017.
Values sent between devices are 32-bit elements; how exact they have to be, the bound alone decides.
No kernel may reach another device: no remote copies, remote signals or barrier semaphores. Data moves between devices by JAX's collectives and lax.ppermute only.
A program may use at most 64 MiB of HBM per device.

```python
import math
import jax
import jax.numpy as jnp

TPS_DEV = 32
SEC_DEV = 1
OV_DEV = 128
MATCH = 32
ITERS = 4
TPS = 256
SECTIONS = 32
CORRELATIONS = 32768


def correlation_table(key):
    subkeys = jax.random.split(key, 6)
    tile_groups = TPS // TPS_DEV
    slot_ids = jnp.arange(CORRELATIONS, dtype=jnp.int32)
    device = slot_ids // OV_DEV
    sec_group = device // tile_groups
    tile_group = device % tile_groups
    first_sec = sec_group * SEC_DEV + jax.random.randint(subkeys[0], (CORRELATIONS,), 0, SEC_DEV)
    first_tile = tile_group * TPS_DEV + jax.random.randint(subkeys[1], (CORRELATIONS,), 0, TPS_DEV)
    tile_step = jax.random.randint(subkeys[2], (CORRELATIONS,), 1, TPS)
    crosses = (jax.random.randint(subkeys[3], (CORRELATIONS,), 0, 5) < 2) & (first_sec > 0)
    second_tile = jnp.where(crosses, jax.random.randint(subkeys[4], (CORRELATIONS,), 0, TPS), (first_tile + tile_step) % TPS)
    second_sec = jnp.where(crosses, first_sec - 1, first_sec)
    live_counts = jax.random.randint(subkeys[5], (CORRELATIONS,), 1, MATCH + 1)
    live_counts = jnp.where(slot_ids % OV_DEV == 0, MATCH, live_counts)
    first_ids = (first_tile * SECTIONS + first_sec).astype(jnp.int32)
    second_ids = (second_tile * SECTIONS + second_sec).astype(jnp.int32)
    return (first_ids, second_ids, live_counts.astype(jnp.int32))


def draw_ov_first(key, part):
    return correlation_table(key)[0]


def draw_ov_second(key, part):
    return correlation_table(key)[1]


def draw_match_count(key, part):
    return correlation_table(key)[2]


def touch_ends(values, key, smallest, largest):
    index_at = [jax.random.randint(jax.random.fold_in(key, axis), (), 0, length) for axis, length in enumerate(values.shape)]
    longest = values.shape.index(max(values.shape))
    next_to = index_at[:longest] + [(index_at[longest] + 1) % values.shape[longest]] + index_at[longest + 1:]
    return values.at[tuple(index_at)].set(smallest).at[tuple(next_to)].set(largest)


def steps_of(key, shape, pieces, smallest, top_value):
    def one(position, shards_of):
        draws = jax.random.uniform(jax.random.fold_in(jax.random.fold_in(key, 6), position), (shards_of,), jnp.float32, smallest / len(pieces), top_value / len(pieces))
        return jnp.repeat(jnp.exp(draws), shape[position] // shards_of).reshape((-1,) + (1,) * (len(shape) - position - 1))

    gain = one(*pieces[0])
    for cut in pieces[1:]:
        gain = gain * one(*cut)
    return gain


def noise(stream_key, shape, deviation, reach, cuts=(), kind=jnp.bfloat16):
    result = jax.random.normal(stream_key, shape, jnp.float32) * deviation
    if len(cuts) > 0:
        result = steps_of(stream_key, shape, cuts, -0.22, 0.18) * result
    return jnp.clip(result, min=-reach, max=reach).astype(kind)


def setup_inputs(seed: int = 0) -> dict:
    keys = jax.random.split(jax.random.key(seed), 10)
    ov_first = draw_ov_first(jax.random.fold_in(keys[9], 71), 0)
    ov_second = draw_ov_second(jax.random.fold_in(keys[9], 71), 0)
    match_count = draw_match_count(jax.random.fold_in(keys[9], 71), 0)
    cell_first = touch_ends(jax.random.randint(keys[3], (MATCH, CORRELATIONS), 0, 49), jax.random.fold_in(keys[3], 1), 0, 48).astype(jnp.int32)
    cell_second = touch_ends(jax.random.randint(keys[4], (MATCH, CORRELATIONS), 0, 49), jax.random.fold_in(keys[4], 1), 0, 48).astype(jnp.int32)
    frac_first = jnp.clip(1.0 * jax.random.uniform(keys[5], (2, MATCH, CORRELATIONS), jnp.float32) ** steps_of(keys[5], (2, MATCH, CORRELATIONS), ((2, 256),), -0.2, 0.2), 0.0, 1.0)
    frac_second = jnp.clip(1.0 * jax.random.uniform(keys[6], (2, MATCH, CORRELATIONS), jnp.float32) ** steps_of(keys[6], (2, MATCH, CORRELATIONS), ((2, 256),), -0.2, 0.2), 0.0, 1.0)
    target = noise(keys[7], (2, MATCH, CORRELATIONS), 1.0, 6.0, ((2, 256),), jnp.float32)
    stiffness = jnp.clip(jnp.exp(math.log(3.0) - 2.3025851 * jax.random.uniform(keys[8], (TPS, SECTIONS), jnp.float32) ** steps_of(keys[8], (TPS, SECTIONS), ((0, 8), (1, 32)), -0.2, 0.2)), 0.3, 3.0)
    return {"ov_first": ov_first, "ov_second": ov_second, "match_count": match_count, "cell_first": cell_first, "cell_second": cell_second, "frac_first": frac_first, "frac_second": frac_second, "target": target, "stiffness": stiffness}


DAMPING = 0.5


def corners(cell_ids, fraction):
    corner_base = (cell_ids // 7) * 8 + cell_ids % 7
    across = fraction[0]
    along = fraction[1]
    node_ids = jnp.stack([corner_base, corner_base + 1, corner_base + 8, corner_base + 9])
    weights = jnp.stack([(1.0 - across) * (1.0 - along), across * (1.0 - along), (1.0 - across) * along, across * along])
    return node_ids, weights


def sample(picked_rows, node_ids, weights):
    owners = jnp.arange(picked_rows.shape[0], dtype=jnp.int32)[None, None, :] * 128
    flattened = picked_rows.reshape(-1)
    return jnp.stack([jnp.sum(weights * flattened[owners + component * 64 + node_ids], 0) for component in range(2)])


def spread(mismatch, node_ids, weights):
    num_rows = mismatch.shape[2]
    owners = jnp.arange(num_rows, dtype=jnp.int32)[None, None, :] * 128
    positions = jnp.concatenate([(owners + component * 64 + node_ids).reshape(-1) for component in range(2)])
    amounts = jnp.concatenate([(weights * mismatch[component][None]).reshape(-1) for component in range(2)])
    return jax.ops.segment_sum(amounts, positions, num_segments=num_rows * 128).reshape(num_rows, 128)


def laplace(field_now):
    lane_ids = jnp.arange(128, dtype=jnp.int32)
    has_right = jnp.where(lane_ids % 8 < 7, 1.0, 0.0).astype(jnp.float32)
    has_down = jnp.where((lane_ids // 8) % 8 < 7, 1.0, 0.0).astype(jnp.float32)
    step_right = (jnp.roll(field_now, -1, -1) - field_now) * has_right
    step_down = (jnp.roll(field_now, -8, -1) - field_now) * has_down
    return jnp.roll(step_right, 1, -1) - step_right + jnp.roll(step_down, 8, -1) - step_down


def reference(ov_first, ov_second, match_count, cell_first, cell_second, frac_first, frac_second, target, stiffness):
    tile_total = TPS * SECTIONS
    live_mask = (jnp.arange(MATCH, dtype=jnp.int32)[:, None] < match_count[None, :]).astype(jnp.float32)
    nodes_first, weights_first = corners(cell_first, frac_first)
    nodes_second, weights_second = corners(cell_second, frac_second)

    def transpose(mismatch):
        forces = jax.ops.segment_sum(spread(mismatch, nodes_first, weights_first), ov_first, num_segments=tile_total)
        forces = forces - jax.ops.segment_sum(spread(mismatch, nodes_second, weights_second), ov_second, num_segments=tile_total)
        return forces.reshape(TPS, SECTIONS, 128)

    def operate(field_now):
        flattened = field_now.reshape(-1, 128)
        mismatch = live_mask[None] * (sample(flattened[ov_first], nodes_first, weights_first) - sample(flattened[ov_second], nodes_second, weights_second))
        return transpose(mismatch) + stiffness[..., None] * laplace(field_now) + DAMPING * field_now

    right_side = transpose(live_mask[None] * target)
    solution_field = jnp.zeros_like(right_side)
    residual = right_side
    direction = right_side
    norm_now = jnp.sum(residual * residual)
    for iteration in range(ITERS):
        applied = operate(direction)
        step_size = norm_now / jnp.sum(direction * applied)
        solution_field = solution_field + step_size * direction
        residual = residual - step_size * applied
        norm_next = jnp.sum(residual * residual)
        direction = residual + (norm_next / norm_now) * direction
        norm_now = norm_next
    return solution_field, residual
```

```python
import functools

import jax
import jax.numpy as jnp
from jax import lax
from jax.experimental import pallas as pl
from jax.experimental.pallas import tpu as pltpu
from jax.sharding import PartitionSpec as P

ITERS = 4
DAMPING = 0.5
SHIFT = 10.0
SCALE = 1.0 / 128.0
BACK = 25.0 / 16384.0
PAIRS = [(i, j) for i in range(5) for j in range(i, 5) if (i, j) != (4, 4)]
VMEM = pl.BlockSpec(memory_space=pltpu.VMEM)
F32 = jnp.float32
NT = (((1,), (1,)), ((), ()))


def split3(x):
    a = x.astype(jnp.bfloat16)
    rest = x - a.astype(F32)
    b = rest.astype(jnp.bfloat16)
    c = (rest - b.astype(F32)).astype(jnp.bfloat16)
    return jnp.concatenate([a, b, c], 0)


def merge3(x):
    n = x.shape[0] // 3
    return x[:n] + (x[n : 2 * n] + x[2 * n :])


def sublane_ids():
    return lax.broadcasted_iota(jnp.int32, (8, 128), 0)


def fold_rows(parts):
    sub = sublane_ids()
    low = sub < 4
    half = [
        jnp.where(low, parts[p], parts[p + 4])
        + pltpu.roll(jnp.where(low, parts[p + 4], parts[p]), 4, 0)
        for p in range(4)
    ]
    two = (sub & 2) != 0
    quarter = [
        jnp.where(two, half[p + 2] + pltpu.roll(half[p + 2], 2, 0), half[p] + pltpu.roll(half[p], 6, 0))
        for p in range(2)
    ]
    one = (sub & 1) != 0
    return jnp.where(
        one, quarter[1] + pltpu.roll(quarter[1], 1, 0), quarter[0] + pltpu.roll(quarter[0], 7, 0)
    )


def spread_block(tops, sides, out_ref, lanes, lead=()):
    for q in range(8):
        parts = []
        for p in range(8):
            acc = tops[q][0] * sides[p][0]
            for group in range(1, 4):
                acc = acc + tops[q][group] * sides[p][group]
            parts.append(acc)
        out_ref[lead + (slice(8 * q, 8 * q + 8), lanes)] = fold_rows(parts)


def sample_block(rows_ref, lanes, wy_ref, fx_ref, col_ref, blk, side):
    out = []
    for group in range(4):
        ms = slice(8 * group, 8 * group + 8)
        col = col_ref[blk, side, ms, :]
        nxt = col + 1
        fx = fx_ref[blk, side, ms, :]
        acc = None
        for q in range(8):
            row = rows_ref[8 * q : 8 * q + 8, lanes]
            left = jnp.take_along_axis(row, col, axis=0, mode="promise_in_bounds")
            right = jnp.take_along_axis(row, nxt, axis=0, mode="promise_in_bounds")
            term = wy_ref[blk, side, q, ms, :] * (left + fx * (right - left))
            acc = term if acc is None else acc + term
        out.append(acc)
    return out


def load_table(ref, blk, side):
    return [[ref[blk, side, p, 8 * g : 8 * g + 8, :] for g in range(4)] for p in range(8)]


def lanes_of(blk):
    return pl.ds(pl.multiple_of(blk * 128, 128), 128)


def tables_kernel(
    comp_ref, data_ref, wx_ref, wy_ref, fx_ref, col_ref, live_ref, ohf_ref, ohs_ref, own_ref, down_ref, f_ref
):
    comp = comp_ref[0]

    def body(blk, carry):
        lanes = lanes_of(blk)
        count = data_ref[blk, 258, :][None, :]
        for group in range(4):
            ms = slice(8 * group, 8 * group + 8)
            slot = (sublane_ids() + 8 * group).astype(F32)
            live_ref[blk, ms, :] = jnp.where(slot < count, SCALE, 0.0)
        for side in range(2):
            for group in range(4):
                ms = slice(8 * group, 8 * group + 8)
                cell = data_ref[blk, 32 * side + 8 * group : 32 * side + 8 * group + 8, :].astype(jnp.int32)
                base = 64 + 64 * side + 8 * group
                fx = data_ref[blk, base : base + 8, :]
                fy = data_ref[blk, base + 32 : base + 40, :]
                row = (cell * 37) >> 8
                col = cell - 7 * row
                fx_ref[blk, side, ms, :] = fx
                col_ref[blk, side, ms, :] = col
                for k in range(8):
                    wx_ref[blk, side, k, ms, :] = jnp.where(
                        col == k, 1.0 - fx, jnp.where(col == k - 1, fx, 0.0)
                    )
                    wy_ref[blk, side, k, ms, :] = jnp.where(
                        row == k, 1.0 - fy, jnp.where(row == k - 1, fy, 0.0)
                    )
        first = data_ref[blk, 256, :][None, :].astype(jnp.int32)
        second = data_ref[blk, 257, :][None, :].astype(jnp.int32)
        ids = lax.broadcasted_iota(jnp.int32, (256, 128), 0)
        ohf_ref[:, lanes] = jnp.where(ids == first, 1.0, 0.0).astype(jnp.bfloat16)
        ohs_ref[0:256, lanes] = jnp.where(ids == second, 1.0, 0.0).astype(jnp.bfloat16)
        ohs_ref[256:512, lanes] = jnp.where(ids + 256 == second, 1.0, 0.0).astype(jnp.bfloat16)
        goal = []
        for group in range(4):
            at = pl.multiple_of(192 + 32 * comp + 8 * group, 8)
            goal.append(
                data_ref[blk, pl.ds(at, 8), :] * (live_ref[blk, 8 * group : 8 * group + 8, :] * (1.0 / SCALE))
            )
        for side in range(2):
            tops = load_table(wy_ref, blk, side)
            tops = [[tops[q][g] * goal[g] for g in range(4)] for q in range(8)]
            spread_block(tops, load_table(wx_ref, blk, side), f_ref, lanes, (side,))
        return carry

    lax.fori_loop(0, 8, body, 0)
    at_first = merge3(lax.dot_general(split3(f_ref[0]), ohf_ref[...], NT, preferred_element_type=F32))
    at_second = merge3(lax.dot_general(split3(f_ref[1]), ohs_ref[...], NT, preferred_element_type=F32))
    own_ref[...] = at_first - at_second[:, :256]
    down_ref[...] = at_second[:, 256:]


def stencil_kernel(wx_ref, wy_ref, live_ref, ohf_ref, ohs_ref, stiff_ref, own_ref, down_ref, f_ref):
    def body(blk, carry):
        lanes = lanes_of(blk)
        live = [live_ref[blk, 8 * g : 8 * g + 8, :] for g in range(4)]
        for side in range(2):
            zero = [jnp.zeros((8, 128), F32)] * 4
            for kind_x in range(2):
                wx = load_table(wx_ref, blk, side) + [zero]
                sides = [[wx[p][g] * wx[p + kind_x][g] for g in range(4)] for p in range(8)]
                for kind_y in range(2):
                    wy = load_table(wy_ref, blk, side) + [zero]
                    tops = [[wy[q][g] * wy[q + kind_y][g] * live[g] for g in range(4)] for q in range(8)]
                    spread_block(tops, sides, f_ref, lanes, (side, 2 * kind_y + kind_x))
        return carry

    lax.fori_loop(0, 8, body, 0)
    node = lax.broadcasted_iota(jnp.int32, (64, 256), 0)
    p = node & 7
    q = node >> 3
    one = lambda cond: jnp.where(cond, 1.0, 0.0)
    stiff = stiff_ref[...] * SCALE
    degree = one(p < 7) + one(p > 0) + one(q < 7) + one(q > 0)
    extra = [
        stiff * degree + (DAMPING - SHIFT) * SCALE,
        -stiff * one(p < 7),
        -stiff * one(q < 7),
        None,
    ]
    for kind in range(4):
        at_first = merge3(lax.dot_general(split3(f_ref[0, kind]), ohf_ref[...], NT, preferred_element_type=F32))
        at_second = merge3(lax.dot_general(split3(f_ref[1, kind]), ohs_ref[...], NT, preferred_element_type=F32))
        total = at_first + at_second[:, :256]
        own_ref[kind] = total if extra[kind] is None else total + extra[kind]
        down_ref[kind] = at_second[:, 256:]


def up_kernel(v_ref, ohf_ref, ohs_ref, wx_ref, wy_ref, fx_ref, col_ref, live_ref, own_ref, down_ref, g_ref, f_ref):
    g_ref[...] = merge3(jnp.dot(split3(v_ref[...]), ohf_ref[...], preferred_element_type=F32))

    def body(blk, carry):
        lanes = lanes_of(blk)
        got = sample_block(g_ref, lanes, wy_ref, fx_ref, col_ref, blk, 0)
        got = [got[g] * live_ref[blk, 8 * g : 8 * g + 8, :] for g in range(4)]
        tops = load_table(wy_ref, blk, 1)
        tops = [[tops[q][g] * got[g] for g in range(4)] for q in range(8)]
        spread_block(tops, load_table(wx_ref, blk, 1), f_ref, lanes)
        return carry

    lax.fori_loop(0, 8, body, 0)
    forces = merge3(lax.dot_general(split3(f_ref[...]), ohs_ref[...], NT, preferred_element_type=F32))
    own_ref[...] = forces[:, :256]
    down_ref[...] = forces[:, 256:]


def down_kernel(
    v_ref, below_ref, prev_ref, part_ref, band_ref, band2_ref,
    ohf_ref, ohs_ref, wx_ref, wy_ref, fx_ref, col_ref, live_ref, out_ref, g_ref, f_ref, *, back
):
    rows = jnp.concatenate([split3(v_ref[...]), split3(below_ref[...])], 1)
    g_ref[...] = merge3(jnp.dot(rows, ohs_ref[...], preferred_element_type=F32))

    def body(blk, carry):
        lanes = lanes_of(blk)
        got = sample_block(g_ref, lanes, wy_ref, fx_ref, col_ref, blk, 1)
        got = [got[g] * live_ref[blk, 8 * g : 8 * g + 8, :] for g in range(4)]
        tops = load_table(wy_ref, blk, 0)
        tops = [[tops[q][g] * got[g] for g in range(4)] for q in range(8)]
        spread_block(tops, load_table(wx_ref, blk, 0), f_ref, lanes)
        return carry

    lax.fori_loop(0, 8, body, 0)
    forces = merge3(lax.dot_general(split3(f_ref[...]), ohf_ref[...], NT, preferred_element_type=F32))
    v = v_ref[...]
    band = [band_ref[k] + band2_ref[k] for k in range(4)]
    up = lambda x, d: pltpu.roll(x, 64 - d, 0)
    dn = lambda x, d: pltpu.roll(x, d, 0)
    total = band[0] * v
    total = total + band[1] * up(v, 1) + dn(band[1] * v, 1)
    total = total + band[2] * up(v, 8) + dn(band[2] * v, 8)
    total = total + band[3] * up(v, 9) + dn(band[3] * v, 9)
    total = total + dn(band[3] * up(v, 8), 1) + dn(band[3] * up(v, 1), 8)
    total = total - forces - part_ref[...]
    if back:
        total = total - BACK * prev_ref[...]
    out_ref[...] = total


def two_sum(a, b):
    s = a + b
    t = s - a
    return s, (a - (s - t)) + (b - t)


def halves(a):
    c = 4097.0 * a
    high = c - (c - a)
    return high, a - high


def two_prod(a, b):
    p = a * b
    ah, al = halves(a)
    bh, bl = halves(b)
    return p, ((ah * bh - p) + ah * bl + al * bh) + al * bl


def quick(a, b):
    s = a + b
    return s, b - (s - a)


def dd_add(x, y):
    s, e = two_sum(x[0], y[0])
    return quick(s, e + (x[1] + y[1]))


def dd_mul(x, y):
    p, e = two_prod(x[0], y[0])
    return quick(p, e + (x[0] * y[1] + x[1] * y[0]))


def dd_neg(x):
    return (-x[0], -x[1])


def dd_div(x, y):
    q = x[0] / y[0]
    rest = dd_add(x, dd_neg(dd_mul(y, (q, jnp.zeros_like(q)))))
    return quick(q, rest[0] / y[0])


def dots_kernel(*refs):
    out_ref = refs[5]
    fields = [r[...] for r in refs[:5]]
    sub = lax.broadcasted_iota(jnp.int32, (16, 128), 0)
    lane = lax.broadcasted_iota(jnp.int32, (16, 128), 1)
    high = jnp.zeros((16, 128), F32)
    low = jnp.zeros((16, 128), F32)
    for k, (i, j) in enumerate(PAIRS):
        acc = two_prod(fields[i], fields[j])
        acc = dd_add((acc[0][:, :128], acc[1][:, :128]), (acc[0][:, 128:], acc[1][:, 128:]))
        n = 64
        while n > 8:
            n //= 2
            acc = dd_add((acc[0][:n], acc[1][:n]), (acc[0][n:], acc[1][n:]))
        for d in (4, 2, 1):
            acc = dd_add(acc, (pltpu.roll(acc[0], d, 0), pltpu.roll(acc[1], d, 0)))
        wide = [jnp.concatenate([a, a], 0) for a in acc]
        high = jnp.where(sub == k, wide[0], high)
        low = jnp.where(sub == k, wide[1], low)
    acc = (high, low)
    for d in (64, 32, 16, 8, 4, 2, 1):
        acc = dd_add(acc, (pltpu.roll(acc[0], d, 1), pltpu.roll(acc[1], d, 1)))
    row = jnp.where(lane == sub, acc[0], 0.0) + jnp.where(lane == sub + 16, acc[1], 0.0)
    out_ref[...] = jnp.sum(row, 0, keepdims=True)


def finish_kernel(tile_ref, gram_ref, gram2_ref, v0, v1, v2, v3, v4, mine_ref, other_ref):
    rows = jnp.concatenate([gram_ref[...], gram2_ref[...]], 0)
    acc = (rows, pltpu.roll(rows, 112, 1))
    n = 64
    while n > 8:
        n //= 2
        acc = dd_add((acc[0][:n], acc[1][:n]), (acc[0][n:], acc[1][n:]))
    for d in (4, 2, 1):
        acc = dd_add(acc, (pltpu.roll(acc[0], d, 0), pltpu.roll(acc[1], d, 0)))
    gram = {}
    for k, (i, j) in enumerate(PAIRS):
        pair = tuple(jnp.broadcast_to(a[:, k : k + 1], (8, 128)) for a in acc)
        gram[(i, j)] = pair
        gram[(j, i)] = pair
    zero = jnp.zeros((8, 128), F32)
    const = lambda c: (jnp.full((8, 128), c, F32), zero)

    def form(a, b):
        total = None
        for j, bj in enumerate(b):
            inner = None
            for i, ai in enumerate(a):
                term = dd_mul(ai, gram[(i, j)])
                inner = term if inner is None else dd_add(inner, term)
            inner = dd_mul(inner, bj)
            total = inner if total is None else dd_add(total, inner)
        return total

    def apply(p):
        out = [const(0.0) for _ in range(len(p) + 1)]
        for k, c in enumerate(p):
            out[k + 1] = dd_add(out[k + 1], (c[0] * 128.0, c[1] * 128.0))
            out[k] = dd_add(out[k], dd_mul(c, const(SHIFT)))
            if k >= 1:
                out[k - 1] = dd_add(out[k - 1], dd_mul(c, const(BACK * 128.0)))
        return out

    def axpy(a, x, y):
        out = []
        for k in range(max(len(x), len(y))):
            if k >= len(x):
                out.append(y[k])
            elif k >= len(y):
                out.append(dd_mul(a, x[k]))
            else:
                out.append(dd_add(y[k], dd_mul(a, x[k])))
        return out

    res = [const(1.0)]
    direc = [const(1.0)]
    sol = []
    norm = gram[(0, 0)]
    for it in range(ITERS):
        image = apply(direc)
        step = dd_div(norm, form(direc, image))
        sol = axpy(step, direc, sol)
        res = axpy(dd_neg(step), image, res)
        if it < ITERS - 1:
            new = form(res, res)
            direc = axpy(dd_div(new, norm), direc, res)
            norm = new
    fields = [r[...] for r in (v0, v1, v2, v3, v4)]

    def combine(coefs):
        total = None
        for c, f in zip(coefs, fields):
            term = c[0][0:1, 0:1] * f
            total = term if total is None else total + term
        return total

    tile = tile_ref[0]
    ids = lax.broadcasted_iota(jnp.int32, (64, 256), 1)
    want = lax.broadcasted_iota(jnp.int32, (64, 256), 0)
    swap = tile + 1 - 2 * (tile & 1)
    want = jnp.where(want < 32, tile * 32 + want, swap * 32 + want - 32)
    pick = jnp.where(ids == want, 1.0, 0.0).astype(jnp.bfloat16)
    for k, coefs in enumerate((sol, res)):
        parts = lax.dot_general(pick, split3(combine(coefs)), NT, preferred_element_type=F32)
        both = parts[:, :64] + (parts[:, 64:128] + parts[:, 128:192])
        mine_ref[k] = both[:32]
        other_ref[k] = both[32:]


def call(kernel, outs, n_in, scratch=(), smem=0, flops=10**7):
    return pl.pallas_call(
        kernel,
        out_shape=[jax.ShapeDtypeStruct(s, d) for s, d in outs],
        in_specs=[pl.BlockSpec(memory_space=pltpu.SMEM)] * smem + [VMEM] * (n_in - smem),
        out_specs=[VMEM] * len(outs),
        scratch_shapes=[pltpu.VMEM(s, d) for s, d in scratch],
        compiler_params=pltpu.CompilerParams(vmem_limit_bytes=48 * 1024 * 1024),
        cost_estimate=pl.CostEstimate(flops=flops, bytes_accessed=1 << 20, transcendentals=0),
    )


def shifted(block, distance):
    devices = range(lax.axis_size("sec"))
    route = [(i - distance, i) for i in devices if i - distance in devices]
    return lax.ppermute(block, "sec", route)


def swapped(block):
    return lax.ppermute(block, "tile", [(i, i ^ 1) for i in range(8)])


def on_device(
    ov_first, ov_second, match_count, cell_first, cell_second, frac_first, frac_second, target, stiffness
):
    sec = lax.axis_index("sec")
    tile = lax.axis_index("tile")
    core = tile % 2
    sections = lax.axis_size("sec")
    second = ov_second // sections + jnp.where(ov_second % sections == sec, 0, 256)
    rows = [
        cell_first.astype(F32),
        cell_second.astype(F32),
        frac_first.reshape(64, 128),
        frac_second.reshape(64, 128),
        target.reshape(64, 128),
        (ov_first // sections).astype(F32)[None],
        second.astype(F32)[None],
        match_count.astype(F32)[None],
        jnp.pad(stiffness.reshape(1, 32), ((0, 0), (0, 96))),
        jnp.zeros((4, 128), F32),
    ]
    packed = jnp.concatenate(rows, 0)
    groups = [[0, 2, 4, 6], [1, 3, 5, 7]]
    same = lax.all_to_all(
        jnp.broadcast_to(packed[None], (4, 264, 128)), "tile", 0, 0, tiled=True, axis_index_groups=groups
    )
    data = jnp.concatenate([same, swapped(same)], 0)
    pair = data[:, 259, :32].reshape(2, 4, 32)
    pair = jnp.where(core == 0, pair, pair[::-1])
    stiff = jnp.transpose(pair, (1, 0, 2)).reshape(1, 256)

    field = ((64, 256), F32)
    bf16 = jnp.bfloat16
    wx, wy, fx, col, live, ohf, ohs, own, down = call(
        tables_kernel,
        [
            ((8, 2, 8, 32, 128), F32),
            ((8, 2, 8, 32, 128), F32),
            ((8, 2, 32, 128), F32),
            ((8, 2, 32, 128), jnp.int32),
            ((8, 32, 128), F32),
            ((256, 1024), bf16),
            ((512, 1024), bf16),
            field,
            field,
        ],
        2,
        [((2, 64, 1024), F32)],
        smem=1,
    )(core.reshape(1), data)
    start_down = shifted(down, -1)
    band, band_down = call(
        stencil_kernel,
        [((4, 64, 256), F32), ((4, 64, 256), F32)],
        6,
        [((2, 4, 64, 1024), F32)],
    )(wx, wy, live, ohf, ohs, stiff)
    band2 = shifted(band_down, -1)
    tables = (ohf, ohs, wx, wy, fx, col, live)
    scratch = [((64, 1024), F32), ((64, 1024), F32)]
    fields = [own - start_down]
    for k in range(ITERS):
        v = fields[-1]
        below = shifted(v, 1)
        part, down = call(up_kernel, [field, field], 8, scratch)(v, *tables)
        above = shifted(down, -1)
        partial = call(functools.partial(down_kernel, back=k > 0), [field], 13, scratch)(
            v, below, fields[max(k - 1, 0)], part, band, band2, *tables
        )[0]
        fields.append(partial - above)
    gram = call(dots_kernel, [((1, 128), F32)], 5)(*fields)[0]
    gram = lax.all_to_all(jnp.broadcast_to(gram, (32, 128)), "sec", 0, 0, tiled=True)
    mine, other = call(
        finish_kernel, [((2, 32, 64), F32), ((2, 32, 64), F32)], 8, smem=1
    )(tile.reshape(1), gram, swapped(gram), *fields)
    other = swapped(other)
    first = jnp.where(core == 0, mine, other)
    last = jnp.where(core == 0, other, mine)
    out = jnp.concatenate([first, last], 2)[:, :, None, :]
    return (out[0], out[1])


def solution(mesh):
    in_specs = (
        P(("sec", "tile")),
        P(("sec", "tile")),
        P(("sec", "tile")),
        P(None, ("sec", "tile")),
        P(None, ("sec", "tile")),
        P(None, None, ("sec", "tile")),
        P(None, None, ("sec", "tile")),
        P(None, None, ("sec", "tile")),
        P("tile", "sec"),
    )
    out_specs = (P("tile", "sec", None), P("tile", "sec", None))
    return jax.shard_map(
        on_device, mesh=mesh, in_specs=in_specs, out_specs=out_specs, check_vma=False
    )
```

```python
import functools

import jax
import jax.numpy as jnp
from jax import lax
from jax.experimental import pallas as pl
from jax.experimental.pallas import tpu as pltpu
from jax.sharding import PartitionSpec as P

ITERS = 4
DAMPING = 0.5
SHIFT = 10.0
SCALE = 1.0 / 128.0
BACK = 25.0 / 16384.0
PAIRS = [(i, j) for i in range(5) for j in range(i, 5) if (i, j) != (4, 4)]
VMEM = pl.BlockSpec(memory_space=pltpu.VMEM)
F32 = jnp.float32
NT = (((1,), (1,)), ((), ()))


def split3(x):
    a = x.astype(jnp.bfloat16)
    rest = x - a.astype(F32)
    b = rest.astype(jnp.bfloat16)
    c = (rest - b.astype(F32)).astype(jnp.bfloat16)
    return jnp.concatenate([a, b, c], 0)


def merge3(x):
    n = x.shape[0] // 3
    return x[:n] + (x[n : 2 * n] + x[2 * n :])


def sublane_ids():
    return lax.broadcasted_iota(jnp.int32, (8, 128), 0)


def fold_rows(parts):
    sub = sublane_ids()
    low = sub < 4
    half = [
        jnp.where(low, parts[p], parts[p + 4])
        + pltpu.roll(jnp.where(low, parts[p + 4], parts[p]), 4, 0)
        for p in range(4)
    ]
    two = (sub & 2) != 0
    quarter = [
        jnp.where(two, half[p + 2] + pltpu.roll(half[p + 2], 2, 0), half[p] + pltpu.roll(half[p], 6, 0))
        for p in range(2)
    ]
    one = (sub & 1) != 0
    return jnp.where(
        one, quarter[1] + pltpu.roll(quarter[1], 1, 0), quarter[0] + pltpu.roll(quarter[0], 7, 0)
    )


def spread_block(tops, sides, out_ref, lanes, lead=()):
    for q in range(8):
        parts = []
        for p in range(8):
            acc = tops[q][0] * sides[p][0]
            for group in range(1, 4):
                acc = acc + tops[q][group] * sides[p][group]
            parts.append(acc)
        out_ref[lead + (slice(8 * q, 8 * q + 8), lanes)] = fold_rows(parts)


def sample_block(rows_ref, lanes, wy_ref, fx_ref, col_ref, blk, side):
    out = []
    for group in range(4):
        ms = slice(8 * group, 8 * group + 8)
        col = col_ref[blk, side, ms, :]
        nxt = col + 1
        fx = fx_ref[blk, side, ms, :]
        acc = None
        for q in range(8):
            row = rows_ref[8 * q : 8 * q + 8, lanes]
            left = jnp.take_along_axis(row, col, axis=0, mode="promise_in_bounds")
            right = jnp.take_along_axis(row, nxt, axis=0, mode="promise_in_bounds")
            term = wy_ref[blk, side, q, ms, :] * (left + fx * (right - left))
            acc = term if acc is None else acc + term
        out.append(acc)
    return out


def load_table(ref, blk, side):
    return [[ref[blk, side, p, 8 * g : 8 * g + 8, :] for g in range(4)] for p in range(8)]


def lanes_of(blk):
    return pl.ds(pl.multiple_of(blk * 128, 128), 128)


def pack_kernel(
    first_ref, second_ref, count_ref, cell1_ref, cell2_ref, frac1_ref, frac2_ref, target_ref, stiff_ref, out_ref
):
    for k in range(4):
        out_ref[k, 0:32, :] = cell1_ref[...].astype(F32)
        out_ref[k, 32:64, :] = cell2_ref[...].astype(F32)
        for c in range(2):
            at = slice(32 * c, 32 * c + 32)
            out_ref[k, 64 + at.start : 64 + at.stop, :] = frac1_ref[c]
            out_ref[k, 128 + at.start : 128 + at.stop, :] = frac2_ref[c]
            out_ref[k, 192 + at.start : 192 + at.stop, :] = target_ref[c]
        rows = [first_ref[...], second_ref[...], count_ref[...]]
        tail = jnp.concatenate([r.astype(F32) for r in rows] + [stiff_ref[...], jnp.zeros((4, 128), F32)], 0)
        out_ref[k, 256:264, :] = tail


def tables_kernel(
    comp_ref, same_ref, other_ref,
    wx_ref, wy_ref, fx_ref, col_ref, live_ref, ohf_ref, ohs_ref, own_ref, down_ref, f_ref
):
    comp = comp_ref[0]

    def fill(data_ref, at_blk, blk):
        lanes = lanes_of(blk)
        count = data_ref[at_blk, 258, :][None, :]
        goal = []
        for group in range(4):
            ms = slice(8 * group, 8 * group + 8)
            slot = (sublane_ids() + 8 * group).astype(F32)
            live = slot < count
            live_ref[blk, ms, :] = jnp.where(live, SCALE, 0.0)
            at = pl.multiple_of(192 + 32 * comp + 8 * group, 8)
            goal.append(jnp.where(live, data_ref[at_blk, pl.ds(at, 8), :], 0.0))
        for side in range(2):
            for group in range(4):
                ms = slice(8 * group, 8 * group + 8)
                at = 32 * side + 8 * group
                cell = data_ref[at_blk, at : at + 8, :].astype(jnp.int32)
                base = 64 + 64 * side + 8 * group
                fx = data_ref[at_blk, base : base + 8, :]
                fy = data_ref[at_blk, base + 32 : base + 40, :]
                row = (cell * 37) >> 8
                col = cell - 7 * row
                fx_ref[blk, side, ms, :] = fx
                col_ref[blk, side, ms, :] = col
                for k in range(8):
                    wx_ref[blk, side, k, ms, :] = jnp.where(
                        col == k, 1.0 - fx, jnp.where(col == k - 1, fx, 0.0)
                    )
                    wy_ref[blk, side, k, ms, :] = jnp.where(
                        row == k, 1.0 - fy, jnp.where(row == k - 1, fy, 0.0)
                    )
        first = data_ref[at_blk, 256, :][None, :].astype(jnp.int32)
        second = data_ref[at_blk, 257, :][None, :].astype(jnp.int32)
        ids = lax.broadcasted_iota(jnp.int32, (256, 128), 0)
        ohf_ref[:, lanes] = jnp.where(ids == first, 1.0, 0.0).astype(jnp.bfloat16)
        ohs_ref[0:256, lanes] = jnp.where(ids == second, 1.0, 0.0).astype(jnp.bfloat16)
        ohs_ref[256:512, lanes] = jnp.where(ids + 256 == second, 1.0, 0.0).astype(jnp.bfloat16)
        for side in range(2):
            tops = load_table(wy_ref, blk, side)
            tops = [[tops[q][g] * goal[g] for g in range(4)] for q in range(8)]
            spread_block(tops, load_table(wx_ref, blk, side), f_ref, lanes, (side,))

    def body(blk, carry):
        fill(same_ref, blk, blk)
        fill(other_ref, blk, blk + 4)
        return carry

    lax.fori_loop(0, 4, body, 0)
    at_first = merge3(lax.dot_general(split3(f_ref[0]), ohf_ref[...], NT, preferred_element_type=F32))
    at_second = merge3(lax.dot_general(split3(f_ref[1]), ohs_ref[...], NT, preferred_element_type=F32))
    own_ref[...] = at_first - at_second[:, :256]
    down_ref[...] = at_second[:, 256:]


def stencil_kernel(comp_ref, wx_ref, wy_ref, live_ref, ohs_ref, half_ref, f_ref):
    step = comp_ref[0]

    def body(blk, carry):
        lanes = lanes_of(blk)
        live = [live_ref[blk, 8 * g : 8 * g + 8, :] for g in range(4)]
        zero = [jnp.zeros((8, 128), F32)] * 4
        wy = load_table(wy_ref, blk, 1) + [zero]
        tops = [
            [wy[q][g] * jnp.where(step == 0, wy[q][g], wy[q + 1][g]) * live[g] for g in range(4)]
            for q in range(8)
        ]
        for kind in range(2):
            wx = load_table(wx_ref, blk, 1) + [zero]
            sides = [[wx[p][g] * wx[p + kind][g] for g in range(4)] for p in range(8)]
            spread_block(tops, sides, f_ref, lanes, (kind,))
        return carry

    lax.fori_loop(0, 8, body, 0)
    for kind in range(2):
        half_ref[kind] = merge3(
            lax.dot_general(split3(f_ref[kind]), ohs_ref[256:512, :], NT, preferred_element_type=F32)
        )


def up_kernel(
    v_ref, ohf_ref, ohs_ref, wx_ref, wy_ref, fx_ref, col_ref, live_ref,
    own_ref, down_ref, gap_ref, g_ref, h_ref, f_ref
):
    parts = split3(v_ref[...])
    g_ref[...] = merge3(jnp.dot(parts, ohf_ref[...], preferred_element_type=F32))
    h_ref[...] = merge3(jnp.dot(parts, ohs_ref[0:256, :], preferred_element_type=F32))

    def body(blk, carry):
        lanes = lanes_of(blk)
        got = sample_block(g_ref, lanes, wy_ref, fx_ref, col_ref, blk, 0)
        less = sample_block(h_ref, lanes, wy_ref, fx_ref, col_ref, blk, 1)
        gap = [(got[g] - less[g]) * live_ref[blk, 8 * g : 8 * g + 8, :] for g in range(4)]
        for g in range(4):
            gap_ref[blk, 8 * g : 8 * g + 8, :] = gap[g]
        tops = load_table(wy_ref, blk, 1)
        tops = [[tops[q][g] * gap[g] for g in range(4)] for q in range(8)]
        spread_block(tops, load_table(wx_ref, blk, 1), f_ref, lanes)
        return carry

    lax.fori_loop(0, 8, body, 0)
    forces = merge3(lax.dot_general(split3(f_ref[...]), ohs_ref[...], NT, preferred_element_type=F32))
    own_ref[...] = forces[:, :256]
    down_ref[...] = forces[:, 256:]


def down_kernel(
    comp_ref, v_ref, below_ref, prev_ref, part_ref, gap_ref, mine_ref, other_ref, stiff_ref,
    ohf_ref, ohs_ref, wx_ref, wy_ref, fx_ref, col_ref, live_ref, out_ref, g_ref, f_ref, *, back
):
    g_ref[...] = merge3(jnp.dot(split3(below_ref[...]), ohs_ref[256:512, :], preferred_element_type=F32))

    def body(blk, carry):
        lanes = lanes_of(blk)
        got = sample_block(g_ref, lanes, wy_ref, fx_ref, col_ref, blk, 1)
        gap = [
            gap_ref[blk, 8 * g : 8 * g + 8, :] - got[g] * live_ref[blk, 8 * g : 8 * g + 8, :]
            for g in range(4)
        ]
        tops = load_table(wy_ref, blk, 0)
        tops = [[tops[q][g] * gap[g] for g in range(4)] for q in range(8)]
        spread_block(tops, load_table(wx_ref, blk, 0), f_ref, lanes)
        return carry

    lax.fori_loop(0, 8, body, 0)
    forces = merge3(lax.dot_general(split3(f_ref[...]), ohf_ref[...], NT, preferred_element_type=F32))
    v = v_ref[...]
    up = lambda x, d: pltpu.roll(x, 64 - d, 0)
    dn = lambda x, d: pltpu.roll(x, d, 0)
    node = lax.broadcasted_iota(jnp.int32, (64, 256), 0)
    right = jnp.where((node & 7) < 7, up(v, 1) - v, 0.0)
    below = jnp.where(node < 56, up(v, 8) - v, 0.0)
    bend = (dn(right, 1) - right) + (dn(below, 8) - below)
    total = forces - part_ref[...] + (stiff_ref[...] * SCALE) * bend + ((DAMPING - SHIFT) * SCALE) * v
    first = comp_ref[0] == 0
    band = [jnp.where(first, mine_ref[k], other_ref[k]) for k in range(2)]
    band += [jnp.where(first, other_ref[k], mine_ref[k]) for k in range(2)]
    total = total + band[0] * v
    total = total + band[1] * up(v, 1) + dn(band[1] * v, 1)
    total = total + band[2] * up(v, 8) + dn(band[2] * v, 8)
    total = total + band[3] * up(v, 9) + dn(band[3] * v, 9)
    total = total + dn(band[3] * up(v, 8), 1) + dn(band[3] * up(v, 1), 8)
    if back:
        total = total - BACK * prev_ref[...]
    out_ref[...] = total


def two_sum(a, b):
    s = a + b
    t = s - a
    return s, (a - (s - t)) + (b - t)


def halves(a):
    c = 4097.0 * a
    high = c - (c - a)
    return high, a - high


def two_prod(a, b):
    p = a * b
    ah, al = halves(a)
    bh, bl = halves(b)
    return p, ((ah * bh - p) + ah * bl + al * bh) + al * bl


def quick(a, b):
    s = a + b
    return s, b - (s - a)


def dd_add(x, y):
    s, e = two_sum(x[0], y[0])
    return quick(s, e + (x[1] + y[1]))


def dd_mul(x, y):
    p, e = two_prod(x[0], y[0])
    return quick(p, e + (x[0] * y[1] + x[1] * y[0]))


def dd_neg(x):
    return (-x[0], -x[1])


def dd_div(x, y):
    q = x[0] / y[0]
    rest = dd_add(x, dd_neg(dd_mul(y, (q, jnp.zeros_like(q)))))
    return quick(q, rest[0] / y[0])


def dots_kernel(*refs):
    out_ref = refs[5]
    fields = [r[...] for r in refs[:5]]
    sub = lax.broadcasted_iota(jnp.int32, (16, 128), 0)
    lane = lax.broadcasted_iota(jnp.int32, (16, 128), 1)
    high = jnp.zeros((16, 128), F32)
    low = jnp.zeros((16, 128), F32)
    for k, (i, j) in enumerate(PAIRS):
        acc = two_prod(fields[i], fields[j])
        acc = dd_add((acc[0][:, :128], acc[1][:, :128]), (acc[0][:, 128:], acc[1][:, 128:]))
        n = 64
        while n > 8:
            n //= 2
            acc = dd_add((acc[0][:n], acc[1][:n]), (acc[0][n:], acc[1][n:]))
        for d in (4, 2, 1):
            acc = dd_add(acc, (pltpu.roll(acc[0], d, 0), pltpu.roll(acc[1], d, 0)))
        wide = [jnp.concatenate([a, a], 0) for a in acc]
        high = jnp.where(sub == k, wide[0], high)
        low = jnp.where(sub == k, wide[1], low)
    acc = (high, low)
    for d in (64, 32, 16, 8, 4, 2, 1):
        acc = dd_add(acc, (pltpu.roll(acc[0], d, 1), pltpu.roll(acc[1], d, 1)))
    row = jnp.where(lane == sub, acc[0], 0.0) + jnp.where(lane == sub + 16, acc[1], 0.0)
    out_ref[...] = jnp.sum(row, 0, keepdims=True)


def finish_kernel(tile_ref, gram_ref, gram2_ref, v0, v1, v2, v3, v4, mine_ref, other_ref):
    rows = jnp.concatenate([gram_ref[...], gram2_ref[...]], 0)
    acc = (rows, pltpu.roll(rows, 112, 1))
    n = 64
    while n > 8:
        n //= 2
        acc = dd_add((acc[0][:n], acc[1][:n]), (acc[0][n:], acc[1][n:]))
    for d in (4, 2, 1):
        acc = dd_add(acc, (pltpu.roll(acc[0], d, 0), pltpu.roll(acc[1], d, 0)))
    gram = {}
    for k, (i, j) in enumerate(PAIRS):
        pair = tuple(jnp.broadcast_to(a[:, k : k + 1], (8, 128)) for a in acc)
        gram[(i, j)] = pair
        gram[(j, i)] = pair
    zero = jnp.zeros((8, 128), F32)
    const = lambda c: (jnp.full((8, 128), c, F32), zero)

    def form(a, b):
        total = None
        for j, bj in enumerate(b):
            inner = None
            for i, ai in enumerate(a):
                term = dd_mul(ai, gram[(i, j)])
                inner = term if inner is None else dd_add(inner, term)
            inner = dd_mul(inner, bj)
            total = inner if total is None else dd_add(total, inner)
        return total

    def apply(p):
        out = [const(0.0) for _ in range(len(p) + 1)]
        for k, c in enumerate(p):
            out[k + 1] = dd_add(out[k + 1], (c[0] * 128.0, c[1] * 128.0))
            out[k] = dd_add(out[k], dd_mul(c, const(SHIFT)))
            if k >= 1:
                out[k - 1] = dd_add(out[k - 1], dd_mul(c, const(BACK * 128.0)))
        return out

    def axpy(a, x, y):
        out = []
        for k in range(max(len(x), len(y))):
            if k >= len(x):
                out.append(y[k])
            elif k >= len(y):
                out.append(dd_mul(a, x[k]))
            else:
                out.append(dd_add(y[k], dd_mul(a, x[k])))
        return out

    res = [const(1.0)]
    direc = [const(1.0)]
    sol = []
    norm = gram[(0, 0)]
    for it in range(ITERS):
        image = apply(direc)
        step = dd_div(norm, form(direc, image))
        sol = axpy(step, direc, sol)
        res = axpy(dd_neg(step), image, res)
        if it < ITERS - 1:
            new = form(res, res)
            direc = axpy(dd_div(new, norm), direc, res)
            norm = new
    fields = [r[...] for r in (v0, v1, v2, v3, v4)]

    def combine(coefs):
        total = None
        for c, f in zip(coefs, fields):
            term = c[0][0:1, 0:1] * f
            total = term if total is None else total + term
        return total

    tile = tile_ref[0]
    ids = lax.broadcasted_iota(jnp.int32, (64, 256), 1)
    want = lax.broadcasted_iota(jnp.int32, (64, 256), 0)
    swap = tile + 1 - 2 * (tile & 1)
    want = jnp.where(want < 32, tile * 32 + want, swap * 32 + want - 32)
    pick = jnp.where(ids == want, 1.0, 0.0).astype(jnp.bfloat16)
    for k, coefs in enumerate((sol, res)):
        parts = lax.dot_general(pick, split3(combine(coefs)), NT, preferred_element_type=F32)
        both = parts[:, :64] + (parts[:, 64:128] + parts[:, 128:192])
        mine_ref[k] = both[:32]
        other_ref[k] = both[32:]


def call(kernel, outs, n_in, scratch=(), smem=0, us=2.0):
    return pl.pallas_call(
        kernel,
        out_shape=[jax.ShapeDtypeStruct(s, d) for s, d in outs],
        in_specs=[pl.BlockSpec(memory_space=pltpu.SMEM)] * smem + [VMEM] * (n_in - smem),
        out_specs=[VMEM] * len(outs),
        scratch_shapes=[pltpu.VMEM(s, d) for s, d in scratch],
        compiler_params=pltpu.CompilerParams(vmem_limit_bytes=20 * 1024 * 1024),
        cost_estimate=pl.CostEstimate(flops=int(us * 1e9), bytes_accessed=1 << 18, transcendentals=0),
    )


def shifted(block, distance):
    devices = range(lax.axis_size("sec"))
    route = [(i - distance, i) for i in devices if i - distance in devices]
    return lax.ppermute(block, "sec", route)


def swapped(block):
    return lax.ppermute(block, "tile", [(i, i ^ 1) for i in range(8)])


def on_device(
    ov_first, ov_second, match_count, cell_first, cell_second, frac_first, frac_second, target, stiffness
):
    sec = lax.axis_index("sec")
    tile = lax.axis_index("tile")
    core = tile % 2
    sections = lax.axis_size("sec")
    second = ov_second // sections + jnp.where(ov_second % sections == sec, 0, 256)
    packed = call(pack_kernel, [((4, 264, 128), F32)], 9)(
        (ov_first // sections).reshape(1, 128),
        second.reshape(1, 128),
        match_count.reshape(1, 128),
        cell_first,
        cell_second,
        frac_first,
        frac_second,
        target,
        jnp.pad(stiffness.reshape(1, 32), ((0, 0), (0, 96))),
    )[0]
    groups = [[0, 2, 4, 6], [1, 3, 5, 7]]
    same = lax.all_to_all(packed, "tile", 0, 0, tiled=True, axis_index_groups=groups)
    other = swapped(same)
    pair = jnp.stack([same[:, 259, :32], other[:, 259, :32]])
    pair = jnp.where(core == 0, pair, pair[::-1])
    stiff = jnp.transpose(pair, (1, 0, 2)).reshape(1, 256)

    field = ((64, 256), F32)
    bf16 = jnp.bfloat16
    comp = core.reshape(1)
    wx, wy, fx, col, live, ohf, ohs, own, down = call(
        tables_kernel,
        [
            ((8, 2, 8, 32, 128), F32),
            ((8, 2, 8, 32, 128), F32),
            ((8, 2, 32, 128), F32),
            ((8, 2, 32, 128), jnp.int32),
            ((8, 32, 128), F32),
            ((256, 1024), bf16),
            ((512, 1024), bf16),
            field,
            field,
        ],
        3,
        [((2, 64, 1024), F32)],
        smem=1,
    )(comp, same, other)
    start_down = shifted(down, -1)
    half = call(stencil_kernel, [((2, 64, 256), F32)], 5, [((2, 64, 1024), F32)], smem=1, us=4.0)(
        comp, wx, wy, live, ohs
    )[0]
    mine = shifted(half, -1)
    other = swapped(mine)
    tables = (ohf, ohs, wx, wy, fx, col, live)
    wide = ((64, 1024), F32)
    fields = [own - start_down]
    for k in range(ITERS):
        v = fields[-1]
        below = shifted(v, 1)
        part, down, gap = call(up_kernel, [field, field, ((8, 32, 128), F32)], 8, [wide, wide, wide])(v, *tables)
        above = shifted(down, -1)
        partial = call(functools.partial(down_kernel, back=k > 0), [field], 16, [wide, wide], smem=1)(
            comp, v, below, fields[max(k - 1, 0)], part, gap, mine, other, stiff, *tables
        )[0]
        fields.append(partial - above)
    gram = call(dots_kernel, [((1, 128), F32)], 5)(*fields)[0]
    gram = lax.all_to_all(jnp.broadcast_to(gram, (32, 128)), "sec", 0, 0, tiled=True)
    mine, other = call(
        finish_kernel, [((2, 32, 64), F32), ((2, 32, 64), F32)], 8, smem=1
    )(tile.reshape(1), gram, swapped(gram), *fields)
    other = swapped(other)
    first = jnp.where(core == 0, mine, other)
    last = jnp.where(core == 0, other, mine)
    out = jnp.concatenate([first, last], 2)[:, :, None, :]
    return (out[0], out[1])


def solution(mesh):
    in_specs = (
        P(("sec", "tile")),
        P(("sec", "tile")),
        P(("sec", "tile")),
        P(None, ("sec", "tile")),
        P(None, ("sec", "tile")),
        P(None, None, ("sec", "tile")),
        P(None, None, ("sec", "tile")),
        P(None, None, ("sec", "tile")),
        P("tile", "sec"),
    )
    out_specs = (P("tile", "sec", None), P("tile", "sec", None))
    return jax.shard_map(
        on_device, mesh=mesh, in_specs=in_specs, out_specs=out_specs, check_vma=False
    )
```

```python
import functools

import jax
import jax.numpy as jnp
from jax import lax
from jax.experimental import pallas as pl
from jax.experimental.pallas import tpu as pltpu
from jax.sharding import PartitionSpec as P

ITERS = 4
DAMPING = 0.5
SHIFT = 10.0
SCALE = 1.0 / 128.0
BACK = 25.0 / 16384.0
PAIRS = [(i, j) for i in range(5) for j in range(i, 5) if (i, j) != (4, 4)]
VMEM = pl.BlockSpec(memory_space=pltpu.VMEM)
F32 = jnp.float32
NT = (((1,), (1,)), ((), ()))


def split3(x):
    a = x.astype(jnp.bfloat16)
    rest = x - a.astype(F32)
    b = rest.astype(jnp.bfloat16)
    c = (rest - b.astype(F32)).astype(jnp.bfloat16)
    return jnp.concatenate([a, b, c], 0)


def merge3(x):
    n = x.shape[0] // 3
    return x[:n] + (x[n : 2 * n] + x[2 * n :])


def sublane_ids():
    return lax.broadcasted_iota(jnp.int32, (8, 128), 0)


def fold_rows(parts):
    sub = sublane_ids()
    low = sub < 4
    half = [
        jnp.where(low, parts[p], parts[p + 4])
        + pltpu.roll(jnp.where(low, parts[p + 4], parts[p]), 4, 0)
        for p in range(4)
    ]
    two = (sub & 2) != 0
    quarter = [
        jnp.where(two, half[p + 2] + pltpu.roll(half[p + 2], 2, 0), half[p] + pltpu.roll(half[p], 6, 0))
        for p in range(2)
    ]
    one = (sub & 1) != 0
    return jnp.where(
        one, quarter[1] + pltpu.roll(quarter[1], 1, 0), quarter[0] + pltpu.roll(quarter[0], 7, 0)
    )


def spread_block(tops, sides, out_ref, lanes, lead=()):
    for q in range(8):
        parts = []
        for p in range(8):
            acc = tops[q][0] * sides[p][0]
            for group in range(1, 4):
                acc = acc + tops[q][group] * sides[p][group]
            parts.append(acc)
        out_ref[lead + (slice(8 * q, 8 * q + 8), lanes)] = fold_rows(parts)


def sample_block(rows_ref, lanes, wy_ref, fx_ref, col_ref, blk, side):
    out = []
    for group in range(4):
        ms = slice(8 * group, 8 * group + 8)
        col = col_ref[blk, side, ms, :]
        nxt = col + 1
        fx = fx_ref[blk, side, ms, :]
        acc = None
        for q in range(8):
            row = rows_ref[8 * q : 8 * q + 8, lanes]
            left = jnp.take_along_axis(row, col, axis=0, mode="promise_in_bounds")
            right = jnp.take_along_axis(row, nxt, axis=0, mode="promise_in_bounds")
            term = wy_ref[blk, side, q, ms, :] * (left + fx * (right - left))
            acc = term if acc is None else acc + term
        out.append(acc)
    return out


def load_table(ref, blk, side):
    return [[ref[blk, side, p, 8 * g : 8 * g + 8, :] for g in range(4)] for p in range(8)]


def lanes_of(blk):
    return pl.ds(pl.multiple_of(blk * 128, 128), 128)


def pack_kernel(
    place_ref, first_hbm, second_hbm, count_hbm, cell1_hbm, cell2_hbm, frac1_hbm, frac2_hbm, target_hbm, stiff_hbm,
    out_ref, ids_ref, stiff_ref, cell_ref, sem, *, sections
):
    copies = [
        pltpu.make_async_copy(cell1_hbm, cell_ref.at[0], sem.at[0]),
        pltpu.make_async_copy(cell2_hbm, cell_ref.at[1], sem.at[1]),
        pltpu.make_async_copy(first_hbm, ids_ref.at[0], sem.at[2]),
        pltpu.make_async_copy(second_hbm, ids_ref.at[1], sem.at[3]),
        pltpu.make_async_copy(count_hbm, ids_ref.at[2], sem.at[4]),
        pltpu.make_async_copy(stiff_hbm, stiff_ref, sem.at[5]),
    ]
    for k, src in enumerate((frac1_hbm, frac2_hbm, target_hbm)):
        for c in range(2):
            at = 64 + 64 * k + 32 * c
            copies.append(pltpu.make_async_copy(src.at[c], out_ref.at[at : at + 32, :], sem.at[6 + 2 * k + c]))
    for copy in copies:
        copy.start()
    for copy in copies:
        copy.wait()
    out_ref[0:32, :] = cell_ref[0].astype(F32)
    out_ref[32:64, :] = cell_ref[1].astype(F32)
    shift = sections.bit_length() - 1
    first = ids_ref[0] >> shift
    second = ids_ref[1] >> shift
    second = second + jnp.where((ids_ref[1] & (sections - 1)) == place_ref[0], 0, 256)
    tile = place_ref[1]
    stiff = jnp.concatenate([stiff_ref[...], jnp.zeros((1, 96), F32)], 1)
    stiff = pltpu.roll(jnp.broadcast_to(stiff, (8, 128)), 32 * (tile & 3), 1)
    row = sublane_ids()
    tail = jnp.where((row >= 3) & (row - 3 == (tile >> 2)), stiff, 0.0)
    for k, x in enumerate((first, second, ids_ref[2])):
        tail = jnp.where(row == k, jnp.broadcast_to(x.astype(F32), (8, 128)), tail)
    out_ref[256:264, :] = tail


def tables_kernel(comp_ref, *refs, blocks, add):
    datas = refs[:blocks]
    refs = refs[blocks:]
    if add:
        before_own, before_down, before_stiff = refs[:3]
        refs = refs[3:]
    wx_ref, wy_ref, fx_ref, col_ref, live_ref, ohf_ref, ohs_ref, own_ref, down_ref, stiff_ref, f_ref = refs
    comp = comp_ref[0]
    for blk, data_ref in enumerate(datas):
        lanes = slice(128 * blk, 128 * blk + 128)
        count = data_ref[258, :][None, :]
        goal = []
        for group in range(4):
            ms = slice(8 * group, 8 * group + 8)
            slot = (sublane_ids() + 8 * group).astype(F32)
            live = slot < count
            live_ref[blk, ms, :] = jnp.where(live, SCALE, 0.0)
            at = pl.multiple_of(192 + 32 * comp + 8 * group, 8)
            goal.append(jnp.where(live, data_ref[pl.ds(at, 8), :], 0.0))
        first = data_ref[256, :][None, :].astype(jnp.int32)
        second = data_ref[257, :][None, :].astype(jnp.int32)
        ids = lax.broadcasted_iota(jnp.int32, (256, 128), 0)
        ohf_ref[:, lanes] = jnp.where(ids == first, 1.0, 0.0).astype(jnp.bfloat16)
        ohs_ref[0:256, lanes] = jnp.where(ids == second, 1.0, 0.0).astype(jnp.bfloat16)
        ohs_ref[256:512, lanes] = jnp.where(ids + 256 == second, 1.0, 0.0).astype(jnp.bfloat16)
        for side in range(2):
            for group in range(4):
                ms = slice(8 * group, 8 * group + 8)
                at = 32 * side + 8 * group
                cell = data_ref[at : at + 8, :].astype(jnp.int32)
                base = 64 + 64 * side + 8 * group
                fx = data_ref[base : base + 8, :]
                fy = data_ref[base + 32 : base + 40, :]
                row = (cell * 37) >> 8
                col = cell - 7 * row
                fx_ref[blk, side, ms, :] = fx
                col_ref[blk, side, ms, :] = col
                for k in range(8):
                    wx_ref[blk, side, k, ms, :] = jnp.where(
                        col == k, 1.0 - fx, jnp.where(col == k - 1, fx, 0.0)
                    )
                    wy_ref[blk, side, k, ms, :] = jnp.where(
                        row == k, 1.0 - fy, jnp.where(row == k - 1, fy, 0.0)
                    )
            tops = load_table(wy_ref, blk, side)
            tops = [[tops[q][g] * goal[g] for g in range(4)] for q in range(8)]
            spread_block(tops, load_table(wx_ref, blk, side), f_ref, lanes, (side,))
    at_first = merge3(lax.dot_general(split3(f_ref[0]), ohf_ref[...], NT, preferred_element_type=F32))
    at_second = merge3(lax.dot_general(split3(f_ref[1]), ohs_ref[...], NT, preferred_element_type=F32))
    own = at_first - at_second[:, :256]
    down = at_second[:, 256:]
    stiff = jnp.concatenate(
        [sum(data_ref[row : row + 1, :] for data_ref in datas) for row in (259, 260)], 1
    )
    if add:
        own = own + before_own[...]
        down = down + before_down[...]
        stiff = stiff + before_stiff[...]
    own_ref[...] = own
    down_ref[...] = down
    stiff_ref[...] = stiff


def stencil_kernel(comp_ref, wx1, wy1, live1, ohs1, wx2, wy2, live2, ohs2, half_ref, f_ref):
    step = comp_ref[0]
    for h, (wx_ref, wy_ref, live_ref) in enumerate(((wx1, wy1, live1), (wx2, wy2, live2))):

        def body(blk, carry):
            lanes = lanes_of(blk + 4 * h)
            live = [live_ref[blk, 8 * g : 8 * g + 8, :] for g in range(4)]
            zero = [jnp.zeros((8, 128), F32)] * 4
            wy = load_table(wy_ref, blk, 1) + [zero]
            tops = [
                [wy[q][g] * jnp.where(step == 0, wy[q][g], wy[q + 1][g]) * live[g] for g in range(4)]
                for q in range(8)
            ]
            for kind in range(2):
                wx = load_table(wx_ref, blk, 1) + [zero]
                sides = [[wx[p][g] * wx[p + kind][g] for g in range(4)] for p in range(8)]
                spread_block(tops, sides, f_ref, lanes, (kind,))
            return carry

        lax.fori_loop(0, 4, body, 0)
    for kind in range(2):
        half_ref[kind] = scatter(f_ref[kind], ohs1[256:512, :], ohs2[256:512, :])


def gather(parts, hot1, hot2, out_ref):
    out_ref[:, 0:512] = merge3(jnp.dot(parts, hot1, preferred_element_type=F32))
    out_ref[:, 512:1024] = merge3(jnp.dot(parts, hot2, preferred_element_type=F32))


def scatter(forces, hot1, hot2):
    parts = split3(forces)
    return merge3(
        lax.dot_general(parts[:, 0:512], hot1, NT, preferred_element_type=F32)
        + lax.dot_general(parts[:, 512:1024], hot2, NT, preferred_element_type=F32)
    )


def up_kernel(v_ref, *refs):
    halves_of = (refs[:7], refs[7:14])
    own_ref, down_ref, gap_ref, g_ref, h_ref, f_ref = refs[14:]
    parts = split3(v_ref[...])
    ohf1, ohs1 = refs[0], refs[1]
    ohf2, ohs2 = refs[7], refs[8]
    gather(parts, ohf1[...], ohf2[...], g_ref)
    gather(parts, ohs1[0:256, :], ohs2[0:256, :], h_ref)
    for h, (_, _, wx_ref, wy_ref, fx_ref, col_ref, live_ref) in enumerate(halves_of):

        def body(blk, carry):
            lanes = lanes_of(blk + 4 * h)
            got = sample_block(g_ref, lanes, wy_ref, fx_ref, col_ref, blk, 0)
            less = sample_block(h_ref, lanes, wy_ref, fx_ref, col_ref, blk, 1)
            gap = [(got[g] - less[g]) * live_ref[blk, 8 * g : 8 * g + 8, :] for g in range(4)]
            for g in range(4):
                gap_ref[blk + 4 * h, 8 * g : 8 * g + 8, :] = gap[g]
            tops = load_table(wy_ref, blk, 1)
            tops = [[tops[q][g] * gap[g] for g in range(4)] for q in range(8)]
            spread_block(tops, load_table(wx_ref, blk, 1), f_ref, lanes)
            return carry

        lax.fori_loop(0, 4, body, 0)
    forces = scatter(f_ref[...], ohs1[...], ohs2[...])
    own_ref[...] = forces[:, :256]
    down_ref[...] = forces[:, 256:]


def down_kernel(
    comp_ref, v_ref, below_ref, prev_ref, part_ref, gap_ref, mine_ref, other_ref, stiff_ref, *refs, back
):
    halves_of = (refs[:7], refs[7:14])
    out_ref, g_ref, f_ref = refs[14:]
    ohf1, ohs1 = refs[0], refs[1]
    ohf2, ohs2 = refs[7], refs[8]
    gather(split3(below_ref[...]), ohs1[256:512, :], ohs2[256:512, :], g_ref)
    for h, (_, _, wx_ref, wy_ref, fx_ref, col_ref, live_ref) in enumerate(halves_of):

        def body(blk, carry):
            lanes = lanes_of(blk + 4 * h)
            got = sample_block(g_ref, lanes, wy_ref, fx_ref, col_ref, blk, 1)
            gap = [
                gap_ref[blk + 4 * h, 8 * g : 8 * g + 8, :] - got[g] * live_ref[blk, 8 * g : 8 * g + 8, :]
                for g in range(4)
            ]
            tops = load_table(wy_ref, blk, 0)
            tops = [[tops[q][g] * gap[g] for g in range(4)] for q in range(8)]
            spread_block(tops, load_table(wx_ref, blk, 0), f_ref, lanes)
            return carry

        lax.fori_loop(0, 4, body, 0)
    forces = scatter(f_ref[...], ohf1[...], ohf2[...])
    v = v_ref[...]
    up = lambda x, d: pltpu.roll(x, 64 - d, 0)
    dn = lambda x, d: pltpu.roll(x, d, 0)
    node = lax.broadcasted_iota(jnp.int32, (64, 256), 0)
    right = jnp.where((node & 7) < 7, up(v, 1) - v, 0.0)
    below = jnp.where(node < 56, up(v, 8) - v, 0.0)
    bend = (dn(right, 1) - right) + (dn(below, 8) - below)
    total = forces - part_ref[...] + (stiff_ref[...] * SCALE) * bend + ((DAMPING - SHIFT) * SCALE) * v
    first = comp_ref[0] == 0
    band = [jnp.where(first, mine_ref[k], other_ref[k]) for k in range(2)]
    band += [jnp.where(first, other_ref[k], mine_ref[k]) for k in range(2)]
    total = total + band[0] * v
    total = total + band[1] * up(v, 1) + dn(band[1] * v, 1)
    total = total + band[2] * up(v, 8) + dn(band[2] * v, 8)
    total = total + band[3] * up(v, 9) + dn(band[3] * v, 9)
    total = total + dn(band[3] * up(v, 8), 1) + dn(band[3] * up(v, 1), 8)
    if back:
        total = total - BACK * prev_ref[...]
    out_ref[...] = total


def two_sum(a, b):
    s = a + b
    t = s - a
    return s, (a - (s - t)) + (b - t)


def halves(a):
    c = 4097.0 * a
    high = c - (c - a)
    return high, a - high


def two_prod(a, b):
    p = a * b
    ah, al = halves(a)
    bh, bl = halves(b)
    return p, ((ah * bh - p) + ah * bl + al * bh) + al * bl


def quick(a, b):
    s = a + b
    return s, b - (s - a)


def dd_add(x, y):
    s, e = two_sum(x[0], y[0])
    return quick(s, e + (x[1] + y[1]))


def dd_mul(x, y):
    p, e = two_prod(x[0], y[0])
    return quick(p, e + (x[0] * y[1] + x[1] * y[0]))


def dd_neg(x):
    return (-x[0], -x[1])


def dd_div(x, y):
    q = x[0] / y[0]
    rest = dd_add(x, dd_neg(dd_mul(y, (q, jnp.zeros_like(q)))))
    return quick(q, rest[0] / y[0])


def dots_kernel(*refs):
    out_ref = refs[5]
    fields = [r[...] for r in refs[:5]]
    sub = lax.broadcasted_iota(jnp.int32, (16, 128), 0)
    lane = lax.broadcasted_iota(jnp.int32, (16, 128), 1)
    high = jnp.zeros((16, 128), F32)
    low = jnp.zeros((16, 128), F32)
    for k, (i, j) in enumerate(PAIRS):
        acc = two_prod(fields[i], fields[j])
        acc = dd_add((acc[0][:, :128], acc[1][:, :128]), (acc[0][:, 128:], acc[1][:, 128:]))
        n = 64
        while n > 8:
            n //= 2
            acc = dd_add((acc[0][:n], acc[1][:n]), (acc[0][n:], acc[1][n:]))
        for d in (4, 2, 1):
            acc = dd_add(acc, (pltpu.roll(acc[0], d, 0), pltpu.roll(acc[1], d, 0)))
        wide = [jnp.concatenate([a, a], 0) for a in acc]
        high = jnp.where(sub == k, wide[0], high)
        low = jnp.where(sub == k, wide[1], low)
    acc = (high, low)
    for d in (64, 32, 16, 8, 4, 2, 1):
        acc = dd_add(acc, (pltpu.roll(acc[0], d, 1), pltpu.roll(acc[1], d, 1)))
    row = jnp.where(lane == sub, acc[0], 0.0) + jnp.where(lane == sub + 16, acc[1], 0.0)
    out_ref[...] = jnp.sum(row, 0, keepdims=True)


def finish_kernel(tile_ref, gram_ref, gram2_ref, v0, v1, v2, v3, v4, mine_ref, other_ref):
    rows = jnp.concatenate([gram_ref[...], gram2_ref[...]], 0)
    acc = (rows, pltpu.roll(rows, 112, 1))
    n = 64
    while n > 8:
        n //= 2
        acc = dd_add((acc[0][:n], acc[1][:n]), (acc[0][n:], acc[1][n:]))
    for d in (4, 2, 1):
        acc = dd_add(acc, (pltpu.roll(acc[0], d, 0), pltpu.roll(acc[1], d, 0)))
    gram = {}
    for k, (i, j) in enumerate(PAIRS):
        pair = tuple(jnp.broadcast_to(a[:, k : k + 1], (8, 128)) for a in acc)
        gram[(i, j)] = pair
        gram[(j, i)] = pair
    zero = jnp.zeros((8, 128), F32)
    const = lambda c: (jnp.full((8, 128), c, F32), zero)

    def form(a, b):
        total = None
        for j, bj in enumerate(b):
            inner = None
            for i, ai in enumerate(a):
                term = dd_mul(ai, gram[(i, j)])
                inner = term if inner is None else dd_add(inner, term)
            inner = dd_mul(inner, bj)
            total = inner if total is None else dd_add(total, inner)
        return total

    def apply(p):
        out = [const(0.0) for _ in range(len(p) + 1)]
        for k, c in enumerate(p):
            out[k + 1] = dd_add(out[k + 1], (c[0] * 128.0, c[1] * 128.0))
            out[k] = dd_add(out[k], dd_mul(c, const(SHIFT)))
            if k >= 1:
                out[k - 1] = dd_add(out[k - 1], dd_mul(c, const(BACK * 128.0)))
        return out

    def axpy(a, x, y):
        out = []
        for k in range(max(len(x), len(y))):
            if k >= len(x):
                out.append(y[k])
            elif k >= len(y):
                out.append(dd_mul(a, x[k]))
            else:
                out.append(dd_add(y[k], dd_mul(a, x[k])))
        return out

    res = [const(1.0)]
    direc = [const(1.0)]
    sol = []
    norm = gram[(0, 0)]
    for it in range(ITERS):
        image = apply(direc)
        step = dd_div(norm, form(direc, image))
        sol = axpy(step, direc, sol)
        res = axpy(dd_neg(step), image, res)
        if it < ITERS - 1:
            new = form(res, res)
            direc = axpy(dd_div(new, norm), direc, res)
            norm = new
    fields = [r[...] for r in (v0, v1, v2, v3, v4)]

    def combine(coefs):
        total = None
        for c, f in zip(coefs, fields):
            term = c[0][0:1, 0:1] * f
            total = term if total is None else total + term
        return total

    tile = tile_ref[0]
    ids = lax.broadcasted_iota(jnp.int32, (64, 256), 1)
    want = lax.broadcasted_iota(jnp.int32, (64, 256), 0)
    swap = tile + 1 - 2 * (tile & 1)
    want = jnp.where(want < 32, tile * 32 + want, swap * 32 + want - 32)
    pick = jnp.where(ids == want, 1.0, 0.0).astype(jnp.bfloat16)
    for k, coefs in enumerate((sol, res)):
        parts = lax.dot_general(pick, split3(combine(coefs)), NT, preferred_element_type=F32)
        both = parts[:, :64] + (parts[:, 64:128] + parts[:, 128:192])
        mine_ref[k] = both[:32]
        other_ref[k] = both[32:]


def call(kernel, outs, n_in, scratch=(), smem=0, us=2.0, hbm=0, grant=8):
    return pl.pallas_call(
        kernel,
        out_shape=[jax.ShapeDtypeStruct(s, d) for s, d in outs],
        in_specs=[pl.BlockSpec(memory_space=pltpu.SMEM)] * smem
        + [VMEM] * (n_in - smem - hbm)
        + [pl.BlockSpec(memory_space=pl.ANY)] * hbm,
        out_specs=[VMEM] * len(outs),
        scratch_shapes=list(scratch),
        compiler_params=pltpu.CompilerParams(vmem_limit_bytes=grant * 1024 * 1024),
        cost_estimate=pl.CostEstimate(flops=int(us * 1e9), bytes_accessed=1 << 18, transcendentals=0),
    )


ROW = 4


def seat(section):
    row, col = divmod(section, ROW)
    return row * ROW + (col if row % 2 == 0 else ROW - 1 - col)


def shifted(block, distance):
    devices = range(lax.axis_size("sec"))
    route = [(seat(i), seat(i + distance)) for i in devices if i + distance in devices]
    return lax.ppermute(block, "sec", route)


def swapped(block):
    return lax.ppermute(block, "tile", [(i, i ^ 1) for i in range(8)])


def moved(block, step, flip):
    route = []
    for section in range(lax.axis_size("sec")):
        for tile in range(8):
            to = ((tile // 2 + step) % 4) * 2 + (tile % 2 ^ flip)
            route.append((section * 8 + tile, seat(section) * 8 + to))
    return lax.ppermute(block, ("sec", "tile"), route)


def on_device(
    ov_first, ov_second, match_count, cell_first, cell_second, frac_first, frac_second, target, stiffness
):
    tile = lax.axis_index("tile")
    core = tile % 2
    sections = lax.axis_size("sec")
    dma = pltpu.SemaphoreType.DMA
    packed = call(
        functools.partial(pack_kernel, sections=sections),
        [((264, 128), F32)],
        10,
        [
            pltpu.VMEM((3, 1, 128), jnp.int32),
            pltpu.VMEM((1, 32), F32),
            pltpu.VMEM((2, 32, 128), jnp.int32),
            dma((12,)),
        ],
        smem=1,
        hbm=9,
        grant=60,
    )(
        jnp.stack([lax.axis_index("sec"), tile]),
        ov_first.reshape(1, 128),
        ov_second.reshape(1, 128),
        match_count.reshape(1, 128),
        cell_first,
        cell_second,
        frac_first,
        frac_second,
        target,
        stiffness.reshape(1, 32),
    )[0]
    same = [moved(packed, step, 0) for step in (2, 1, 3, 0)]
    other = swapped(jnp.stack(same))

    field = ((64, 256), F32)
    bf16 = jnp.bfloat16
    comp = core.reshape(1)
    half_tables = [
        ((4, 2, 8, 32, 128), F32),
        ((4, 2, 8, 32, 128), F32),
        ((4, 2, 32, 128), F32),
        ((4, 2, 32, 128), jnp.int32),
        ((4, 32, 128), F32),
        ((256, 512), bf16),
        ((512, 512), bf16),
        field,
        field,
        ((1, 256), F32),
    ]
    work = [pltpu.VMEM((2, 64, 512), F32)]
    one = call(functools.partial(tables_kernel, blocks=4, add=False), half_tables, 5, work, smem=1)(comp, *same)
    two = call(functools.partial(tables_kernel, blocks=4, add=True), half_tables, 8, work, smem=1)(
        comp, other[0], other[1], other[2], other[3], *one[7:]
    )
    own, down, stiff = two[7:]
    start_down = shifted(down, -1)
    half = call(stencil_kernel, [((2, 64, 256), F32)], 9, [pltpu.VMEM((2, 64, 1024), F32)], smem=1, us=4.0)(
        comp, one[0], one[1], one[4], one[6], two[0], two[1], two[4], two[6]
    )[0]
    fields = [own - start_down]
    half, fields[0] = lax.optimization_barrier((half, fields[0]))
    mine = shifted(half, -1)
    other = swapped(mine)
    tables = []
    for wx, wy, fx, col, live, ohf, ohs in (one[:7], two[:7]):
        tables += [ohf, ohs, wx, wy, fx, col, live]
    wide = pltpu.VMEM((64, 1024), F32)
    for k in range(ITERS):
        v = fields[-1]
        below = shifted(v, 1)
        part, down, gap = call(up_kernel, [field, field, ((8, 32, 128), F32)], 15, [wide, wide, wide])(v, *tables)
        above = shifted(down, -1)
        partial = call(functools.partial(down_kernel, back=k > 0), [field], 23, [wide, wide], smem=1)(
            comp, v, below, fields[max(k - 1, 0)], part, gap, mine, other, stiff, *tables
        )[0]
        fields.append(partial - above)
    gram = call(dots_kernel, [((1, 128), F32)], 5)(*fields)[0]
    gram = lax.all_to_all(jnp.broadcast_to(gram, (32, 128)), "sec", 0, 0, tiled=True)
    mine, other = call(
        finish_kernel, [((2, 32, 64), F32), ((2, 32, 64), F32)], 8, smem=1
    )(tile.reshape(1), gram, swapped(gram), *fields)
    other = moved(other, 0, 1)
    mine = moved(mine, 0, 0)
    first = jnp.where(core == 0, mine, other)
    last = jnp.where(core == 0, other, mine)
    out = jnp.concatenate([first, last], 2)[:, :, None, :]
    return (out[0], out[1])


def solution(mesh):
    in_specs = (
        P(("sec", "tile")),
        P(("sec", "tile")),
        P(("sec", "tile")),
        P(None, ("sec", "tile")),
        P(None, ("sec", "tile")),
        P(None, None, ("sec", "tile")),
        P(None, None, ("sec", "tile")),
        P(None, None, ("sec", "tile")),
        P("tile", "sec"),
    )
    out_specs = (P("tile", "sec", None), P("tile", "sec", None))
    return jax.shard_map(
        on_device, mesh=mesh, in_specs=in_specs, out_specs=out_specs, check_vma=False
    )
```

```python
import functools

import jax
import jax.numpy as jnp
from jax import lax
from jax.experimental import pallas as pl
from jax.experimental.pallas import tpu as pltpu
from jax.sharding import PartitionSpec as P

ITERS = 4
DAMPING = 0.5
SHIFT = 10.0
SCALE = 1.0 / 128.0
BACK = 25.0 / 16384.0
PAIRS = [(i, j) for i in range(5) for j in range(i, 5) if (i, j) != (4, 4)]
VMEM = pl.BlockSpec(memory_space=pltpu.VMEM)
F32 = jnp.float32
NT = (((1,), (1,)), ((), ()))


def split3(x):
    a = x.astype(jnp.bfloat16)
    rest = x - a.astype(F32)
    b = rest.astype(jnp.bfloat16)
    c = (rest - b.astype(F32)).astype(jnp.bfloat16)
    return jnp.concatenate([a, b, c], 0)


def merge3(x):
    n = x.shape[0] // 3
    return x[:n] + (x[n : 2 * n] + x[2 * n :])


def sublane_ids():
    return lax.broadcasted_iota(jnp.int32, (8, 128), 0)


def fold_rows(parts):
    sub = sublane_ids()
    low = sub < 4
    half = [
        jnp.where(low, parts[p], parts[p + 4])
        + pltpu.roll(jnp.where(low, parts[p + 4], parts[p]), 4, 0)
        for p in range(4)
    ]
    two = (sub & 2) != 0
    quarter = [
        jnp.where(two, half[p + 2] + pltpu.roll(half[p + 2], 2, 0), half[p] + pltpu.roll(half[p], 6, 0))
        for p in range(2)
    ]
    one = (sub & 1) != 0
    return jnp.where(
        one, quarter[1] + pltpu.roll(quarter[1], 1, 0), quarter[0] + pltpu.roll(quarter[0], 7, 0)
    )


def spread_block(tops, sides, out_ref, lanes, lead=()):
    for q in range(8):
        parts = []
        for p in range(8):
            acc = tops[q][0] * sides[p][0]
            for group in range(1, 4):
                acc = acc + tops[q][group] * sides[p][group]
            parts.append(acc)
        out_ref[lead + (slice(8 * q, 8 * q + 8), lanes)] = fold_rows(parts)


def sample_block(rows_ref, lanes, wy_ref, fx_ref, col_ref, blk, side):
    out = []
    for group in range(4):
        ms = slice(8 * group, 8 * group + 8)
        col = col_ref[blk, side, ms, :]
        nxt = col + 1
        fx = fx_ref[blk, side, ms, :]
        acc = None
        for q in range(8):
            row = rows_ref[8 * q : 8 * q + 8, lanes]
            left = jnp.take_along_axis(row, col, axis=0, mode="promise_in_bounds")
            right = jnp.take_along_axis(row, nxt, axis=0, mode="promise_in_bounds")
            term = wy_ref[blk, side, q, ms, :] * (left + fx * (right - left))
            acc = term if acc is None else acc + term
        out.append(acc)
    return out


def load_table(ref, blk, side):
    return [[ref[blk, side, p, 8 * g : 8 * g + 8, :] for g in range(4)] for p in range(8)]


def lanes_of(blk):
    return pl.ds(pl.multiple_of(blk * 128, 128), 128)


def pack_kernel(
    first_hbm, second_hbm, count_hbm, cell1_hbm, cell2_hbm, frac1_hbm, frac2_hbm, target_hbm, stiff_hbm,
    out_ref, ids_ref, stiff_ref, cell_ref, sem, *, sections
):
    copies = [
        pltpu.make_async_copy(cell1_hbm, cell_ref.at[0], sem.at[0]),
        pltpu.make_async_copy(cell2_hbm, cell_ref.at[1], sem.at[1]),
        pltpu.make_async_copy(first_hbm, ids_ref.at[0], sem.at[2]),
        pltpu.make_async_copy(second_hbm, ids_ref.at[1], sem.at[3]),
        pltpu.make_async_copy(count_hbm, ids_ref.at[2], sem.at[4]),
        pltpu.make_async_copy(stiff_hbm, stiff_ref, sem.at[5]),
    ]
    for k, src in enumerate((frac1_hbm, frac2_hbm, target_hbm)):
        for c in range(2):
            at = 64 + 64 * k + 32 * c
            copies.append(pltpu.make_async_copy(src.at[c], out_ref.at[at : at + 32, :], sem.at[6 + 2 * k + c]))
    for copy in copies:
        copy.start()
    for copy in copies:
        copy.wait()
    out_ref[0:32, :] = cell_ref[0].astype(F32)
    out_ref[32:64, :] = cell_ref[1].astype(F32)
    shift = sections.bit_length() - 1
    first = ids_ref[0] >> shift
    second = ids_ref[1] >> shift
    second = second + jnp.where((ids_ref[1] & (sections - 1)) == lax.axis_index("sec"), 0, 256)
    tile = lax.axis_index("tile")
    stiff = jnp.concatenate([stiff_ref[...], jnp.zeros((1, 96), F32)], 1)
    stiff = pltpu.roll(jnp.broadcast_to(stiff, (8, 128)), 32 * (tile & 3), 1)
    row = sublane_ids()
    tail = jnp.where((row >= 3) & (row - 3 == (tile >> 2)), stiff, 0.0)
    for k, x in enumerate((first, second, ids_ref[2])):
        tail = jnp.where(row == k, jnp.broadcast_to(x.astype(F32), (8, 128)), tail)
    out_ref[256:264, :] = tail


def tables_kernel(*refs, blocks, add):
    datas = refs[:blocks]
    refs = refs[blocks:]
    if add:
        before_own, before_down, before_stiff = refs[:3]
        refs = refs[3:]
    wx_ref, wy_ref, fx_ref, col_ref, live_ref, ohf_ref, ohs_ref, own_ref, down_ref, stiff_ref, f_ref = refs
    comp = lax.axis_index("tile") & 1
    for blk, data_ref in enumerate(datas):
        lanes = slice(128 * blk, 128 * blk + 128)
        count = data_ref[258, :][None, :]
        goal = []
        for group in range(4):
            ms = slice(8 * group, 8 * group + 8)
            slot = (sublane_ids() + 8 * group).astype(F32)
            live = slot < count
            live_ref[blk, ms, :] = jnp.where(live, SCALE, 0.0)
            at = pl.multiple_of(192 + 32 * comp + 8 * group, 8)
            goal.append(jnp.where(live, data_ref[pl.ds(at, 8), :], 0.0))
        first = data_ref[256, :][None, :].astype(jnp.int32)
        second = data_ref[257, :][None, :].astype(jnp.int32)
        ids = lax.broadcasted_iota(jnp.int32, (256, 128), 0)
        ohf_ref[:, lanes] = jnp.where(ids == first, 1.0, 0.0).astype(jnp.bfloat16)
        ohs_ref[0:256, lanes] = jnp.where(ids == second, 1.0, 0.0).astype(jnp.bfloat16)
        ohs_ref[256:512, lanes] = jnp.where(ids + 256 == second, 1.0, 0.0).astype(jnp.bfloat16)
        for side in range(2):
            for group in range(4):
                ms = slice(8 * group, 8 * group + 8)
                at = 32 * side + 8 * group
                cell = data_ref[at : at + 8, :].astype(jnp.int32)
                base = 64 + 64 * side + 8 * group
                fx = data_ref[base : base + 8, :]
                fy = data_ref[base + 32 : base + 40, :]
                row = (cell * 37) >> 8
                col = cell - 7 * row
                fx_ref[blk, side, ms, :] = fx
                col_ref[blk, side, ms, :] = col
                for k in range(8):
                    wx_ref[blk, side, k, ms, :] = jnp.where(
                        col == k, 1.0 - fx, jnp.where(col == k - 1, fx, 0.0)
                    )
                    wy_ref[blk, side, k, ms, :] = jnp.where(
                        row == k, 1.0 - fy, jnp.where(row == k - 1, fy, 0.0)
                    )
            tops = load_table(wy_ref, blk, side)
            tops = [[tops[q][g] * goal[g] for g in range(4)] for q in range(8)]
            spread_block(tops, load_table(wx_ref, blk, side), f_ref, lanes, (side,))
    at_first = merge3(lax.dot_general(split3(f_ref[0]), ohf_ref[...], NT, preferred_element_type=F32))
    at_second = merge3(lax.dot_general(split3(f_ref[1]), ohs_ref[...], NT, preferred_element_type=F32))
    own = at_first - at_second[:, :256]
    down = at_second[:, 256:]
    stiff = jnp.concatenate(
        [sum(data_ref[row : row + 1, :] for data_ref in datas) for row in (259, 260)], 1
    )
    if add:
        own = own + before_own[...]
        down = down + before_down[...]
        stiff = stiff + before_stiff[...]
    own_ref[...] = own
    down_ref[...] = down
    stiff_ref[...] = stiff


def stencil_kernel(wx1, wy1, live1, ohs1, wx2, wy2, live2, ohs2, half_ref, f_ref):
    step = lax.axis_index("tile") & 1
    for h, (wx_ref, wy_ref, live_ref) in enumerate(((wx1, wy1, live1), (wx2, wy2, live2))):

        def body(blk, carry):
            lanes = lanes_of(blk + 4 * h)
            live = [live_ref[blk, 8 * g : 8 * g + 8, :] for g in range(4)]
            zero = [jnp.zeros((8, 128), F32)] * 4
            wy = load_table(wy_ref, blk, 1) + [zero]
            tops = [
                [wy[q][g] * jnp.where(step == 0, wy[q][g], wy[q + 1][g]) * live[g] for g in range(4)]
                for q in range(8)
            ]
            for kind in range(2):
                wx = load_table(wx_ref, blk, 1) + [zero]
                sides = [[wx[p][g] * wx[p + kind][g] for g in range(4)] for p in range(8)]
                spread_block(tops, sides, f_ref, lanes, (kind,))
            return carry

        lax.fori_loop(0, 4, body, 0)
    for kind in range(2):
        half_ref[kind] = scatter(f_ref[kind], ohs1[256:512, :], ohs2[256:512, :])


def gather(parts, hot1, hot2, out_ref):
    out_ref[:, 0:512] = merge3(jnp.dot(parts, hot1, preferred_element_type=F32))
    out_ref[:, 512:1024] = merge3(jnp.dot(parts, hot2, preferred_element_type=F32))


def scatter(forces, hot1, hot2):
    parts = split3(forces)
    return merge3(
        lax.dot_general(parts[:, 0:512], hot1, NT, preferred_element_type=F32)
        + lax.dot_general(parts[:, 512:1024], hot2, NT, preferred_element_type=F32)
    )


def up_kernel(v_ref, *refs):
    halves_of = (refs[:7], refs[7:14])
    own_ref, down_ref, gap_ref, g_ref, h_ref, f_ref = refs[14:]
    parts = split3(v_ref[...])
    ohf1, ohs1 = refs[0], refs[1]
    ohf2, ohs2 = refs[7], refs[8]
    gather(parts, ohf1[...], ohf2[...], g_ref)
    gather(parts, ohs1[0:256, :], ohs2[0:256, :], h_ref)
    for h, (_, _, wx_ref, wy_ref, fx_ref, col_ref, live_ref) in enumerate(halves_of):

        def body(blk, carry):
            lanes = lanes_of(blk + 4 * h)
            got = sample_block(g_ref, lanes, wy_ref, fx_ref, col_ref, blk, 0)
            less = sample_block(h_ref, lanes, wy_ref, fx_ref, col_ref, blk, 1)
            gap = [(got[g] - less[g]) * live_ref[blk, 8 * g : 8 * g + 8, :] for g in range(4)]
            for g in range(4):
                gap_ref[blk + 4 * h, 8 * g : 8 * g + 8, :] = gap[g]
            tops = load_table(wy_ref, blk, 1)
            tops = [[tops[q][g] * gap[g] for g in range(4)] for q in range(8)]
            spread_block(tops, load_table(wx_ref, blk, 1), f_ref, lanes)
            return carry

        lax.fori_loop(0, 4, body, 0)
    forces = scatter(f_ref[...], ohs1[...], ohs2[...])
    own_ref[...] = forces[:, :256]
    down_ref[...] = forces[:, 256:]


def down_kernel(
    v_ref, below_ref, prev_ref, part_ref, gap_ref, mine_ref, other_ref, stiff_ref, *refs, back
):
    halves_of = (refs[:7], refs[7:14])
    out_ref, g_ref, f_ref = refs[14:]
    ohf1, ohs1 = refs[0], refs[1]
    ohf2, ohs2 = refs[7], refs[8]
    gather(split3(below_ref[...]), ohs1[256:512, :], ohs2[256:512, :], g_ref)
    for h, (_, _, wx_ref, wy_ref, fx_ref, col_ref, live_ref) in enumerate(halves_of):

        def body(blk, carry):
            lanes = lanes_of(blk + 4 * h)
            got = sample_block(g_ref, lanes, wy_ref, fx_ref, col_ref, blk, 1)
            gap = [
                gap_ref[blk + 4 * h, 8 * g : 8 * g + 8, :] - got[g] * live_ref[blk, 8 * g : 8 * g + 8, :]
                for g in range(4)
            ]
            tops = load_table(wy_ref, blk, 0)
            tops = [[tops[q][g] * gap[g] for g in range(4)] for q in range(8)]
            spread_block(tops, load_table(wx_ref, blk, 0), f_ref, lanes)
            return carry

        lax.fori_loop(0, 4, body, 0)
    forces = scatter(f_ref[...], ohf1[...], ohf2[...])
    v = v_ref[...]
    up = lambda x, d: pltpu.roll(x, 64 - d, 0)
    dn = lambda x, d: pltpu.roll(x, d, 0)
    node = lax.broadcasted_iota(jnp.int32, (64, 256), 0)
    right = jnp.where((node & 7) < 7, up(v, 1) - v, 0.0)
    below = jnp.where(node < 56, up(v, 8) - v, 0.0)
    bend = (dn(right, 1) - right) + (dn(below, 8) - below)
    total = forces - part_ref[...] + (stiff_ref[...] * SCALE) * bend + ((DAMPING - SHIFT) * SCALE) * v
    first = (lax.axis_index("tile") & 1) == 0
    band = [jnp.where(first, mine_ref[k], other_ref[k]) for k in range(2)]
    band += [jnp.where(first, other_ref[k], mine_ref[k]) for k in range(2)]
    total = total + band[0] * v
    total = total + band[1] * up(v, 1) + dn(band[1] * v, 1)
    total = total + band[2] * up(v, 8) + dn(band[2] * v, 8)
    total = total + band[3] * up(v, 9) + dn(band[3] * v, 9)
    total = total + dn(band[3] * up(v, 8), 1) + dn(band[3] * up(v, 1), 8)
    if back:
        total = total - BACK * prev_ref[...]
    out_ref[...] = total


def two_sum(a, b):
    s = a + b
    t = s - a
    return s, (a - (s - t)) + (b - t)


def halves(a):
    c = 4097.0 * a
    high = c - (c - a)
    return high, a - high


def two_prod(a, b):
    p = a * b
    ah, al = halves(a)
    bh, bl = halves(b)
    return p, ((ah * bh - p) + ah * bl + al * bh) + al * bl


def quick(a, b):
    s = a + b
    return s, b - (s - a)


def dd_add(x, y):
    s, e = two_sum(x[0], y[0])
    return quick(s, e + (x[1] + y[1]))


def dd_mul(x, y):
    p, e = two_prod(x[0], y[0])
    return quick(p, e + (x[0] * y[1] + x[1] * y[0]))


def dd_neg(x):
    return (-x[0], -x[1])


def dd_div(x, y):
    q = x[0] / y[0]
    rest = dd_add(x, dd_neg(dd_mul(y, (q, jnp.zeros_like(q)))))
    return quick(q, rest[0] / y[0])


def dots_kernel(*refs):
    out_ref = refs[5]
    fields = [r[...] for r in refs[:5]]
    sub = lax.broadcasted_iota(jnp.int32, (16, 128), 0)
    lane = lax.broadcasted_iota(jnp.int32, (16, 128), 1)
    high = jnp.zeros((16, 128), F32)
    low = jnp.zeros((16, 128), F32)
    for k, (i, j) in enumerate(PAIRS):
        acc = two_prod(fields[i], fields[j])
        acc = dd_add((acc[0][:, :128], acc[1][:, :128]), (acc[0][:, 128:], acc[1][:, 128:]))
        n = 64
        while n > 8:
            n //= 2
            acc = dd_add((acc[0][:n], acc[1][:n]), (acc[0][n:], acc[1][n:]))
        for d in (4, 2, 1):
            acc = dd_add(acc, (pltpu.roll(acc[0], d, 0), pltpu.roll(acc[1], d, 0)))
        wide = [jnp.concatenate([a, a], 0) for a in acc]
        high = jnp.where(sub == k, wide[0], high)
        low = jnp.where(sub == k, wide[1], low)
    acc = (high, low)
    for d in (64, 32, 16, 8, 4, 2, 1):
        acc = dd_add(acc, (pltpu.roll(acc[0], d, 1), pltpu.roll(acc[1], d, 1)))
    row = jnp.where(lane == sub, acc[0], 0.0) + jnp.where(lane == sub + 16, acc[1], 0.0)
    out_ref[...] = jnp.sum(row, 0, keepdims=True)


def finish_kernel(gram_ref, gram2_ref, v0, v1, v2, v3, v4, mine_ref, other_ref):
    rows = jnp.concatenate([gram_ref[...], gram2_ref[...]], 0)
    acc = (rows, pltpu.roll(rows, 112, 1))
    n = 64
    while n > 8:
        n //= 2
        acc = dd_add((acc[0][:n], acc[1][:n]), (acc[0][n:], acc[1][n:]))
    for d in (4, 2, 1):
        acc = dd_add(acc, (pltpu.roll(acc[0], d, 0), pltpu.roll(acc[1], d, 0)))
    gram = {}
    for k, (i, j) in enumerate(PAIRS):
        pair = tuple(jnp.broadcast_to(a[:, k : k + 1], (8, 128)) for a in acc)
        gram[(i, j)] = pair
        gram[(j, i)] = pair
    zero = jnp.zeros((8, 128), F32)
    const = lambda c: (jnp.full((8, 128), c, F32), zero)

    def form(a, b):
        total = None
        for j, bj in enumerate(b):
            inner = None
            for i, ai in enumerate(a):
                term = dd_mul(ai, gram[(i, j)])
                inner = term if inner is None else dd_add(inner, term)
            inner = dd_mul(inner, bj)
            total = inner if total is None else dd_add(total, inner)
        return total

    def apply(p):
        out = [const(0.0) for _ in range(len(p) + 1)]
        for k, c in enumerate(p):
            out[k + 1] = dd_add(out[k + 1], (c[0] * 128.0, c[1] * 128.0))
            out[k] = dd_add(out[k], dd_mul(c, const(SHIFT)))
            if k >= 1:
                out[k - 1] = dd_add(out[k - 1], dd_mul(c, const(BACK * 128.0)))
        return out

    def axpy(a, x, y):
        out = []
        for k in range(max(len(x), len(y))):
            if k >= len(x):
                out.append(y[k])
            elif k >= len(y):
                out.append(dd_mul(a, x[k]))
            else:
                out.append(dd_add(y[k], dd_mul(a, x[k])))
        return out

    res = [const(1.0)]
    direc = [const(1.0)]
    sol = []
    norm = gram[(0, 0)]
    for it in range(ITERS):
        image = apply(direc)
        step = dd_div(norm, form(direc, image))
        sol = axpy(step, direc, sol)
        res = axpy(dd_neg(step), image, res)
        if it < ITERS - 1:
            new = form(res, res)
            direc = axpy(dd_div(new, norm), direc, res)
            norm = new
    fields = [r[...] for r in (v0, v1, v2, v3, v4)]

    def combine(coefs):
        total = None
        for c, f in zip(coefs, fields):
            term = c[0][0:1, 0:1] * f
            total = term if total is None else total + term
        return total

    tile = lax.axis_index("tile")
    ids = lax.broadcasted_iota(jnp.int32, (64, 256), 1)
    want = lax.broadcasted_iota(jnp.int32, (64, 256), 0)
    swap = tile + 1 - 2 * (tile & 1)
    want = jnp.where(want < 32, tile * 32 + want, swap * 32 + want - 32)
    pick = jnp.where(ids == want, 1.0, 0.0).astype(jnp.bfloat16)
    for k, coefs in enumerate((sol, res)):
        parts = lax.dot_general(pick, split3(combine(coefs)), NT, preferred_element_type=F32)
        both = parts[:, :64] + (parts[:, 64:128] + parts[:, 128:192])
        mine_ref[k] = both[:32]
        other_ref[k] = both[32:]


def call(kernel, outs, n_in, scratch=(), us=2.0, hbm=0, grant=8):
    return pl.pallas_call(
        kernel,
        out_shape=[jax.ShapeDtypeStruct(s, d) for s, d in outs],
        in_specs=[VMEM] * (n_in - hbm)
        + [pl.BlockSpec(memory_space=pl.ANY)] * hbm,
        out_specs=[VMEM] * len(outs),
        scratch_shapes=list(scratch),
        compiler_params=pltpu.CompilerParams(vmem_limit_bytes=grant * 1024 * 1024),
        cost_estimate=pl.CostEstimate(flops=int(us * 1e9), bytes_accessed=1 << 18, transcendentals=0),
    )


ROW = 4
CHIPS = 4


def seat(section, y, sections):
    row, col = divmod(section, ROW)
    col = col if row % 2 == 0 else ROW - 1 - col
    row = row if y % 2 == 0 else sections // ROW - 1 - row
    return row * ROW + col


def shifted(block, distance):
    sections = lax.axis_size("sec")
    route = []
    for section in range(sections):
        there = section + distance
        if not 0 <= there < sections:
            continue
        crosses = (section < sections // 2) != (there < sections // 2)
        for y in range(CHIPS):
            to = y ^ 1 if crosses else y
            for core in range(2):
                route.append(
                    (seat(section, y, sections) * 8 + 2 * y + core, seat(there, to, sections) * 8 + 2 * to + core)
                )
    return lax.ppermute(block, ("sec", "tile"), route)


def swapped(block):
    return lax.ppermute(block, "tile", [(i, i ^ 1) for i in range(8)])


def dealt(block, step):
    sections = lax.axis_size("sec")
    route = []
    for section in range(sections):
        for y in range(CHIPS):
            to = (y + step) % CHIPS
            for core in range(2):
                route.append((section * 8 + 2 * y + core, seat(section, to, sections) * 8 + 2 * to + core))
    return lax.ppermute(block, ("sec", "tile"), route)


def returned(block, flip):
    sections = lax.axis_size("sec")
    route = []
    for section in range(sections):
        for tile in range(2 * CHIPS):
            route.append((seat(section, tile // 2, sections) * 8 + tile, section * 8 + (tile ^ flip)))
    return lax.ppermute(block, ("sec", "tile"), route)


def on_device(
    ov_first, ov_second, match_count, cell_first, cell_second, frac_first, frac_second, target, stiffness
):
    tile = lax.axis_index("tile")
    core = tile % 2
    sections = lax.axis_size("sec")
    dma = pltpu.SemaphoreType.DMA
    packed = call(
        functools.partial(pack_kernel, sections=sections),
        [((264, 128), F32)],
        9,
        [
            pltpu.VMEM((3, 1, 128), jnp.int32),
            pltpu.VMEM((1, 32), F32),
            pltpu.VMEM((2, 32, 128), jnp.int32),
            dma((12,)),
        ],
        hbm=9,
        grant=60,
    )(
        ov_first.reshape(1, 128),
        ov_second.reshape(1, 128),
        match_count.reshape(1, 128),
        cell_first,
        cell_second,
        frac_first,
        frac_second,
        target,
        stiffness.reshape(1, 32),
    )[0]
    same = [dealt(packed, step) for step in (2, 1, 3, 0)]
    other = swapped(jnp.stack(same))

    field = ((64, 256), F32)
    bf16 = jnp.bfloat16
    half_tables = [
        ((4, 2, 8, 32, 128), F32),
        ((4, 2, 8, 32, 128), F32),
        ((4, 2, 32, 128), F32),
        ((4, 2, 32, 128), jnp.int32),
        ((4, 32, 128), F32),
        ((256, 512), bf16),
        ((512, 512), bf16),
        field,
        field,
        ((1, 256), F32),
    ]
    work = [pltpu.VMEM((2, 64, 512), F32)]
    one = call(functools.partial(tables_kernel, blocks=4, add=False), half_tables, 4, work)(*same)
    two = call(functools.partial(tables_kernel, blocks=4, add=True), half_tables, 7, work)(
        other[0], other[1], other[2], other[3], *one[7:]
    )
    own, down, stiff = two[7:]
    start_down = shifted(down, -1)
    half = call(stencil_kernel, [((2, 64, 256), F32)], 8, [pltpu.VMEM((2, 64, 1024), F32)], us=4.0)(
        one[0], one[1], one[4], one[6], two[0], two[1], two[4], two[6]
    )[0]
    fields = [own - start_down]
    half, fields[0] = lax.optimization_barrier((half, fields[0]))
    mine = shifted(half, -1)
    other = swapped(mine)
    tables = []
    for wx, wy, fx, col, live, ohf, ohs in (one[:7], two[:7]):
        tables += [ohf, ohs, wx, wy, fx, col, live]
    wide = pltpu.VMEM((64, 1024), F32)
    for k in range(ITERS):
        v = fields[-1]
        below = shifted(v, 1)
        part, down, gap = call(up_kernel, [field, field, ((8, 32, 128), F32)], 15, [wide, wide, wide])(v, *tables)
        above = shifted(down, -1)
        partial = call(functools.partial(down_kernel, back=k > 0), [field], 22, [wide, wide])(
            v, below, fields[max(k - 1, 0)], part, gap, mine, other, stiff, *tables
        )[0]
        fields.append(partial - above)
    gram = call(dots_kernel, [((1, 128), F32)], 5)(*fields)[0]
    gram = lax.all_to_all(jnp.broadcast_to(gram, (32, 128)), "sec", 0, 0, tiled=True)
    mine, other = call(
        finish_kernel, [((2, 32, 64), F32), ((2, 32, 64), F32)], 7
    )(gram, swapped(gram), *fields)
    other = returned(other, 1)
    mine = returned(mine, 0)
    first = jnp.where(core == 0, mine, other)
    last = jnp.where(core == 0, other, mine)
    out = jnp.concatenate([first, last], 2)[:, :, None, :]
    return (out[0], out[1])


def solution(mesh):
    in_specs = (
        P(("sec", "tile")),
        P(("sec", "tile")),
        P(("sec", "tile")),
        P(None, ("sec", "tile")),
        P(None, ("sec", "tile")),
        P(None, None, ("sec", "tile")),
        P(None, None, ("sec", "tile")),
        P(None, None, ("sec", "tile")),
        P("tile", "sec"),
    )
    out_specs = (P("tile", "sec", None), P("tile", "sec", None))
    return jax.shard_map(
        on_device, mesh=mesh, in_specs=in_specs, out_specs=out_specs, check_vma=False
    )
```

```python
import functools

import jax
import jax.numpy as jnp
from jax import lax
from jax.experimental import pallas as pl
from jax.experimental.pallas import tpu as pltpu
from jax.sharding import PartitionSpec as P

ITERS = 4
DAMPING = 0.5
SHIFT = 10.0
SCALE = 1.0 / 128.0
BACK = 25.0 / 16384.0
PAIRS = [(i, j) for i in range(5) for j in range(i, 5) if (i, j) != (4, 4)]
VMEM = pl.BlockSpec(memory_space=pltpu.VMEM)
F32 = jnp.float32
NT = (((1,), (1,)), ((), ()))


def split3(x):
    a = x.astype(jnp.bfloat16)
    rest = x - a.astype(F32)
    b = rest.astype(jnp.bfloat16)
    c = (rest - b.astype(F32)).astype(jnp.bfloat16)
    return jnp.concatenate([a, b, c], 0)


def merge3(x):
    n = x.shape[0] // 3
    return x[:n] + (x[n : 2 * n] + x[2 * n :])


def sublane_ids():
    return lax.broadcasted_iota(jnp.int32, (8, 128), 0)


def fold_rows(parts):
    sub = sublane_ids()
    low = sub < 4
    half = [
        jnp.where(low, parts[p], parts[p + 4])
        + pltpu.roll(jnp.where(low, parts[p + 4], parts[p]), 4, 0)
        for p in range(4)
    ]
    two = (sub & 2) != 0
    quarter = [
        jnp.where(two, half[p + 2] + pltpu.roll(half[p + 2], 2, 0), half[p] + pltpu.roll(half[p], 6, 0))
        for p in range(2)
    ]
    one = (sub & 1) != 0
    return jnp.where(
        one, quarter[1] + pltpu.roll(quarter[1], 1, 0), quarter[0] + pltpu.roll(quarter[0], 7, 0)
    )


def spread_block(tops, sides, out_ref, lanes, lead=()):
    for q in range(8):
        parts = []
        for p in range(8):
            acc = tops[q][0] * sides[p][0]
            for group in range(1, 4):
                acc = acc + tops[q][group] * sides[p][group]
            parts.append(acc)
        out_ref[lead + (slice(8 * q, 8 * q + 8), lanes)] = fold_rows(parts)


def sample_block(rows_ref, lanes, wy_ref, fx_ref, col_ref, blk, side):
    out = []
    for group in range(4):
        ms = slice(8 * group, 8 * group + 8)
        col = col_ref[blk, side, ms, :]
        nxt = col + 1
        fx = fx_ref[blk, side, ms, :]
        acc = None
        for q in range(8):
            row = rows_ref[8 * q : 8 * q + 8, lanes]
            left = jnp.take_along_axis(row, col, axis=0, mode="promise_in_bounds")
            right = jnp.take_along_axis(row, nxt, axis=0, mode="promise_in_bounds")
            term = wy_ref[blk, side, q, ms, :] * (left + fx * (right - left))
            acc = term if acc is None else acc + term
        out.append(acc)
    return out


def load_table(ref, blk, side):
    return [[ref[blk, side, p, 8 * g : 8 * g + 8, :] for g in range(4)] for p in range(8)]


def lanes_of(blk):
    return pl.ds(pl.multiple_of(blk * 128, 128), 128)


def pack_kernel(
    first_hbm, second_hbm, count_hbm, cell1_hbm, cell2_hbm, frac1_hbm, frac2_hbm, target_hbm, stiff_hbm,
    out_ref, ids_ref, stiff_ref, cell_ref, sem, *, sections
):
    copies = [
        pltpu.make_async_copy(cell1_hbm, cell_ref.at[0], sem.at[0]),
        pltpu.make_async_copy(cell2_hbm, cell_ref.at[1], sem.at[1]),
        pltpu.make_async_copy(first_hbm, ids_ref.at[0], sem.at[2]),
        pltpu.make_async_copy(second_hbm, ids_ref.at[1], sem.at[3]),
        pltpu.make_async_copy(count_hbm, ids_ref.at[2], sem.at[4]),
        pltpu.make_async_copy(stiff_hbm, stiff_ref, sem.at[5]),
    ]
    for k, src in enumerate((frac1_hbm, frac2_hbm, target_hbm)):
        for c in range(2):
            at = 64 + 64 * k + 32 * c
            copies.append(pltpu.make_async_copy(src.at[c], out_ref.at[at : at + 32, :], sem.at[6 + 2 * k + c]))
    for copy in copies:
        copy.start()
    for copy in copies:
        copy.wait()
    out_ref[0:32, :] = cell_ref[0].astype(F32)
    out_ref[32:64, :] = cell_ref[1].astype(F32)
    shift = sections.bit_length() - 1
    first = ids_ref[0] >> shift
    second = ids_ref[1] >> shift
    second = second + jnp.where((ids_ref[1] & (sections - 1)) == lax.axis_index("sec"), 0, 256)
    tile = lax.axis_index("tile")
    stiff = jnp.concatenate([stiff_ref[...], jnp.zeros((1, 96), F32)], 1)
    stiff = pltpu.roll(jnp.broadcast_to(stiff, (8, 128)), 32 * (tile & 3), 1)
    row = sublane_ids()
    tail = jnp.where((row >= 3) & (row - 3 == (tile >> 2)), stiff, 0.0)
    for k, x in enumerate((first, second, ids_ref[2])):
        tail = jnp.where(row == k, jnp.broadcast_to(x.astype(F32), (8, 128)), tail)
    out_ref[256:264, :] = tail


def tables_kernel(*refs, blocks, add):
    datas = refs[:blocks]
    refs = refs[blocks:]
    if add:
        before_own, before_down, before_stiff = refs[:3]
        refs = refs[3:]
    wx_ref, wy_ref, fx_ref, col_ref, live_ref, ohf_ref, ohs_ref, own_ref, down_ref, stiff_ref, f_ref = refs
    comp = lax.axis_index("tile") & 1
    for blk, data_ref in enumerate(datas):
        lanes = slice(128 * blk, 128 * blk + 128)
        count = data_ref[258, :][None, :]
        goal = []
        for group in range(4):
            ms = slice(8 * group, 8 * group + 8)
            slot = (sublane_ids() + 8 * group).astype(F32)
            live = slot < count
            live_ref[blk, ms, :] = jnp.where(live, SCALE, 0.0)
            at = pl.multiple_of(192 + 32 * comp + 8 * group, 8)
            goal.append(jnp.where(live, data_ref[pl.ds(at, 8), :], 0.0))
        first = data_ref[256, :][None, :].astype(jnp.int32)
        second = data_ref[257, :][None, :].astype(jnp.int32)
        ids = lax.broadcasted_iota(jnp.int32, (256, 128), 0)
        ohf_ref[:, lanes] = jnp.where(ids == first, 1.0, 0.0).astype(jnp.bfloat16)
        ohs_ref[0:256, lanes] = jnp.where(ids == second, 1.0, 0.0).astype(jnp.bfloat16)
        ohs_ref[256:512, lanes] = jnp.where(ids + 256 == second, 1.0, 0.0).astype(jnp.bfloat16)
        for side in range(2):
            for group in range(4):
                ms = slice(8 * group, 8 * group + 8)
                at = 32 * side + 8 * group
                cell = data_ref[at : at + 8, :].astype(jnp.int32)
                base = 64 + 64 * side + 8 * group
                fx = data_ref[base : base + 8, :]
                fy = data_ref[base + 32 : base + 40, :]
                row = (cell * 37) >> 8
                col = cell - 7 * row
                fx_ref[blk, side, ms, :] = fx
                col_ref[blk, side, ms, :] = col
                for k in range(8):
                    wx_ref[blk, side, k, ms, :] = jnp.where(
                        col == k, 1.0 - fx, jnp.where(col == k - 1, fx, 0.0)
                    )
                    wy_ref[blk, side, k, ms, :] = jnp.where(
                        row == k, 1.0 - fy, jnp.where(row == k - 1, fy, 0.0)
                    )
            tops = load_table(wy_ref, blk, side)
            tops = [[tops[q][g] * goal[g] for g in range(4)] for q in range(8)]
            spread_block(tops, load_table(wx_ref, blk, side), f_ref, lanes, (side,))
    at_first = merge3(lax.dot_general(split3(f_ref[0]), ohf_ref[...], NT, preferred_element_type=F32))
    at_second = merge3(lax.dot_general(split3(f_ref[1]), ohs_ref[...], NT, preferred_element_type=F32))
    own = at_first - at_second[:, :256]
    down = at_second[:, 256:]
    stiff = jnp.concatenate(
        [sum(data_ref[row : row + 1, :] for data_ref in datas) for row in (259, 260)], 1
    )
    if add:
        own = own + before_own[...]
        down = down + before_down[...]
        stiff = stiff + before_stiff[...]
    own_ref[...] = own
    down_ref[...] = down
    stiff_ref[...] = stiff


def stencil_kernel(wx1, wy1, live1, ohs1, wx2, wy2, live2, ohs2, half_ref, f_ref):
    step = lax.axis_index("tile") & 1
    for h, (wx_ref, wy_ref, live_ref) in enumerate(((wx1, wy1, live1), (wx2, wy2, live2))):

        def body(blk, carry):
            lanes = lanes_of(blk + 4 * h)
            live = [live_ref[blk, 8 * g : 8 * g + 8, :] for g in range(4)]
            zero = [jnp.zeros((8, 128), F32)] * 4
            wy = load_table(wy_ref, blk, 1) + [zero]
            tops = [
                [wy[q][g] * jnp.where(step == 0, wy[q][g], wy[q + 1][g]) * live[g] for g in range(4)]
                for q in range(8)
            ]
            for kind in range(2):
                wx = load_table(wx_ref, blk, 1) + [zero]
                sides = [[wx[p][g] * wx[p + kind][g] for g in range(4)] for p in range(8)]
                spread_block(tops, sides, f_ref, lanes, (kind,))
            return carry

        lax.fori_loop(0, 4, body, 0)
    for kind in range(2):
        half_ref[kind] = scatter(f_ref[kind], ohs1[256:512, :], ohs2[256:512, :])


def gather(parts, hot1, hot2, out_ref):
    out_ref[:, 0:512] = merge3(jnp.dot(parts, hot1, preferred_element_type=F32))
    out_ref[:, 512:1024] = merge3(jnp.dot(parts, hot2, preferred_element_type=F32))


def scatter(forces, hot1, hot2):
    parts = split3(forces)
    return merge3(
        lax.dot_general(parts[:, 0:512], hot1, NT, preferred_element_type=F32)
        + lax.dot_general(parts[:, 512:1024], hot2, NT, preferred_element_type=F32)
    )


def up_kernel(v_ref, *refs):
    halves_of = (refs[:7], refs[7:14])
    own_ref, down_ref, gap_ref, g_ref, h_ref, f_ref = refs[14:]
    parts = split3(v_ref[...])
    ohf1, ohs1 = refs[0], refs[1]
    ohf2, ohs2 = refs[7], refs[8]
    gather(parts, ohf1[...], ohf2[...], g_ref)
    gather(parts, ohs1[0:256, :], ohs2[0:256, :], h_ref)
    for h, (_, _, wx_ref, wy_ref, fx_ref, col_ref, live_ref) in enumerate(halves_of):

        def body(blk, carry):
            lanes = lanes_of(blk + 4 * h)
            got = sample_block(g_ref, lanes, wy_ref, fx_ref, col_ref, blk, 0)
            less = sample_block(h_ref, lanes, wy_ref, fx_ref, col_ref, blk, 1)
            gap = [(got[g] - less[g]) * live_ref[blk, 8 * g : 8 * g + 8, :] for g in range(4)]
            for g in range(4):
                gap_ref[blk + 4 * h, 8 * g : 8 * g + 8, :] = gap[g]
            tops = load_table(wy_ref, blk, 1)
            tops = [[tops[q][g] * gap[g] for g in range(4)] for q in range(8)]
            spread_block(tops, load_table(wx_ref, blk, 1), f_ref, lanes)
            return carry

        lax.fori_loop(0, 4, body, 0)
    forces = scatter(f_ref[...], ohs1[...], ohs2[...])
    own_ref[...] = forces[:, :256]
    down_ref[...] = forces[:, 256:]


def down_kernel(
    v_ref, raw_ref, sent_ref, prev_ref, part_ref, gap_ref, mine_ref, other_ref, stiff_ref, *refs, back
):
    halves_of = (refs[:7], refs[7:14])
    out_ref, g_ref, f_ref = refs[14:]
    ohf1, ohs1 = refs[0], refs[1]
    ohf2, ohs2 = refs[7], refs[8]
    gather(split3(raw_ref[...] - sent_ref[...]), ohs1[256:512, :], ohs2[256:512, :], g_ref)
    for h, (_, _, wx_ref, wy_ref, fx_ref, col_ref, live_ref) in enumerate(halves_of):

        def body(blk, carry):
            lanes = lanes_of(blk + 4 * h)
            got = sample_block(g_ref, lanes, wy_ref, fx_ref, col_ref, blk, 1)
            gap = [
                gap_ref[blk + 4 * h, 8 * g : 8 * g + 8, :] - got[g] * live_ref[blk, 8 * g : 8 * g + 8, :]
                for g in range(4)
            ]
            tops = load_table(wy_ref, blk, 0)
            tops = [[tops[q][g] * gap[g] for g in range(4)] for q in range(8)]
            spread_block(tops, load_table(wx_ref, blk, 0), f_ref, lanes)
            return carry

        lax.fori_loop(0, 4, body, 0)
    forces = scatter(f_ref[...], ohf1[...], ohf2[...])
    v = v_ref[...]
    up = lambda x, d: pltpu.roll(x, 64 - d, 0)
    dn = lambda x, d: pltpu.roll(x, d, 0)
    node = lax.broadcasted_iota(jnp.int32, (64, 256), 0)
    right = jnp.where((node & 7) < 7, up(v, 1) - v, 0.0)
    below = jnp.where(node < 56, up(v, 8) - v, 0.0)
    bend = (dn(right, 1) - right) + (dn(below, 8) - below)
    total = forces - part_ref[...] + (stiff_ref[...] * SCALE) * bend + ((DAMPING - SHIFT) * SCALE) * v
    first = (lax.axis_index("tile") & 1) == 0
    band = [jnp.where(first, mine_ref[k], other_ref[k]) for k in range(2)]
    band += [jnp.where(first, other_ref[k], mine_ref[k]) for k in range(2)]
    total = total + band[0] * v
    total = total + band[1] * up(v, 1) + dn(band[1] * v, 1)
    total = total + band[2] * up(v, 8) + dn(band[2] * v, 8)
    total = total + band[3] * up(v, 9) + dn(band[3] * v, 9)
    total = total + dn(band[3] * up(v, 8), 1) + dn(band[3] * up(v, 1), 8)
    if back:
        total = total - BACK * prev_ref[...]
    out_ref[...] = total


def two_sum(a, b):
    s = a + b
    t = s - a
    return s, (a - (s - t)) + (b - t)


def halves(a):
    c = 4097.0 * a
    high = c - (c - a)
    return high, a - high


def two_prod(a, b):
    p = a * b
    ah, al = halves(a)
    bh, bl = halves(b)
    return p, ((ah * bh - p) + ah * bl + al * bh) + al * bl


def quick(a, b):
    s = a + b
    return s, b - (s - a)


def dd_add(x, y):
    s, e = two_sum(x[0], y[0])
    return quick(s, e + (x[1] + y[1]))


def dd_mul(x, y):
    p, e = two_prod(x[0], y[0])
    return quick(p, e + (x[0] * y[1] + x[1] * y[0]))


def dd_neg(x):
    return (-x[0], -x[1])


def dd_div(x, y):
    q = x[0] / y[0]
    rest = dd_add(x, dd_neg(dd_mul(y, (q, jnp.zeros_like(q)))))
    return quick(q, rest[0] / y[0])


def dots_kernel(*refs):
    out_ref = refs[5]
    fields = [r[...] for r in refs[:5]]
    sub = lax.broadcasted_iota(jnp.int32, (16, 128), 0)
    lane = lax.broadcasted_iota(jnp.int32, (16, 128), 1)
    high = jnp.zeros((16, 128), F32)
    low = jnp.zeros((16, 128), F32)
    for k, (i, j) in enumerate(PAIRS):
        acc = two_prod(fields[i], fields[j])
        acc = dd_add((acc[0][:, :128], acc[1][:, :128]), (acc[0][:, 128:], acc[1][:, 128:]))
        n = 64
        while n > 8:
            n //= 2
            acc = dd_add((acc[0][:n], acc[1][:n]), (acc[0][n:], acc[1][n:]))
        for d in (4, 2, 1):
            acc = dd_add(acc, (pltpu.roll(acc[0], d, 0), pltpu.roll(acc[1], d, 0)))
        wide = [jnp.concatenate([a, a], 0) for a in acc]
        high = jnp.where(sub == k, wide[0], high)
        low = jnp.where(sub == k, wide[1], low)
    acc = (high, low)
    for d in (64, 32, 16, 8, 4, 2, 1):
        acc = dd_add(acc, (pltpu.roll(acc[0], d, 1), pltpu.roll(acc[1], d, 1)))
    row = jnp.where(lane == sub, acc[0], 0.0) + jnp.where(lane == sub + 16, acc[1], 0.0)
    out_ref[...] = jnp.sum(row, 0, keepdims=True)


def finish_kernel(gram_ref, gram2_ref, v0, v1, v2, v3, v4, mine_ref, other_ref):
    rows = jnp.concatenate([gram_ref[...], gram2_ref[...]], 0)
    acc = (rows, pltpu.roll(rows, 112, 1))
    n = 64
    while n > 8:
        n //= 2
        acc = dd_add((acc[0][:n], acc[1][:n]), (acc[0][n:], acc[1][n:]))
    for d in (4, 2, 1):
        acc = dd_add(acc, (pltpu.roll(acc[0], d, 0), pltpu.roll(acc[1], d, 0)))
    gram = {}
    for k, (i, j) in enumerate(PAIRS):
        pair = tuple(jnp.broadcast_to(a[:, k : k + 1], (8, 128)) for a in acc)
        gram[(i, j)] = pair
        gram[(j, i)] = pair
    zero = jnp.zeros((8, 128), F32)
    const = lambda c: (jnp.full((8, 128), c, F32), zero)

    def form(a, b):
        total = None
        for j, bj in enumerate(b):
            inner = None
            for i, ai in enumerate(a):
                term = dd_mul(ai, gram[(i, j)])
                inner = term if inner is None else dd_add(inner, term)
            inner = dd_mul(inner, bj)
            total = inner if total is None else dd_add(total, inner)
        return total

    def apply(p):
        out = [const(0.0) for _ in range(len(p) + 1)]
        for k, c in enumerate(p):
            out[k + 1] = dd_add(out[k + 1], (c[0] * 128.0, c[1] * 128.0))
            out[k] = dd_add(out[k], dd_mul(c, const(SHIFT)))
            if k >= 1:
                out[k - 1] = dd_add(out[k - 1], dd_mul(c, const(BACK * 128.0)))
        return out

    def axpy(a, x, y):
        out = []
        for k in range(max(len(x), len(y))):
            if k >= len(x):
                out.append(y[k])
            elif k >= len(y):
                out.append(dd_mul(a, x[k]))
            else:
                out.append(dd_add(y[k], dd_mul(a, x[k])))
        return out

    res = [const(1.0)]
    direc = [const(1.0)]
    sol = []
    norm = gram[(0, 0)]
    for it in range(ITERS):
        image = apply(direc)
        step = dd_div(norm, form(direc, image))
        sol = axpy(step, direc, sol)
        res = axpy(dd_neg(step), image, res)
        if it < ITERS - 1:
            new = form(res, res)
            direc = axpy(dd_div(new, norm), direc, res)
            norm = new
    fields = [r[...] for r in (v0, v1, v2, v3, v4)]

    def combine(coefs):
        total = None
        for c, f in zip(coefs, fields):
            term = c[0][0:1, 0:1] * f
            total = term if total is None else total + term
        return total

    tile = lax.axis_index("tile")
    ids = lax.broadcasted_iota(jnp.int32, (64, 256), 1)
    want = lax.broadcasted_iota(jnp.int32, (64, 256), 0)
    swap = tile + 1 - 2 * (tile & 1)
    want = jnp.where(want < 32, tile * 32 + want, swap * 32 + want - 32)
    pick = jnp.where(ids == want, 1.0, 0.0).astype(jnp.bfloat16)
    for k, coefs in enumerate((sol, res)):
        parts = lax.dot_general(pick, split3(combine(coefs)), NT, preferred_element_type=F32)
        both = parts[:, :64] + (parts[:, 64:128] + parts[:, 128:192])
        mine_ref[k] = both[:32]
        other_ref[k] = both[32:]


def call(kernel, outs, n_in, scratch=(), us=2.0, hbm=0, grant=8):
    return pl.pallas_call(
        kernel,
        out_shape=[jax.ShapeDtypeStruct(s, d) for s, d in outs],
        in_specs=[VMEM] * (n_in - hbm)
        + [pl.BlockSpec(memory_space=pl.ANY)] * hbm,
        out_specs=[VMEM] * len(outs),
        scratch_shapes=list(scratch),
        compiler_params=pltpu.CompilerParams(vmem_limit_bytes=grant * 1024 * 1024),
        cost_estimate=pl.CostEstimate(flops=int(us * 1e9), bytes_accessed=1 << 18, transcendentals=0),
    )


ROW = 4
CHIPS = 4


def seat(section, y, sections):
    row, col = divmod(section, ROW)
    col = col if row % 2 == 0 else ROW - 1 - col
    row = row if y % 2 == 0 else sections // ROW - 1 - row
    return row * ROW + col


def shifted(block, distance):
    sections = lax.axis_size("sec")
    route = []
    for section in range(sections):
        there = section + distance
        if not 0 <= there < sections:
            continue
        crosses = (section < sections // 2) != (there < sections // 2)
        for y in range(CHIPS):
            to = y ^ 1 if crosses else y
            for core in range(2):
                route.append(
                    (seat(section, y, sections) * 8 + 2 * y + core, seat(there, to, sections) * 8 + 2 * to + core)
                )
    return lax.ppermute(block, ("sec", "tile"), route)


def swapped(block):
    return lax.ppermute(block, "tile", [(i, i ^ 1) for i in range(8)])


def dealt(block, step):
    sections = lax.axis_size("sec")
    route = []
    for section in range(sections):
        for y in range(CHIPS):
            to = (y + step) % CHIPS
            for core in range(2):
                route.append((section * 8 + 2 * y + core, seat(section, to, sections) * 8 + 2 * to + core))
    return lax.ppermute(block, ("sec", "tile"), route)


def returned(block, flip):
    sections = lax.axis_size("sec")
    route = []
    for section in range(sections):
        for tile in range(2 * CHIPS):
            route.append((seat(section, tile // 2, sections) * 8 + tile, section * 8 + (tile ^ flip)))
    return lax.ppermute(block, ("sec", "tile"), route)


def on_device(
    ov_first, ov_second, match_count, cell_first, cell_second, frac_first, frac_second, target, stiffness
):
    tile = lax.axis_index("tile")
    core = tile % 2
    sections = lax.axis_size("sec")
    dma = pltpu.SemaphoreType.DMA
    packed = call(
        functools.partial(pack_kernel, sections=sections),
        [((264, 128), F32)],
        9,
        [
            pltpu.VMEM((3, 1, 128), jnp.int32),
            pltpu.VMEM((1, 32), F32),
            pltpu.VMEM((2, 32, 128), jnp.int32),
            dma((12,)),
        ],
        hbm=9,
        grant=60,
    )(
        ov_first.reshape(1, 128),
        ov_second.reshape(1, 128),
        match_count.reshape(1, 128),
        cell_first,
        cell_second,
        frac_first,
        frac_second,
        target,
        stiffness.reshape(1, 32),
    )[0]
    same = [dealt(packed, step) for step in (2, 1, 3, 0)]
    other = swapped(jnp.stack(same))

    field = ((64, 256), F32)
    bf16 = jnp.bfloat16
    half_tables = [
        ((4, 2, 8, 32, 128), F32),
        ((4, 2, 8, 32, 128), F32),
        ((4, 2, 32, 128), F32),
        ((4, 2, 32, 128), jnp.int32),
        ((4, 32, 128), F32),
        ((256, 512), bf16),
        ((512, 512), bf16),
        field,
        field,
        ((1, 256), F32),
    ]
    work = [pltpu.VMEM((2, 64, 512), F32)]
    one = call(functools.partial(tables_kernel, blocks=4, add=False), half_tables, 4, work)(*same)
    two = call(functools.partial(tables_kernel, blocks=4, add=True), half_tables, 7, work)(
        other[0], other[1], other[2], other[3], *one[7:]
    )
    own, down, stiff = two[7:]
    above = shifted(down, -1)
    raw = shifted(own, 1)
    half = call(stencil_kernel, [((2, 64, 256), F32)], 8, [pltpu.VMEM((2, 64, 1024), F32)], us=4.0)(
        one[0], one[1], one[4], one[6], two[0], two[1], two[4], two[6]
    )[0]
    fields = [own - above]
    half, fields[0] = lax.optimization_barrier((half, fields[0]))
    mine = shifted(half, -1)
    other = swapped(mine)
    tables = []
    for wx, wy, fx, col, live, ohf, ohs in (one[:7], two[:7]):
        tables += [ohf, ohs, wx, wy, fx, col, live]
    wide = pltpu.VMEM((64, 1024), F32)
    for k in range(ITERS):
        v = fields[-1]
        sent = down
        part, down, gap = call(up_kernel, [field, field, ((8, 32, 128), F32)], 15, [wide, wide, wide])(v, *tables)
        above = shifted(down, -1)
        partial = call(functools.partial(down_kernel, back=k > 0), [field], 23, [wide, wide])(
            v, raw, sent, fields[max(k - 1, 0)], part, gap, mine, other, stiff, *tables
        )[0]
        if k < ITERS - 1:
            raw = shifted(partial, 1)
        fields.append(partial - above)
    gram = call(dots_kernel, [((1, 128), F32)], 5)(*fields)[0]
    gram = lax.all_to_all(jnp.broadcast_to(gram, (32, 128)), "sec", 0, 0, tiled=True)
    mine, other = call(
        finish_kernel, [((2, 32, 64), F32), ((2, 32, 64), F32)], 7
    )(gram, swapped(gram), *fields)
    other = returned(other, 1)
    mine = returned(mine, 0)
    first = jnp.where(core == 0, mine, other)
    last = jnp.where(core == 0, other, mine)
    out = jnp.concatenate([first, last], 2)[:, :, None, :]
    return (out[0], out[1])


def solution(mesh):
    in_specs = (
        P(("sec", "tile")),
        P(("sec", "tile")),
        P(("sec", "tile")),
        P(None, ("sec", "tile")),
        P(None, ("sec", "tile")),
        P(None, None, ("sec", "tile")),
        P(None, None, ("sec", "tile")),
        P(None, None, ("sec", "tile")),
        P("tile", "sec"),
    )
    out_specs = (P("tile", "sec", None), P("tile", "sec", None))
    return jax.shard_map(
        on_device, mesh=mesh, in_specs=in_specs, out_specs=out_specs, check_vma=False
    )
```

```python
import functools

import jax
import jax.numpy as jnp
from jax import lax
from jax.experimental import pallas as pl
from jax.experimental.pallas import tpu as pltpu
from jax.sharding import PartitionSpec as P

ITERS = 4
DAMPING = 0.5
SHIFT = 10.0
SCALE = 1.0 / 128.0
BACK = 25.0 / 16384.0
PAIRS = [(i, j) for i in range(5) for j in range(i, 5) if (i, j) != (4, 4)]
VMEM = pl.BlockSpec(memory_space=pltpu.VMEM)
F32 = jnp.float32
NT = (((1,), (1,)), ((), ()))


def split3(x):
    a = x.astype(jnp.bfloat16)
    rest = x - a.astype(F32)
    b = rest.astype(jnp.bfloat16)
    c = (rest - b.astype(F32)).astype(jnp.bfloat16)
    return jnp.concatenate([a, b, c], 0)


def merge3(x):
    n = x.shape[0] // 3
    return x[:n] + (x[n : 2 * n] + x[2 * n :])


def sublane_ids():
    return lax.broadcasted_iota(jnp.int32, (8, 128), 0)


def fold_rows(parts):
    sub = sublane_ids()
    low = sub < 4
    half = [
        jnp.where(low, parts[p], parts[p + 4])
        + pltpu.roll(jnp.where(low, parts[p + 4], parts[p]), 4, 0)
        for p in range(4)
    ]
    two = (sub & 2) != 0
    quarter = [
        jnp.where(two, half[p + 2] + pltpu.roll(half[p + 2], 2, 0), half[p] + pltpu.roll(half[p], 6, 0))
        for p in range(2)
    ]
    one = (sub & 1) != 0
    return jnp.where(
        one, quarter[1] + pltpu.roll(quarter[1], 1, 0), quarter[0] + pltpu.roll(quarter[0], 7, 0)
    )


def spread_block(tops, sides, out_ref, lanes, lead=()):
    for q in range(8):
        parts = []
        for p in range(8):
            acc = tops[q][0] * sides[p][0]
            for group in range(1, 4):
                acc = acc + tops[q][group] * sides[p][group]
            parts.append(acc)
        out_ref[lead + (slice(8 * q, 8 * q + 8), lanes)] = fold_rows(parts)


def sample_block(rows_ref, lanes, wy_ref, fx_ref, col_ref, blk, side):
    out = []
    for group in range(4):
        ms = slice(8 * group, 8 * group + 8)
        col = col_ref[blk, side, ms, :]
        nxt = col + 1
        fx = fx_ref[blk, side, ms, :]
        acc = None
        for q in range(8):
            row = rows_ref[8 * q : 8 * q + 8, lanes]
            left = jnp.take_along_axis(row, col, axis=0, mode="promise_in_bounds")
            right = jnp.take_along_axis(row, nxt, axis=0, mode="promise_in_bounds")
            term = wy_ref[blk, side, q, ms, :] * (left + fx * (right - left))
            acc = term if acc is None else acc + term
        out.append(acc)
    return out


def load_table(ref, blk, side):
    return [[ref[blk, side, p, 8 * g : 8 * g + 8, :] for g in range(4)] for p in range(8)]


def lanes_of(blk):
    return pl.ds(pl.multiple_of(blk * 128, 128), 128)


def pack_kernel(
    first_hbm, second_hbm, count_hbm, cell1_hbm, cell2_hbm, frac1_hbm, frac2_hbm, target_hbm, stiff_hbm,
    out_ref, ids_ref, stiff_ref, cell_ref, sem, *, sections
):
    copies = [
        pltpu.make_async_copy(cell1_hbm, cell_ref.at[0], sem.at[0]),
        pltpu.make_async_copy(cell2_hbm, cell_ref.at[1], sem.at[1]),
        pltpu.make_async_copy(first_hbm, ids_ref.at[0], sem.at[2]),
        pltpu.make_async_copy(second_hbm, ids_ref.at[1], sem.at[3]),
        pltpu.make_async_copy(count_hbm, ids_ref.at[2], sem.at[4]),
        pltpu.make_async_copy(stiff_hbm, stiff_ref, sem.at[5]),
    ]
    for k, src in enumerate((frac1_hbm, frac2_hbm, target_hbm)):
        for c in range(2):
            at = 64 + 64 * k + 32 * c
            copies.append(pltpu.make_async_copy(src.at[c], out_ref.at[at : at + 32, :], sem.at[6 + 2 * k + c]))
    for copy in copies:
        copy.start()
    for copy in copies:
        copy.wait()
    out_ref[0:32, :] = cell_ref[0].astype(F32)
    out_ref[32:64, :] = cell_ref[1].astype(F32)
    shift = sections.bit_length() - 1
    first = ids_ref[0] >> shift
    second = ids_ref[1] >> shift
    second = second + jnp.where((ids_ref[1] & (sections - 1)) == lax.axis_index("sec"), 0, 256)
    tile = lax.axis_index("tile")
    stiff = jnp.concatenate([stiff_ref[...], jnp.zeros((1, 96), F32)], 1)
    stiff = pltpu.roll(jnp.broadcast_to(stiff, (8, 128)), 32 * (tile & 3), 1)
    row = sublane_ids()
    tail = jnp.where((row >= 3) & (row - 3 == (tile >> 2)), stiff, 0.0)
    for k, x in enumerate((first, second, ids_ref[2])):
        tail = jnp.where(row == k, jnp.broadcast_to(x.astype(F32), (8, 128)), tail)
    out_ref[256:264, :] = tail


def tables_kernel(*refs, blocks, add):
    datas = refs[:blocks]
    refs = refs[blocks:]
    if add:
        before_own, before_down, before_stiff = refs[:3]
        refs = refs[3:]
    wx_ref, wy_ref, fx_ref, col_ref, live_ref, ohf_ref, ohs_ref, own_ref, down_ref, stiff_ref, f_ref = refs
    comp = lax.axis_index("tile") & 1
    for blk, data_ref in enumerate(datas):
        lanes = slice(128 * blk, 128 * blk + 128)
        count = data_ref[258, :][None, :]
        goal = []
        for group in range(4):
            ms = slice(8 * group, 8 * group + 8)
            slot = (sublane_ids() + 8 * group).astype(F32)
            live = slot < count
            live_ref[blk, ms, :] = jnp.where(live, SCALE, 0.0)
            at = pl.multiple_of(192 + 32 * comp + 8 * group, 8)
            goal.append(jnp.where(live, data_ref[pl.ds(at, 8), :], 0.0))
        first = data_ref[256, :][None, :].astype(jnp.int32)
        second = data_ref[257, :][None, :].astype(jnp.int32)
        ids = lax.broadcasted_iota(jnp.int32, (256, 128), 0)
        ohf_ref[:, lanes] = jnp.where(ids == first, 1.0, 0.0).astype(jnp.bfloat16)
        ohs_ref[0:256, lanes] = jnp.where(ids == second, 1.0, 0.0).astype(jnp.bfloat16)
        ohs_ref[256:512, lanes] = jnp.where(ids + 256 == second, 1.0, 0.0).astype(jnp.bfloat16)
        for side in range(2):
            for group in range(4):
                ms = slice(8 * group, 8 * group + 8)
                at = 32 * side + 8 * group
                cell = data_ref[at : at + 8, :].astype(jnp.int32)
                base = 64 + 64 * side + 8 * group
                fx = data_ref[base : base + 8, :]
                fy = data_ref[base + 32 : base + 40, :]
                row = (cell * 37) >> 8
                col = cell - 7 * row
                fx_ref[blk, side, ms, :] = fx
                col_ref[blk, side, ms, :] = col
                for k in range(8):
                    wx_ref[blk, side, k, ms, :] = jnp.where(
                        col == k, 1.0 - fx, jnp.where(col == k - 1, fx, 0.0)
                    )
                    wy_ref[blk, side, k, ms, :] = jnp.where(
                        row == k, 1.0 - fy, jnp.where(row == k - 1, fy, 0.0)
                    )
            tops = load_table(wy_ref, blk, side)
            tops = [[tops[q][g] * goal[g] for g in range(4)] for q in range(8)]
            spread_block(tops, load_table(wx_ref, blk, side), f_ref, lanes, (side,))
    at_first = merge3(lax.dot_general(split3(f_ref[0]), ohf_ref[...], NT, preferred_element_type=F32))
    at_second = merge3(lax.dot_general(split3(f_ref[1]), ohs_ref[...], NT, preferred_element_type=F32))
    own = at_first - at_second[:, :256]
    down = at_second[:, 256:]
    stiff = jnp.concatenate(
        [sum(data_ref[row : row + 1, :] for data_ref in datas) for row in (259, 260)], 1
    )
    if add:
        own = own + before_own[...]
        down = down + before_down[...]
        stiff = stiff + before_stiff[...]
    own_ref[...] = own
    down_ref[...] = down
    stiff_ref[...] = stiff


def stencil_kernel(down_ref, wx1, wy1, live1, ohs1, wx2, wy2, live2, ohs2, send_ref, keep_ref, f_ref):
    step = lax.axis_index("tile") & 1
    send_ref[0] = down_ref[...]
    for h, (wx_ref, wy_ref, live_ref) in enumerate(((wx1, wy1, live1), (wx2, wy2, live2))):

        def body(blk, carry):
            lanes = lanes_of(blk + 4 * h)
            live = [live_ref[blk, 8 * g : 8 * g + 8, :] for g in range(4)]
            zero = [jnp.zeros((8, 128), F32)] * 4
            wy = load_table(wy_ref, blk, 1) + [zero]
            tops = [
                [wy[q][g] * jnp.where(step == 0, wy[q][g], wy[q + 1][g]) * live[g] for g in range(4)]
                for q in range(8)
            ]
            for kind in range(2):
                wx = load_table(wx_ref, blk, 1) + [zero]
                sides = [[wx[p][g] * wx[p + kind][g] for g in range(4)] for p in range(8)]
                spread_block(tops, sides, f_ref, lanes, (kind,))
            return carry

        lax.fori_loop(0, 4, body, 0)
    for kind in range(2):
        both = scatter(f_ref[kind], ohs1[...], ohs2[...])
        keep_ref[kind] = both[:, :256]
        send_ref[kind + 1] = both[:, 256:]


def gather(parts, hot1, hot2, out_ref):
    out_ref[:, 0:512] = merge3(jnp.dot(parts, hot1, preferred_element_type=F32))
    out_ref[:, 512:1024] = merge3(jnp.dot(parts, hot2, preferred_element_type=F32))


def scatter(forces, hot1, hot2):
    parts = split3(forces)
    return merge3(
        lax.dot_general(parts[:, 0:512], hot1, NT, preferred_element_type=F32)
        + lax.dot_general(parts[:, 512:1024], hot2, NT, preferred_element_type=F32)
    )


def up_kernel(v_ref, *refs):
    halves_of = (refs[:7], refs[7:14])
    own_ref, down_ref, gap_ref, g_ref, f_ref = refs[14:]
    ohf1, ohs1 = refs[0], refs[1]
    ohf2, ohs2 = refs[7], refs[8]
    gather(split3(v_ref[...]), ohf1[...], ohf2[...], g_ref)
    for h, (_, _, wx_ref, wy_ref, fx_ref, col_ref, live_ref) in enumerate(halves_of):

        def body(blk, carry):
            lanes = lanes_of(blk + 4 * h)
            got = sample_block(g_ref, lanes, wy_ref, fx_ref, col_ref, blk, 0)
            gap = [got[g] * live_ref[blk, 8 * g : 8 * g + 8, :] for g in range(4)]
            for g in range(4):
                gap_ref[blk + 4 * h, 8 * g : 8 * g + 8, :] = gap[g]
            tops = load_table(wy_ref, blk, 1)
            tops = [[tops[q][g] * gap[g] for g in range(4)] for q in range(8)]
            spread_block(tops, load_table(wx_ref, blk, 1), f_ref, lanes)
            return carry

        lax.fori_loop(0, 4, body, 0, unroll=2)
    forces = scatter(f_ref[...], ohs1[...], ohs2[...])
    own_ref[...] = forces[:, :256]
    down_ref[...] = forces[:, 256:]


def down_kernel(
    v_ref, raw_ref, sent_ref, prev_ref, part_ref, gap_ref, mine_ref, other_ref, stiff_ref, *refs, back
):
    halves_of = (refs[:7], refs[7:14])
    out_ref, g_ref, f_ref = refs[14:]
    ohf1, ohs1 = refs[0], refs[1]
    ohf2, ohs2 = refs[7], refs[8]
    v = v_ref[...]
    parts = jnp.concatenate([split3(v), split3(raw_ref[...] - sent_ref[...])], 1)
    gather(parts, ohs1[...], ohs2[...], g_ref)
    for h, (_, _, wx_ref, wy_ref, fx_ref, col_ref, live_ref) in enumerate(halves_of):

        def body(blk, carry):
            lanes = lanes_of(blk + 4 * h)
            got = sample_block(g_ref, lanes, wy_ref, fx_ref, col_ref, blk, 1)
            gap = [
                gap_ref[blk + 4 * h, 8 * g : 8 * g + 8, :] - got[g] * live_ref[blk, 8 * g : 8 * g + 8, :]
                for g in range(4)
            ]
            tops = load_table(wy_ref, blk, 0)
            tops = [[tops[q][g] * gap[g] for g in range(4)] for q in range(8)]
            spread_block(tops, load_table(wx_ref, blk, 0), f_ref, lanes)
            return carry

        lax.fori_loop(0, 4, body, 0, unroll=2)
    forces = scatter(f_ref[...], ohf1[...], ohf2[...])
    up = lambda x, d: pltpu.roll(x, 64 - d, 0)
    dn = lambda x, d: pltpu.roll(x, d, 0)
    node = lax.broadcasted_iota(jnp.int32, (64, 256), 0)
    right = jnp.where((node & 7) < 7, up(v, 1) - v, 0.0)
    below = jnp.where(node < 56, up(v, 8) - v, 0.0)
    bend = (dn(right, 1) - right) + (dn(below, 8) - below)
    total = forces - part_ref[...] + (stiff_ref[...] * SCALE) * bend + ((DAMPING - SHIFT) * SCALE) * v
    first = (lax.axis_index("tile") & 1) == 0
    band = [jnp.where(first, mine_ref[k], other_ref[k]) for k in range(2)]
    band += [jnp.where(first, other_ref[k], mine_ref[k]) for k in range(2)]
    total = total + band[0] * v
    total = total + band[1] * up(v, 1) + dn(band[1] * v, 1)
    total = total + band[2] * up(v, 8) + dn(band[2] * v, 8)
    total = total + band[3] * up(v, 9) + dn(band[3] * v, 9)
    total = total + dn(band[3] * up(v, 8), 1) + dn(band[3] * up(v, 1), 8)
    if back:
        total = total - BACK * prev_ref[...]
    out_ref[...] = total


def two_sum(a, b):
    s = a + b
    t = s - a
    return s, (a - (s - t)) + (b - t)


def halves(a):
    c = 4097.0 * a
    high = c - (c - a)
    return high, a - high


def two_prod(a, b):
    p = a * b
    ah, al = halves(a)
    bh, bl = halves(b)
    return p, ((ah * bh - p) + ah * bl + al * bh) + al * bl


def quick(a, b):
    s = a + b
    return s, b - (s - a)


def dd_add(x, y):
    s, e = two_sum(x[0], y[0])
    return quick(s, e + (x[1] + y[1]))


def dd_mul(x, y):
    p, e = two_prod(x[0], y[0])
    return quick(p, e + (x[0] * y[1] + x[1] * y[0]))


def dd_neg(x):
    return (-x[0], -x[1])


def dd_div(x, y):
    q = x[0] / y[0]
    rest = dd_add(x, dd_neg(dd_mul(y, (q, jnp.zeros_like(q)))))
    return quick(q, rest[0] / y[0])


def dots(fields, pairs):
    sub = lax.broadcasted_iota(jnp.int32, (16, 128), 0)
    lane = lax.broadcasted_iota(jnp.int32, (16, 128), 1)
    high = jnp.zeros((16, 128), F32)
    low = jnp.zeros((16, 128), F32)
    for i, j in pairs:
        acc = two_prod(fields[i], fields[j])
        acc = dd_add((acc[0][:, :128], acc[1][:, :128]), (acc[0][:, 128:], acc[1][:, 128:]))
        n = 64
        while n > 8:
            n //= 2
            acc = dd_add((acc[0][:n], acc[1][:n]), (acc[0][n:], acc[1][n:]))
        for d in (4, 2, 1):
            acc = dd_add(acc, (pltpu.roll(acc[0], d, 0), pltpu.roll(acc[1], d, 0)))
        wide = [jnp.concatenate([a, a], 0) for a in acc]
        here = sub == PAIRS.index((i, j))
        high = jnp.where(here, wide[0], high)
        low = jnp.where(here, wide[1], low)
    acc = (high, low)
    for d in (64, 32, 16, 8, 4, 2, 1):
        acc = dd_add(acc, (pltpu.roll(acc[0], d, 1), pltpu.roll(acc[1], d, 1)))
    row = jnp.where(lane == sub, acc[0], 0.0) + jnp.where(lane == sub + 16, acc[1], 0.0)
    return jnp.sum(row, 0, keepdims=True)


def dots_kernel(v0, v1, v2, v3, out_ref):
    out_ref[...] = dots([r[...] for r in (v0, v1, v2, v3)], [p for p in PAIRS if p[1] < 4])


def last_kernel(row_ref, v0, v1, v2, v3, v4, out_ref, slice_ref):
    fields = [r[...] for r in (v0, v1, v2, v3, v4)]
    y = lax.axis_index("tile") >> 1
    for k in range(3):
        sides = []
        for m in (2 * k, 2 * k + 1):
            if m < 5:
                x = jnp.where(y >= 2, fields[m][:, 128:], fields[m][:, :128])
                sides.append((x, pltpu.roll(x, 64, 1)))
            else:
                sides.append((jnp.zeros((64, 128), F32),) * 2)
        left = jnp.where((y & 1) == 0, sides[0][0], sides[0][1])
        right = jnp.where((y & 1) == 0, sides[1][1], sides[1][0])
        lane = lax.broadcasted_iota(jnp.int32, (64, 128), 1)
        slice_ref[k] = jnp.where(lane < 64, left, right)
    out_ref[...] = row_ref[...] + dots(fields, [p for p in PAIRS if p[1] == 4])


def finish_kernel(gram_ref, slice_ref, mine_ref, other_ref):
    rows = gram_ref[...]
    acc = dd_add((rows, pltpu.roll(rows, 112, 1)), (pltpu.roll(rows, 96, 1), pltpu.roll(rows, 80, 1)))
    n = 32
    while n > 8:
        n //= 2
        acc = dd_add((acc[0][:n], acc[1][:n]), (acc[0][n:], acc[1][n:]))
    for d in (4, 2, 1):
        acc = dd_add(acc, (pltpu.roll(acc[0], d, 0), pltpu.roll(acc[1], d, 0)))
    gram = {}
    for k, (i, j) in enumerate(PAIRS):
        pair = tuple(jnp.broadcast_to(a[:, k : k + 1], (8, 128)) for a in acc)
        gram[(i, j)] = pair
        gram[(j, i)] = pair
    zero = jnp.zeros((8, 128), F32)
    const = lambda c: (jnp.full((8, 128), c, F32), zero)

    def form(a, b):
        total = None
        for j, bj in enumerate(b):
            inner = None
            for i, ai in enumerate(a):
                term = dd_mul(ai, gram[(i, j)])
                inner = term if inner is None else dd_add(inner, term)
            inner = dd_mul(inner, bj)
            total = inner if total is None else dd_add(total, inner)
        return total

    def apply(p):
        out = [const(0.0) for _ in range(len(p) + 1)]
        for k, c in enumerate(p):
            out[k + 1] = dd_add(out[k + 1], (c[0] * 128.0, c[1] * 128.0))
            out[k] = dd_add(out[k], dd_mul(c, const(SHIFT)))
            if k >= 1:
                out[k - 1] = dd_add(out[k - 1], dd_mul(c, const(BACK * 128.0)))
        return out

    def axpy(a, x, y):
        out = []
        for k in range(max(len(x), len(y))):
            if k >= len(x):
                out.append(y[k])
            elif k >= len(y):
                out.append(dd_mul(a, x[k]))
            else:
                out.append(dd_add(y[k], dd_mul(a, x[k])))
        return out

    res = [const(1.0)]
    direc = [const(1.0)]
    sol = []
    norm = gram[(0, 0)]
    for it in range(ITERS):
        image = apply(direc)
        step = dd_div(norm, form(direc, image))
        sol = axpy(step, direc, sol)
        res = axpy(dd_neg(step), image, res)
        if it < ITERS - 1:
            new = form(res, res)
            direc = axpy(dd_div(new, norm), direc, res)
            norm = new
    lane = lax.broadcasted_iota(jnp.int32, (64, 128), 1)

    def combine(coefs):
        total = jnp.zeros((64, 128), F32)
        flat = [c[0][0:1, 0:1] for c in coefs] + [jnp.zeros((1, 1), F32)] * (6 - len(coefs))
        for k in range(3):
            total = total + jnp.where(lane < 64, flat[2 * k], flat[2 * k + 1]) * slice_ref[k]
        return total + pltpu.roll(total, 64, 1)

    core = lax.axis_index("tile") & 1
    want = lax.broadcasted_iota(jnp.int32, (64, 128), 0)
    want = jnp.where(want < 32, want + 32 * core, want - 32 * core)
    pick = jnp.where(lane == want, 1.0, 0.0).astype(jnp.bfloat16)
    for k, coefs in enumerate((sol, res)):
        parts = lax.dot_general(pick, split3(combine(coefs)), NT, preferred_element_type=F32)
        both = parts[:, :64] + (parts[:, 64:128] + parts[:, 128:192])
        mine_ref[k] = both[:32]
        other_ref[k] = both[32:]


def call(kernel, outs, n_in, scratch=(), us=2.0, hbm=0, grant=8):
    return pl.pallas_call(
        kernel,
        out_shape=[jax.ShapeDtypeStruct(s, d) for s, d in outs],
        in_specs=[VMEM] * (n_in - hbm)
        + [pl.BlockSpec(memory_space=pl.ANY)] * hbm,
        out_specs=[VMEM] * len(outs),
        scratch_shapes=list(scratch),
        compiler_params=pltpu.CompilerParams(vmem_limit_bytes=grant * 1024 * 1024),
        cost_estimate=pl.CostEstimate(flops=int(us * 1e9), bytes_accessed=1 << 18, transcendentals=0),
    )


ROW = 4
CHIPS = 4


def seat(section, y, sections):
    row, col = divmod(section, ROW)
    col = col if row % 2 == 0 else ROW - 1 - col
    row = row if y % 2 == 0 else sections // ROW - 1 - row
    return row * ROW + col


def shifted(block, distance):
    sections = lax.axis_size("sec")
    route = []
    for section in range(sections):
        there = section + distance
        if not 0 <= there < sections:
            continue
        crosses = (section < sections // 2) != (there < sections // 2)
        for y in range(CHIPS):
            to = y ^ 1 if crosses else y
            for core in range(2):
                route.append(
                    (seat(section, y, sections) * 8 + 2 * y + core, seat(there, to, sections) * 8 + 2 * to + core)
                )
    return lax.ppermute(block, ("sec", "tile"), route)


def swapped(block):
    return lax.ppermute(block, "tile", [(i, i ^ 1) for i in range(8)])


def dealt(block, step):
    sections = lax.axis_size("sec")
    route = []
    for section in range(sections):
        for y in range(CHIPS):
            to = (y + step) % CHIPS
            for core in range(2):
                route.append((section * 8 + 2 * y + core, seat(section, to, sections) * 8 + 2 * to + core))
    return lax.ppermute(block, ("sec", "tile"), route)


def returned(block):
    sections = lax.axis_size("sec")
    route = []
    for section in range(sections):
        for tile in range(2 * CHIPS):
            route.append((seat(section, tile // 2, sections) * 8 + tile, section * 8 + tile))
    return lax.ppermute(block, ("sec", "tile"), route)


def on_device(
    ov_first, ov_second, match_count, cell_first, cell_second, frac_first, frac_second, target, stiffness
):
    tile = lax.axis_index("tile")
    core = tile % 2
    sections = lax.axis_size("sec")
    dma = pltpu.SemaphoreType.DMA
    packed = call(
        functools.partial(pack_kernel, sections=sections),
        [((264, 128), F32)],
        9,
        [
            pltpu.VMEM((3, 1, 128), jnp.int32),
            pltpu.VMEM((1, 32), F32),
            pltpu.VMEM((2, 32, 128), jnp.int32),
            dma((12,)),
        ],
        hbm=9,
        grant=60,
    )(
        ov_first.reshape(1, 128),
        ov_second.reshape(1, 128),
        match_count.reshape(1, 128),
        cell_first,
        cell_second,
        frac_first,
        frac_second,
        target,
        stiffness.reshape(1, 32),
    )[0]
    same = [dealt(packed, step) for step in (2, 1, 3, 0)]
    other = swapped(jnp.stack(same))

    field = ((64, 256), F32)
    bf16 = jnp.bfloat16
    half_tables = [
        ((4, 2, 8, 32, 128), F32),
        ((4, 2, 8, 32, 128), F32),
        ((4, 2, 32, 128), F32),
        ((4, 2, 32, 128), jnp.int32),
        ((4, 32, 128), F32),
        ((256, 512), bf16),
        ((512, 512), bf16),
        field,
        field,
        ((1, 256), F32),
    ]
    work = [pltpu.VMEM((2, 64, 512), F32)]
    one = call(functools.partial(tables_kernel, blocks=4, add=False), half_tables, 4, work)(*same)
    two = call(functools.partial(tables_kernel, blocks=4, add=True), half_tables, 7, work)(
        other[0], other[1], other[2], other[3], *one[7:]
    )
    own, down, stiff = two[7:]
    send, keep = call(
        stencil_kernel, [((3, 64, 256), F32), ((2, 64, 256), F32)], 9, [pltpu.VMEM((2, 64, 1024), F32)], us=4.0
    )(down, one[0], one[1], one[4], one[6], two[0], two[1], two[4], two[6])
    above = shifted(send, -1)
    raw = shifted(own, 1)
    fields = [own - above[0]]
    mine = keep + above[1:]
    other = swapped(mine)
    tables = []
    for wx, wy, fx, col, live, ohf, ohs in (one[:7], two[:7]):
        tables += [ohf, ohs, wx, wy, fx, col, live]
    wide = pltpu.VMEM((64, 1024), F32)
    for k in range(ITERS):
        v = fields[-1]
        sent = down
        part, down, gap = call(up_kernel, [field, field, ((8, 32, 128), F32)], 15, [wide, wide])(v, *tables)
        above = shifted(down, -1)
        partial = call(functools.partial(down_kernel, back=k > 0), [field], 23, [wide, wide])(
            v, raw, sent, fields[max(k - 1, 0)], part, gap, mine, other, stiff, *tables
        )[0]
        if k < ITERS - 1:
            raw = shifted(partial, 1)
        fields.append(partial - above)
    row = call(dots_kernel, [((1, 128), F32)], 4, us=1.0)(*fields[:4])[0]
    row, slices = call(last_kernel, [((1, 128), F32), ((3, 64, 128), F32)], 6, us=1.0)(row, *fields)
    slices = returned(slices)
    row = row + jnp.roll(swapped(row), 32, 1)
    gram = lax.all_to_all(jnp.broadcast_to(row, (32, 128)), "sec", 0, 0, tiled=True)
    mine, other = call(finish_kernel, [((2, 32, 64), F32), ((2, 32, 64), F32)], 2)(gram, slices)
    other = swapped(other)
    first = jnp.where(core == 0, mine, other)
    last = jnp.where(core == 0, other, mine)
    out = jnp.concatenate([first, last], 2)[:, :, None, :]
    return (out[0], out[1])


def solution(mesh):
    in_specs = (
        P(("sec", "tile")),
        P(("sec", "tile")),
        P(("sec", "tile")),
        P(None, ("sec", "tile")),
        P(None, ("sec", "tile")),
        P(None, None, ("sec", "tile")),
        P(None, None, ("sec", "tile")),
        P(None, None, ("sec", "tile")),
        P("tile", "sec"),
    )
    out_specs = (P("tile", "sec", None), P("tile", "sec", None))
    return jax.shard_map(
        on_device, mesh=mesh, in_specs=in_specs, out_specs=out_specs, check_vma=False
    )
```

```python
import functools

import jax
import jax.numpy as jnp
from jax import lax
from jax.experimental import pallas as pl
from jax.experimental.pallas import tpu as pltpu
from jax.sharding import PartitionSpec as P

ITERS = 4
DAMPING = 0.5
SHIFT = 10.0
SCALE = 1.0 / 128.0
BACK = 25.0 / 16384.0
PAIRS = [(i, j) for i in range(5) for j in range(i, 5) if (i, j) != (4, 4)]
VMEM = pl.BlockSpec(memory_space=pltpu.VMEM)
F32 = jnp.float32
NT = (((1,), (1,)), ((), ()))


def split3(x):
    a = x.astype(jnp.bfloat16)
    rest = x - a.astype(F32)
    b = rest.astype(jnp.bfloat16)
    c = (rest - b.astype(F32)).astype(jnp.bfloat16)
    return jnp.concatenate([a, b, c], 0)


def merge3(x):
    n = x.shape[0] // 3
    return x[:n] + (x[n : 2 * n] + x[2 * n :])


def sublane_ids():
    return lax.broadcasted_iota(jnp.int32, (8, 128), 0)


def fold_rows(parts):
    sub = sublane_ids()
    low = sub < 4
    half = [
        jnp.where(low, parts[p], parts[p + 4])
        + pltpu.roll(jnp.where(low, parts[p + 4], parts[p]), 4, 0)
        for p in range(4)
    ]
    two = (sub & 2) != 0
    quarter = [
        jnp.where(two, half[p + 2] + pltpu.roll(half[p + 2], 2, 0), half[p] + pltpu.roll(half[p], 6, 0))
        for p in range(2)
    ]
    one = (sub & 1) != 0
    return jnp.where(
        one, quarter[1] + pltpu.roll(quarter[1], 1, 0), quarter[0] + pltpu.roll(quarter[0], 7, 0)
    )


def spread_rows(tops, sides):
    rows = []
    for q in range(8):
        parts = []
        for p in range(8):
            acc = tops[q][0] * sides[p][0]
            for group in range(1, 4):
                acc = acc + tops[q][group] * sides[p][group]
            parts.append(acc)
        rows.append(fold_rows(parts))
    return jnp.concatenate(rows, 0)


def sample_block(rows, wy_ref, fx_ref, col_ref, blk, side):
    out = []
    for group in range(4):
        ms = slice(8 * group, 8 * group + 8)
        col = col_ref[blk, side, ms, :]
        nxt = col + 1
        fx = fx_ref[blk, side, ms, :]
        acc = None
        for q in range(8):
            row = rows[8 * q : 8 * q + 8]
            left = jnp.take_along_axis(row, col, axis=0, mode="promise_in_bounds")
            right = jnp.take_along_axis(row, nxt, axis=0, mode="promise_in_bounds")
            term = wy_ref[blk, side, q, ms, :] * (left + fx * (right - left))
            acc = term if acc is None else acc + term
        out.append(acc)
    return out


def load_table(ref, blk, side):
    return [[ref[blk, side, p, 8 * g : 8 * g + 8, :] for g in range(4)] for p in range(8)]


def lanes_of(blk):
    return pl.ds(pl.multiple_of(blk * 128, 128), 128)


def pack_kernel(
    first_hbm, second_hbm, count_hbm, cell1_hbm, cell2_hbm, frac1_hbm, frac2_hbm, target_hbm, stiff_hbm,
    out_ref, ids_ref, stiff_ref, cell_ref, sem, *, sections
):
    copies = [
        pltpu.make_async_copy(cell1_hbm, cell_ref.at[0], sem.at[0]),
        pltpu.make_async_copy(cell2_hbm, cell_ref.at[1], sem.at[1]),
        pltpu.make_async_copy(first_hbm, ids_ref.at[0], sem.at[2]),
        pltpu.make_async_copy(second_hbm, ids_ref.at[1], sem.at[3]),
        pltpu.make_async_copy(count_hbm, ids_ref.at[2], sem.at[4]),
        pltpu.make_async_copy(stiff_hbm, stiff_ref, sem.at[5]),
    ]
    for k, src in enumerate((frac1_hbm, frac2_hbm, target_hbm)):
        for c in range(2):
            at = 64 + 64 * k + 32 * c
            copies.append(pltpu.make_async_copy(src.at[c], out_ref.at[at : at + 32, :], sem.at[6 + 2 * k + c]))
    for copy in copies:
        copy.start()
    for copy in copies:
        copy.wait()
    out_ref[0:32, :] = cell_ref[0].astype(F32)
    out_ref[32:64, :] = cell_ref[1].astype(F32)
    shift = sections.bit_length() - 1
    first = ids_ref[0] >> shift
    second = ids_ref[1] >> shift
    second = second + jnp.where((ids_ref[1] & (sections - 1)) == lax.axis_index("sec"), 0, 256)
    tile = lax.axis_index("tile")
    stiff = jnp.concatenate([stiff_ref[...], jnp.zeros((1, 96), F32)], 1)
    stiff = pltpu.roll(jnp.broadcast_to(stiff, (8, 128)), 32 * (tile & 3), 1)
    row = sublane_ids()
    tail = jnp.where((row >= 3) & (row - 3 == (tile >> 2)), stiff, 0.0)
    for k, x in enumerate((first, second, ids_ref[2])):
        tail = jnp.where(row == k, jnp.broadcast_to(x.astype(F32), (8, 128)), tail)
    out_ref[256:264, :] = tail


def tables_kernel(*refs, blocks, add):
    datas = refs[:blocks]
    refs = refs[blocks:]
    if add:
        before_own, before_down, before_stiff = refs[:3]
        refs = refs[3:]
    wx_ref, wy_ref, fx_ref, col_ref, live_ref, ohf_ref, ohs_ref, own_ref, down_ref, stiff_ref = refs
    comp = lax.axis_index("tile") & 1
    columns = [[], []]
    for blk, data_ref in enumerate(datas):
        lanes = slice(128 * blk, 128 * blk + 128)
        count = data_ref[258, :][None, :]
        goal = []
        for group in range(4):
            ms = slice(8 * group, 8 * group + 8)
            slot = (sublane_ids() + 8 * group).astype(F32)
            live = slot < count
            live_ref[blk, ms, :] = jnp.where(live, SCALE, 0.0)
            at = pl.multiple_of(192 + 32 * comp + 8 * group, 8)
            goal.append(jnp.where(live, data_ref[pl.ds(at, 8), :], 0.0))
        first = data_ref[256, :][None, :].astype(jnp.int32)
        second = data_ref[257, :][None, :].astype(jnp.int32)
        ids = lax.broadcasted_iota(jnp.int32, (256, 128), 0)
        ohf_ref[:, lanes] = jnp.where(ids == first, 1.0, 0.0).astype(jnp.bfloat16)
        ohs_ref[0:256, lanes] = jnp.where(ids == second, 1.0, 0.0).astype(jnp.bfloat16)
        ohs_ref[256:512, lanes] = jnp.where(ids + 256 == second, 1.0, 0.0).astype(jnp.bfloat16)
        for side in range(2):
            for group in range(4):
                ms = slice(8 * group, 8 * group + 8)
                at = 32 * side + 8 * group
                cell = data_ref[at : at + 8, :].astype(jnp.int32)
                base = 64 + 64 * side + 8 * group
                fx = data_ref[base : base + 8, :]
                fy = data_ref[base + 32 : base + 40, :]
                row = (cell * 37) >> 8
                col = cell - 7 * row
                fx_ref[blk, side, ms, :] = fx
                col_ref[blk, side, ms, :] = col
                for k in range(8):
                    wx_ref[blk, side, k, ms, :] = jnp.where(
                        col == k, 1.0 - fx, jnp.where(col == k - 1, fx, 0.0)
                    )
                    wy_ref[blk, side, k, ms, :] = jnp.where(
                        row == k, 1.0 - fy, jnp.where(row == k - 1, fy, 0.0)
                    )
            tops = load_table(wy_ref, blk, side)
            tops = [[tops[q][g] * goal[g] for g in range(4)] for q in range(8)]
            columns[side].append(spread_rows(tops, load_table(wx_ref, blk, side)))
    spreads = [jnp.concatenate(c, 1) for c in columns]
    at_first = merge3(lax.dot_general(split3(spreads[0]), ohf_ref[...], NT, preferred_element_type=F32))
    at_second = merge3(lax.dot_general(split3(spreads[1]), ohs_ref[...], NT, preferred_element_type=F32))
    own = at_first - at_second[:, :256]
    down = at_second[:, 256:]
    stiff = jnp.concatenate(
        [sum(data_ref[row : row + 1, :] for data_ref in datas) for row in (259, 260)], 1
    )
    if add:
        own = own + before_own[...]
        down = down + before_down[...]
        stiff = stiff + before_stiff[...]
    own_ref[...] = own
    down_ref[...] = down
    stiff_ref[...] = stiff


def stencil_kernel(down_ref, wx1, wy1, live1, ohs1, wx2, wy2, live2, ohs2, send_ref, keep_ref):
    step = lax.axis_index("tile") & 1
    send_ref[0] = down_ref[...]
    zero = [jnp.zeros((8, 128), F32)] * 4
    columns = [[], []]
    for wx_ref, wy_ref, live_ref in ((wx1, wy1, live1), (wx2, wy2, live2)):
        for blk in range(4):
            live = [live_ref[blk, 8 * g : 8 * g + 8, :] for g in range(4)]
            wy = load_table(wy_ref, blk, 1) + [zero]
            tops = [
                [wy[q][g] * jnp.where(step == 0, wy[q][g], wy[q + 1][g]) * live[g] for g in range(4)]
                for q in range(8)
            ]
            wx = load_table(wx_ref, blk, 1) + [zero]
            for kind in range(2):
                sides = [[wx[p][g] * wx[p + kind][g] for g in range(4)] for p in range(8)]
                columns[kind].append(spread_rows(tops, sides))
    for kind in range(2):
        both = scatter(jnp.concatenate(columns[kind], 1), ohs1[...], ohs2[...])
        keep_ref[kind] = both[:, :256]
        send_ref[kind + 1] = both[:, 256:]


def scatter(forces, hot1, hot2):
    parts = split3(forces)
    return merge3(
        lax.dot_general(parts[:, 0:512], hot1, NT, preferred_element_type=F32)
        + lax.dot_general(parts[:, 512:1024], hot2, NT, preferred_element_type=F32)
    )


def passed(parts, hot_in, hot_out, tables, side_in, side_out, scale):
    terms = []
    for h in range(2):
        wx_ref, wy_ref, fx_ref, col_ref = tables[h][2:6]
        columns = []
        for pair in range(2):
            at = slice(256 * pair, 256 * pair + 256)
            rows = merge3(jnp.dot(parts, hot_in[h][:, at], preferred_element_type=F32))
            for sub in range(2):
                blk = 2 * pair + sub
                got = sample_block(rows[:, 128 * sub : 128 * sub + 128], wy_ref, fx_ref, col_ref, blk, side_in)
                gap = scale(h, blk, got)
                tops = load_table(wy_ref, blk, side_out)
                tops = [[tops[q][g] * gap[g] for g in range(4)] for q in range(8)]
                columns.append(spread_rows(tops, load_table(wx_ref, blk, side_out)))
        terms.append(jnp.concatenate(columns, 1))
    return scatter(jnp.concatenate(terms, 1), hot_out[0][...], hot_out[1][...])


def up_kernel(v_ref, *refs):
    tables = (refs[:7], refs[7:14])
    own_ref, down_ref, gap_ref = refs[14:]

    def scale(h, blk, got):
        gap = []
        for g in range(4):
            ms = slice(8 * g, 8 * g + 8)
            gap.append(got[g] * tables[h][6][blk, ms, :])
            gap_ref[blk + 4 * h, ms, :] = gap[g]
        return gap

    forces = passed(split3(v_ref[...]), [t[0] for t in tables], [t[1] for t in tables], tables, 0, 1, scale)
    own_ref[...] = forces[:, :256]
    down_ref[...] = forces[:, 256:]


def down_kernel(
    v_ref, raw_ref, sent_ref, prev_ref, part_ref, gap_ref, mine_ref, other_ref, stiff_ref, *refs, back
):
    tables = (refs[:7], refs[7:14])
    (out_ref,) = refs[14:]
    v = v_ref[...]
    parts = jnp.concatenate([split3(v), split3(raw_ref[...] - sent_ref[...])], 1)

    def scale(h, blk, got):
        return [
            gap_ref[blk + 4 * h, 8 * g : 8 * g + 8, :] - got[g] * tables[h][6][blk, 8 * g : 8 * g + 8, :]
            for g in range(4)
        ]

    forces = passed(parts, [t[1] for t in tables], [t[0] for t in tables], tables, 1, 0, scale)
    up = lambda x, d: pltpu.roll(x, 64 - d, 0)
    dn = lambda x, d: pltpu.roll(x, d, 0)
    node = lax.broadcasted_iota(jnp.int32, (64, 256), 0)
    right = jnp.where((node & 7) < 7, up(v, 1) - v, 0.0)
    below = jnp.where(node < 56, up(v, 8) - v, 0.0)
    bend = (dn(right, 1) - right) + (dn(below, 8) - below)
    total = forces - part_ref[...] + (stiff_ref[...] * SCALE) * bend + ((DAMPING - SHIFT) * SCALE) * v
    first = (lax.axis_index("tile") & 1) == 0
    band = [jnp.where(first, mine_ref[k], other_ref[k]) for k in range(2)]
    band += [jnp.where(first, other_ref[k], mine_ref[k]) for k in range(2)]
    total = total + band[0] * v
    total = total + band[1] * up(v, 1) + dn(band[1] * v, 1)
    total = total + band[2] * up(v, 8) + dn(band[2] * v, 8)
    total = total + band[3] * up(v, 9) + dn(band[3] * v, 9)
    total = total + dn(band[3] * up(v, 8), 1) + dn(band[3] * up(v, 1), 8)
    if back:
        total = total - BACK * prev_ref[...]
    out_ref[...] = total


def two_sum(a, b):
    s = a + b
    t = s - a
    return s, (a - (s - t)) + (b - t)


def halves(a):
    c = 4097.0 * a
    high = c - (c - a)
    return high, a - high


def two_prod(a, b):
    p = a * b
    ah, al = halves(a)
    bh, bl = halves(b)
    return p, ((ah * bh - p) + ah * bl + al * bh) + al * bl


def quick(a, b):
    s = a + b
    return s, b - (s - a)


def dd_add(x, y):
    s, e = two_sum(x[0], y[0])
    return quick(s, e + (x[1] + y[1]))


def dd_mul(x, y):
    p, e = two_prod(x[0], y[0])
    return quick(p, e + (x[0] * y[1] + x[1] * y[0]))


def dd_neg(x):
    return (-x[0], -x[1])


def dd_div(x, y):
    q = x[0] / y[0]
    rest = dd_add(x, dd_neg(dd_mul(y, (q, jnp.zeros_like(q)))))
    return quick(q, rest[0] / y[0])


def dots(fields, pairs):
    sub = lax.broadcasted_iota(jnp.int32, (16, 128), 0)
    lane = lax.broadcasted_iota(jnp.int32, (16, 128), 1)
    high = jnp.zeros((16, 128), F32)
    low = jnp.zeros((16, 128), F32)
    for i, j in pairs:
        acc = two_prod(fields[i], fields[j])
        acc = dd_add((acc[0][:, :128], acc[1][:, :128]), (acc[0][:, 128:], acc[1][:, 128:]))
        n = 64
        while n > 8:
            n //= 2
            acc = dd_add((acc[0][:n], acc[1][:n]), (acc[0][n:], acc[1][n:]))
        for d in (4, 2, 1):
            acc = dd_add(acc, (pltpu.roll(acc[0], d, 0), pltpu.roll(acc[1], d, 0)))
        wide = [jnp.concatenate([a, a], 0) for a in acc]
        here = sub == PAIRS.index((i, j))
        high = jnp.where(here, wide[0], high)
        low = jnp.where(here, wide[1], low)
    acc = (high, low)
    for d in (64, 32, 16, 8, 4, 2, 1):
        acc = dd_add(acc, (pltpu.roll(acc[0], d, 1), pltpu.roll(acc[1], d, 1)))
    row = jnp.where(lane == sub, acc[0], 0.0) + jnp.where(lane == sub + 16, acc[1], 0.0)
    return jnp.sum(row, 0, keepdims=True)


def dots_kernel(v0, v1, v2, v3, out_ref):
    out_ref[...] = dots([r[...] for r in (v0, v1, v2, v3)], [p for p in PAIRS if p[1] < 4])


def last_kernel(row_ref, v0, v1, v2, v3, v4, out_ref, slice_ref):
    fields = [r[...] for r in (v0, v1, v2, v3, v4)]
    y = lax.axis_index("tile") >> 1
    for k in range(3):
        sides = []
        for m in (2 * k, 2 * k + 1):
            if m < 5:
                x = jnp.where(y >= 2, fields[m][:, 128:], fields[m][:, :128])
                sides.append((x, pltpu.roll(x, 64, 1)))
            else:
                sides.append((jnp.zeros((64, 128), F32),) * 2)
        left = jnp.where((y & 1) == 0, sides[0][0], sides[0][1])
        right = jnp.where((y & 1) == 0, sides[1][1], sides[1][0])
        lane = lax.broadcasted_iota(jnp.int32, (64, 128), 1)
        slice_ref[k] = jnp.where(lane < 64, left, right)
    out_ref[...] = row_ref[...] + dots(fields, [p for p in PAIRS if p[1] == 4])


def finish_kernel(gram_ref, slice_ref, mine_ref, other_ref):
    rows = gram_ref[...]
    acc = dd_add((rows, pltpu.roll(rows, 112, 1)), (pltpu.roll(rows, 96, 1), pltpu.roll(rows, 80, 1)))
    n = 32
    while n > 8:
        n //= 2
        acc = dd_add((acc[0][:n], acc[1][:n]), (acc[0][n:], acc[1][n:]))
    for d in (4, 2, 1):
        acc = dd_add(acc, (pltpu.roll(acc[0], d, 0), pltpu.roll(acc[1], d, 0)))
    gram = {}
    for k, (i, j) in enumerate(PAIRS):
        pair = tuple(jnp.broadcast_to(a[:, k : k + 1], (8, 128)) for a in acc)
        gram[(i, j)] = pair
        gram[(j, i)] = pair
    zero = jnp.zeros((8, 128), F32)
    const = lambda c: (jnp.full((8, 128), c, F32), zero)

    def tree(terms):
        while len(terms) > 1:
            terms = [dd_add(*terms[k : k + 2]) if k + 1 < len(terms) else terms[k] for k in range(0, len(terms), 2)]
        return terms[0]

    def form(a, b):
        return tree([dd_mul(bj, tree([dd_mul(ai, gram[(i, j)]) for i, ai in enumerate(a)])) for j, bj in enumerate(b)])

    def apply(p):
        out = [const(0.0) for _ in range(len(p) + 1)]
        for k, c in enumerate(p):
            out[k + 1] = dd_add(out[k + 1], (c[0] * 128.0, c[1] * 128.0))
            out[k] = dd_add(out[k], dd_mul(c, const(SHIFT)))
            if k >= 1:
                out[k - 1] = dd_add(out[k - 1], dd_mul(c, const(BACK * 128.0)))
        return out

    def axpy(a, x, y):
        out = []
        for k in range(max(len(x), len(y))):
            if k >= len(x):
                out.append(y[k])
            elif k >= len(y):
                out.append(dd_mul(a, x[k]))
            else:
                out.append(dd_add(y[k], dd_mul(a, x[k])))
        return out

    res = [const(1.0)]
    direc = [const(1.0)]
    sol = []
    norm = gram[(0, 0)]
    for it in range(ITERS):
        image = apply(direc)
        step = dd_div(norm, form(direc, image))
        sol = axpy(step, direc, sol)
        res = axpy(dd_neg(step), image, res)
        if it < ITERS - 1:
            new = form(res, res)
            direc = axpy(dd_div(new, norm), direc, res)
            norm = new
    lane = lax.broadcasted_iota(jnp.int32, (64, 128), 1)

    def combine(coefs):
        total = jnp.zeros((64, 128), F32)
        flat = [c[0][0:1, 0:1] for c in coefs] + [jnp.zeros((1, 1), F32)] * (6 - len(coefs))
        for k in range(3):
            total = total + jnp.where(lane < 64, flat[2 * k], flat[2 * k + 1]) * slice_ref[k]
        return total + pltpu.roll(total, 64, 1)

    core = lax.axis_index("tile") & 1
    want = lax.broadcasted_iota(jnp.int32, (64, 128), 0)
    want = jnp.where(want < 32, want + 32 * core, want - 32 * core)
    pick = jnp.where(lane == want, 1.0, 0.0).astype(jnp.bfloat16)
    for k, coefs in enumerate((sol, res)):
        parts = lax.dot_general(pick, split3(combine(coefs)), NT, preferred_element_type=F32)
        both = parts[:, :64] + (parts[:, 64:128] + parts[:, 128:192])
        mine_ref[k] = both[:32]
        other_ref[k] = both[32:]


def call(kernel, outs, n_in, scratch=(), us=2.0, hbm=0, grant=8):
    return pl.pallas_call(
        kernel,
        out_shape=[jax.ShapeDtypeStruct(s, d) for s, d in outs],
        in_specs=[VMEM] * (n_in - hbm)
        + [pl.BlockSpec(memory_space=pl.ANY)] * hbm,
        out_specs=[VMEM] * len(outs),
        scratch_shapes=list(scratch),
        compiler_params=pltpu.CompilerParams(vmem_limit_bytes=grant * 1024 * 1024),
        cost_estimate=pl.CostEstimate(flops=int(us * 1e9), bytes_accessed=1 << 18, transcendentals=0),
    )


ROW = 4
CHIPS = 4


def seat(section, y, sections):
    row, col = divmod(section, ROW)
    col = col if row % 2 == 0 else ROW - 1 - col
    row = row if y % 2 == 0 else sections // ROW - 1 - row
    return row * ROW + col


def shifted(block, distance):
    sections = lax.axis_size("sec")
    route = []
    for section in range(sections):
        there = (section + distance) % sections
        crosses = (section < sections // 2) != (there < sections // 2)
        for y in range(CHIPS):
            to = y ^ 1 if crosses else y
            for core in range(2):
                route.append(
                    (seat(section, y, sections) * 8 + 2 * y + core, seat(there, to, sections) * 8 + 2 * to + core)
                )
    return lax.ppermute(block, ("sec", "tile"), route)


def swapped(block):
    return lax.ppermute(block, "tile", [(i, i ^ 1) for i in range(8)])


def dealt(block, step):
    sections = lax.axis_size("sec")
    route = []
    for section in range(sections):
        for y in range(CHIPS):
            to = (y + step) % CHIPS
            for core in range(2):
                route.append((section * 8 + 2 * y + core, seat(section, to, sections) * 8 + 2 * to + core))
    return lax.ppermute(block, ("sec", "tile"), route)


def returned(block):
    sections = lax.axis_size("sec")
    route = []
    for section in range(sections):
        for tile in range(2 * CHIPS):
            route.append((seat(section, tile // 2, sections) * 8 + tile, section * 8 + tile))
    return lax.ppermute(block, ("sec", "tile"), route)


def on_device(
    ov_first, ov_second, match_count, cell_first, cell_second, frac_first, frac_second, target, stiffness
):
    tile = lax.axis_index("tile")
    core = tile % 2
    sections = lax.axis_size("sec")
    dma = pltpu.SemaphoreType.DMA
    packed = call(
        functools.partial(pack_kernel, sections=sections),
        [((264, 128), F32)],
        9,
        [
            pltpu.VMEM((3, 1, 128), jnp.int32),
            pltpu.VMEM((1, 32), F32),
            pltpu.VMEM((2, 32, 128), jnp.int32),
            dma((12,)),
        ],
        hbm=9,
        grant=60,
    )(
        ov_first.reshape(1, 128),
        ov_second.reshape(1, 128),
        match_count.reshape(1, 128),
        cell_first,
        cell_second,
        frac_first,
        frac_second,
        target,
        stiffness.reshape(1, 32),
    )[0]
    same = [dealt(packed, step) for step in (2, 1, 3, 0)]
    other = swapped(jnp.stack(same))

    field = ((64, 256), F32)
    bf16 = jnp.bfloat16
    half_tables = [
        ((4, 2, 8, 32, 128), F32),
        ((4, 2, 8, 32, 128), F32),
        ((4, 2, 32, 128), F32),
        ((4, 2, 32, 128), jnp.int32),
        ((4, 32, 128), F32),
        ((256, 512), bf16),
        ((512, 512), bf16),
        field,
        field,
        ((1, 256), F32),
    ]
    one = call(functools.partial(tables_kernel, blocks=4, add=False), half_tables, 4)(*same)
    two = call(functools.partial(tables_kernel, blocks=4, add=True), half_tables, 7)(
        other[0], other[1], other[2], other[3], *one[7:]
    )
    own, down, stiff = two[7:]
    send, keep = call(
        stencil_kernel, [((3, 64, 256), F32), ((2, 64, 256), F32)], 9, us=4.0
    )(down, one[0], one[1], one[4], one[6], two[0], two[1], two[4], two[6])
    above = shifted(send, -1)
    raw = shifted(own, 1)
    fields = [own - above[0]]
    mine = keep + above[1:]
    other = swapped(mine)
    tables = []
    for wx, wy, fx, col, live, ohf, ohs in (one[:7], two[:7]):
        tables += [ohf, ohs, wx, wy, fx, col, live]
    for k in range(ITERS):
        v = fields[-1]
        sent = down
        part, down, gap = call(up_kernel, [field, field, ((8, 32, 128), F32)], 15)(v, *tables)
        above = shifted(down, -1)
        partial = call(functools.partial(down_kernel, back=k > 0), [field], 23)(
            v, raw, sent, fields[max(k - 1, 0)], part, gap, mine, other, stiff, *tables
        )[0]
        if k < ITERS - 1:
            raw = shifted(partial, 1)
        fields.append(partial - above)
    row = call(dots_kernel, [((1, 128), F32)], 4, us=1.0)(*fields[:4])[0]
    row, slices = call(last_kernel, [((1, 128), F32), ((3, 64, 128), F32)], 6, us=1.0)(row, *fields)
    slices = returned(slices)
    row = row + jnp.roll(swapped(row), 32, 1)
    gram = lax.all_to_all(jnp.broadcast_to(row, (32, 128)), "sec", 0, 0, tiled=True)
    mine, other = call(finish_kernel, [((2, 32, 64), F32), ((2, 32, 64), F32)], 2)(gram, slices)
    other = swapped(other)
    first = jnp.where(core == 0, mine, other)
    last = jnp.where(core == 0, other, mine)
    out = jnp.concatenate([first, last], 2)[:, :, None, :]
    return (out[0], out[1])


def solution(mesh):
    in_specs = (
        P(("sec", "tile")),
        P(("sec", "tile")),
        P(("sec", "tile")),
        P(None, ("sec", "tile")),
        P(None, ("sec", "tile")),
        P(None, None, ("sec", "tile")),
        P(None, None, ("sec", "tile")),
        P(None, None, ("sec", "tile")),
        P("tile", "sec"),
    )
    out_specs = (P("tile", "sec", None), P("tile", "sec", None))
    return jax.shard_map(
        on_device, mesh=mesh, in_specs=in_specs, out_specs=out_specs, check_vma=False
    )
```

```python
import functools

import jax
import jax.numpy as jnp
from jax import lax
from jax.experimental import pallas as pl
from jax.experimental.pallas import tpu as pltpu
from jax.sharding import PartitionSpec as P

ITERS = 4
DAMPING = 0.5
SHIFT = 10.0
SCALE = 1.0 / 128.0
BACK = 25.0 / 16384.0
PAIRS = [(i, j) for i in range(5) for j in range(i, 5) if (i, j) != (4, 4)]
VMEM = pl.BlockSpec(memory_space=pltpu.VMEM)
F32 = jnp.float32
NT = (((1,), (1,)), ((), ()))


def split3(x):
    a = x.astype(jnp.bfloat16)
    rest = x - a.astype(F32)
    b = rest.astype(jnp.bfloat16)
    c = (rest - b.astype(F32)).astype(jnp.bfloat16)
    return jnp.concatenate([a, b, c], 0)


def merge3(x):
    n = x.shape[0] // 3
    return x[:n] + (x[n : 2 * n] + x[2 * n :])


def sublane_ids():
    return lax.broadcasted_iota(jnp.int32, (8, 128), 0)


def fold_rows(parts):
    sub = sublane_ids()
    low = sub < 4
    half = [
        jnp.where(low, parts[p], parts[p + 4])
        + pltpu.roll(jnp.where(low, parts[p + 4], parts[p]), 4, 0)
        for p in range(4)
    ]
    two = (sub & 2) != 0
    quarter = [
        jnp.where(two, half[p + 2] + pltpu.roll(half[p + 2], 2, 0), half[p] + pltpu.roll(half[p], 6, 0))
        for p in range(2)
    ]
    one = (sub & 1) != 0
    return jnp.where(
        one, quarter[1] + pltpu.roll(quarter[1], 1, 0), quarter[0] + pltpu.roll(quarter[0], 7, 0)
    )


def spread_rows(tops, sides):
    rows = []
    for q in range(8):
        parts = []
        for p in range(8):
            acc = tops[q][0] * sides[p][0]
            for group in range(1, 4):
                acc = acc + tops[q][group] * sides[p][group]
            parts.append(acc)
        rows.append(fold_rows(parts))
    return jnp.concatenate(rows, 0)


def sample_block(rows, wy_ref, fx_ref, col_ref, blk, side):
    out = []
    for group in range(4):
        ms = slice(8 * group, 8 * group + 8)
        col = col_ref[blk, side, ms, :]
        nxt = col + 1
        fx = fx_ref[blk, side, ms, :]
        acc = None
        for q in range(8):
            row = rows[8 * q : 8 * q + 8]
            left = jnp.take_along_axis(row, col, axis=0, mode="promise_in_bounds")
            right = jnp.take_along_axis(row, nxt, axis=0, mode="promise_in_bounds")
            term = wy_ref[blk, side, q, ms, :] * (left + fx * (right - left))
            acc = term if acc is None else acc + term
        out.append(acc)
    return out


def load_table(ref, blk, side):
    return [[ref[blk, side, p, 8 * g : 8 * g + 8, :] for g in range(4)] for p in range(8)]


def lanes_of(blk):
    return pl.ds(pl.multiple_of(blk * 128, 128), 128)


def pack_kernel(
    first_hbm, second_hbm, count_hbm, cell1_hbm, cell2_hbm, frac1_hbm, frac2_hbm, target_hbm, stiff_hbm,
    out_ref, ids_ref, stiff_ref, cell_ref, sem, *, sections
):
    copies = [
        pltpu.make_async_copy(cell1_hbm, cell_ref.at[0], sem.at[0]),
        pltpu.make_async_copy(cell2_hbm, cell_ref.at[1], sem.at[1]),
        pltpu.make_async_copy(first_hbm, ids_ref.at[0], sem.at[2]),
        pltpu.make_async_copy(second_hbm, ids_ref.at[1], sem.at[3]),
        pltpu.make_async_copy(count_hbm, ids_ref.at[2], sem.at[4]),
        pltpu.make_async_copy(stiff_hbm, stiff_ref, sem.at[5]),
    ]
    for k, src in enumerate((frac1_hbm, frac2_hbm, target_hbm)):
        for c in range(2):
            at = 64 + 64 * k + 32 * c
            copies.append(pltpu.make_async_copy(src.at[c], out_ref.at[at : at + 32, :], sem.at[6 + 2 * k + c]))
    for copy in copies:
        copy.start()
    for copy in copies:
        copy.wait()
    out_ref[0:32, :] = cell_ref[0].astype(F32)
    out_ref[32:64, :] = cell_ref[1].astype(F32)
    shift = sections.bit_length() - 1
    first = ids_ref[0] >> shift
    second = ids_ref[1] >> shift
    second = second + jnp.where((ids_ref[1] & (sections - 1)) == lax.axis_index("sec"), 0, 256)
    tile = lax.axis_index("tile")
    stiff = jnp.concatenate([stiff_ref[...], jnp.zeros((1, 96), F32)], 1)
    stiff = pltpu.roll(jnp.broadcast_to(stiff, (8, 128)), 32 * (tile & 3), 1)
    row = sublane_ids()
    tail = jnp.where((row >= 3) & (row - 3 == (tile >> 2)), stiff, 0.0)
    for k, x in enumerate((first, second, ids_ref[2])):
        tail = jnp.where(row == k, jnp.broadcast_to(x.astype(F32), (8, 128)), tail)
    out_ref[256:264, :] = tail


def tables_kernel(*refs, blocks, add):
    datas = refs[:blocks]
    refs = refs[blocks:]
    if add:
        before_own, before_down, before_stiff = refs[:3]
        refs = refs[3:]
    wx_ref, wy_ref, fx_ref, col_ref, live_ref, ohf_ref, ohs_ref, own_ref, down_ref, stiff_ref = refs
    comp = lax.axis_index("tile") & 1
    columns = [[], []]
    for blk, data_ref in enumerate(datas):
        lanes = slice(128 * blk, 128 * blk + 128)
        count = data_ref[258, :][None, :]
        goal = []
        for group in range(4):
            ms = slice(8 * group, 8 * group + 8)
            slot = (sublane_ids() + 8 * group).astype(F32)
            live = slot < count
            live_ref[blk, ms, :] = jnp.where(live, SCALE, 0.0)
            at = pl.multiple_of(192 + 32 * comp + 8 * group, 8)
            goal.append(jnp.where(live, data_ref[pl.ds(at, 8), :], 0.0))
        first = data_ref[256, :][None, :].astype(jnp.int32)
        second = data_ref[257, :][None, :].astype(jnp.int32)
        ids = lax.broadcasted_iota(jnp.int32, (256, 128), 0)
        ohf_ref[:, lanes] = jnp.where(ids == first, 1.0, 0.0).astype(jnp.bfloat16)
        ohs_ref[0:256, lanes] = jnp.where(ids == second, 1.0, 0.0).astype(jnp.bfloat16)
        ohs_ref[256:512, lanes] = jnp.where(ids + 256 == second, 1.0, 0.0).astype(jnp.bfloat16)
        for side in range(2):
            for group in range(4):
                ms = slice(8 * group, 8 * group + 8)
                at = 32 * side + 8 * group
                cell = data_ref[at : at + 8, :].astype(jnp.int32)
                base = 64 + 64 * side + 8 * group
                fx = data_ref[base : base + 8, :]
                fy = data_ref[base + 32 : base + 40, :]
                row = (cell * 37) >> 8
                col = cell - 7 * row
                fx_ref[blk, side, ms, :] = fx
                col_ref[blk, side, ms, :] = col
                for k in range(8):
                    wx_ref[blk, side, k, ms, :] = jnp.where(
                        col == k, 1.0 - fx, jnp.where(col == k - 1, fx, 0.0)
                    )
                    wy_ref[blk, side, k, ms, :] = jnp.where(
                        row == k, 1.0 - fy, jnp.where(row == k - 1, fy, 0.0)
                    )
            tops = load_table(wy_ref, blk, side)
            tops = [[tops[q][g] * goal[g] for g in range(4)] for q in range(8)]
            columns[side].append(spread_rows(tops, load_table(wx_ref, blk, side)))
    spreads = [jnp.concatenate(c, 1) for c in columns]
    at_first = merge3(lax.dot_general(split3(spreads[0]), ohf_ref[...], NT, preferred_element_type=F32))
    at_second = merge3(lax.dot_general(split3(spreads[1]), ohs_ref[...], NT, preferred_element_type=F32))
    own = at_first - at_second[:, :256]
    down = at_second[:, 256:]
    stiff = jnp.concatenate(
        [sum(data_ref[row : row + 1, :] for data_ref in datas) for row in (259, 260)], 1
    )
    if add:
        own = own + before_own[...]
        down = down + before_down[...]
        stiff = stiff + before_stiff[...]
    own_ref[...] = own
    down_ref[...] = down
    stiff_ref[...] = stiff


def stencil_kernel(down_ref, *refs):
    step = lax.axis_index("tile") & 1
    send_ref, keep_ref = refs[12:]
    send_ref[0] = down_ref[...]
    zero = [jnp.zeros((8, 128), F32)] * 4
    terms = [[], []]
    for h, blocks in enumerate(BLOCKS):
        wx_ref, wy_ref, live_ref = refs[4 * h : 4 * h + 3]
        columns = [[], []]
        for blk in range(blocks):
            live = [live_ref[blk, 8 * g : 8 * g + 8, :] for g in range(4)]
            wy = load_table(wy_ref, blk, 1) + [zero]
            tops = [
                [wy[q][g] * jnp.where(step == 0, wy[q][g], wy[q + 1][g]) * live[g] for g in range(4)]
                for q in range(8)
            ]
            wx = load_table(wx_ref, blk, 1) + [zero]
            for kind in range(2):
                sides = [[wx[p][g] * wx[p + kind][g] for g in range(4)] for p in range(8)]
                columns[kind].append(spread_rows(tops, sides))
        for kind in range(2):
            terms[kind].append(split3(jnp.concatenate(columns[kind], 1)))
    for kind in range(2):
        both = scatter(terms[kind], refs[3:12:4])
        keep_ref[kind] = both[:, :256]
        send_ref[kind + 1] = both[:, 256:]


def scatter(terms, hots):
    total = None
    for parts, hot in zip(terms, hots):
        term = lax.dot_general(parts, hot[...], NT, preferred_element_type=F32)
        total = term if total is None else total + term
    return merge3(total)


BLOCKS = (2, 3, 3)
AT = (0, 2, 5)


def passed(parts, hot_in, hot_out, tables, side_in, side_out, scale):
    terms = []
    for h, blocks in enumerate(BLOCKS):
        wx_ref, wy_ref, fx_ref, col_ref = tables[h][2:6]
        columns = []
        for start in range(0, blocks, 2):
            stop = min(start + 2, blocks)
            rows = merge3(jnp.dot(parts, hot_in[h][:, 128 * start : 128 * stop], preferred_element_type=F32))
            for blk in range(start, stop):
                at = 128 * (blk - start)
                got = sample_block(rows[:, at : at + 128], wy_ref, fx_ref, col_ref, blk, side_in)
                gap = scale(h, blk, got)
                tops = load_table(wy_ref, blk, side_out)
                tops = [[tops[q][g] * gap[g] for g in range(4)] for q in range(8)]
                columns.append(spread_rows(tops, load_table(wx_ref, blk, side_out)))
        terms.append(split3(jnp.concatenate(columns, 1)))
    return scatter(terms, hot_out)


def up_kernel(v_ref, *refs):
    tables = (refs[:7], refs[7:14], refs[14:21])
    own_ref, down_ref, gap_ref = refs[21:]

    def scale(h, blk, got):
        gap = []
        for g in range(4):
            ms = slice(8 * g, 8 * g + 8)
            gap.append(got[g] * tables[h][6][blk, ms, :])
            gap_ref[blk + AT[h], ms, :] = gap[g]
        return gap

    forces = passed(split3(v_ref[...]), [t[0] for t in tables], [t[1] for t in tables], tables, 0, 1, scale)
    own_ref[...] = forces[:, :256]
    down_ref[...] = forces[:, 256:]


def down_kernel(
    v_ref, raw_ref, sent_ref, prev_ref, part_ref, gap_ref, mine_ref, other_ref, stiff_ref, *refs, back
):
    tables = (refs[:7], refs[7:14], refs[14:21])
    (out_ref,) = refs[21:]
    v = v_ref[...]
    parts = jnp.concatenate([split3(v), split3(raw_ref[...] - sent_ref[...])], 1)

    def scale(h, blk, got):
        return [
            gap_ref[blk + AT[h], 8 * g : 8 * g + 8, :] - got[g] * tables[h][6][blk, 8 * g : 8 * g + 8, :]
            for g in range(4)
        ]

    forces = passed(parts, [t[1] for t in tables], [t[0] for t in tables], tables, 1, 0, scale)
    up = lambda x, d: pltpu.roll(x, 64 - d, 0)
    dn = lambda x, d: pltpu.roll(x, d, 0)
    node = lax.broadcasted_iota(jnp.int32, (64, 256), 0)
    right = jnp.where((node & 7) < 7, up(v, 1) - v, 0.0)
    below = jnp.where(node < 56, up(v, 8) - v, 0.0)
    bend = (dn(right, 1) - right) + (dn(below, 8) - below)
    total = forces - part_ref[...] + (stiff_ref[...] * SCALE) * bend + ((DAMPING - SHIFT) * SCALE) * v
    first = (lax.axis_index("tile") & 1) == 0
    band = [jnp.where(first, mine_ref[k], other_ref[k]) for k in range(2)]
    band += [jnp.where(first, other_ref[k], mine_ref[k]) for k in range(2)]
    total = total + band[0] * v
    total = total + band[1] * up(v, 1) + dn(band[1] * v, 1)
    total = total + band[2] * up(v, 8) + dn(band[2] * v, 8)
    total = total + band[3] * up(v, 9) + dn(band[3] * v, 9)
    total = total + dn(band[3] * up(v, 8), 1) + dn(band[3] * up(v, 1), 8)
    if back:
        total = total - BACK * prev_ref[...]
    out_ref[...] = total


def two_sum(a, b):
    s = a + b
    t = s - a
    return s, (a - (s - t)) + (b - t)


def halves(a):
    c = 4097.0 * a
    high = c - (c - a)
    return high, a - high


def two_prod(a, b):
    p = a * b
    ah, al = halves(a)
    bh, bl = halves(b)
    return p, ((ah * bh - p) + ah * bl + al * bh) + al * bl


def quick(a, b):
    s = a + b
    return s, b - (s - a)


def dd_add(x, y):
    s, e = two_sum(x[0], y[0])
    return quick(s, e + (x[1] + y[1]))


def dd_mul(x, y):
    p, e = two_prod(x[0], y[0])
    return quick(p, e + (x[0] * y[1] + x[1] * y[0]))


def dd_neg(x):
    return (-x[0], -x[1])


def dd_div(x, y):
    q = x[0] / y[0]
    rest = dd_add(x, dd_neg(dd_mul(y, (q, jnp.zeros_like(q)))))
    return quick(q, rest[0] / y[0])


def dots(fields, pairs):
    sub = lax.broadcasted_iota(jnp.int32, (16, 128), 0)
    lane = lax.broadcasted_iota(jnp.int32, (16, 128), 1)
    high = jnp.zeros((16, 128), F32)
    low = jnp.zeros((16, 128), F32)
    for i, j in pairs:
        acc = two_prod(fields[i], fields[j])
        acc = dd_add((acc[0][:, :128], acc[1][:, :128]), (acc[0][:, 128:], acc[1][:, 128:]))
        n = 64
        while n > 8:
            n //= 2
            acc = dd_add((acc[0][:n], acc[1][:n]), (acc[0][n:], acc[1][n:]))
        for d in (4, 2, 1):
            acc = dd_add(acc, (pltpu.roll(acc[0], d, 0), pltpu.roll(acc[1], d, 0)))
        wide = [jnp.concatenate([a, a], 0) for a in acc]
        here = sub == PAIRS.index((i, j))
        high = jnp.where(here, wide[0], high)
        low = jnp.where(here, wide[1], low)
    acc = (high, low)
    for d in (64, 32, 16, 8, 4, 2, 1):
        acc = dd_add(acc, (pltpu.roll(acc[0], d, 1), pltpu.roll(acc[1], d, 1)))
    row = jnp.where(lane == sub, acc[0], 0.0) + jnp.where(lane == sub + 16, acc[1], 0.0)
    return jnp.sum(row, 0, keepdims=True)


def dots_kernel(v0, v1, v2, v3, out_ref):
    out_ref[...] = dots([r[...] for r in (v0, v1, v2, v3)], [p for p in PAIRS if p[1] < 4])


def last_kernel(row_ref, v0, v1, v2, v3, v4, out_ref):
    fields = [r[...] for r in (v0, v1, v2, v3, v4)]
    out_ref[...] = row_ref[...] + dots(fields, [p for p in PAIRS if p[1] == 4])


def finish_kernel(gram_ref, v0, v1, v2, v3, v4, mine_ref, other_ref):
    rows = gram_ref[...]
    acc = dd_add((rows, pltpu.roll(rows, 112, 1)), (pltpu.roll(rows, 96, 1), pltpu.roll(rows, 80, 1)))
    n = 32
    while n > 8:
        n //= 2
        acc = dd_add((acc[0][:n], acc[1][:n]), (acc[0][n:], acc[1][n:]))
    for d in (4, 2, 1):
        acc = dd_add(acc, (pltpu.roll(acc[0], d, 0), pltpu.roll(acc[1], d, 0)))
    gram = {}
    for k, (i, j) in enumerate(PAIRS):
        pair = tuple(jnp.broadcast_to(a[:, k : k + 1], (8, 128)) for a in acc)
        gram[(i, j)] = pair
        gram[(j, i)] = pair
    zero = jnp.zeros((8, 128), F32)
    const = lambda c: (jnp.full((8, 128), c, F32), zero)

    def tree(terms):
        while len(terms) > 1:
            terms = [dd_add(*terms[k : k + 2]) if k + 1 < len(terms) else terms[k] for k in range(0, len(terms), 2)]
        return terms[0]

    def form(a, b):
        return tree([dd_mul(bj, tree([dd_mul(ai, gram[(i, j)]) for i, ai in enumerate(a)])) for j, bj in enumerate(b)])

    def apply(p):
        out = [const(0.0) for _ in range(len(p) + 1)]
        for k, c in enumerate(p):
            out[k + 1] = dd_add(out[k + 1], (c[0] * 128.0, c[1] * 128.0))
            out[k] = dd_add(out[k], dd_mul(c, const(SHIFT)))
            if k >= 1:
                out[k - 1] = dd_add(out[k - 1], dd_mul(c, const(BACK * 128.0)))
        return out

    def axpy(a, x, y):
        out = []
        for k in range(max(len(x), len(y))):
            if k >= len(x):
                out.append(y[k])
            elif k >= len(y):
                out.append(dd_mul(a, x[k]))
            else:
                out.append(dd_add(y[k], dd_mul(a, x[k])))
        return out

    res = [const(1.0)]
    direc = [const(1.0)]
    sol = []
    norm = gram[(0, 0)]
    for it in range(ITERS):
        image = apply(direc)
        step = dd_div(norm, form(direc, image))
        sol = axpy(step, direc, sol)
        res = axpy(dd_neg(step), image, res)
        if it < ITERS - 1:
            new = form(res, res)
            direc = axpy(dd_div(new, norm), direc, res)
            norm = new
    fields = [r[...] for r in (v0, v1, v2, v3, v4)]

    def combine(coefs):
        total = None
        for c, f in zip(coefs, fields):
            term = c[0][0:1, 0:1] * f
            total = term if total is None else total + term
        return total

    tile = lax.axis_index("tile")
    ids = lax.broadcasted_iota(jnp.int32, (64, 256), 1)
    want = lax.broadcasted_iota(jnp.int32, (64, 256), 0)
    want = jnp.where(want < 32, tile * 32 + want, (tile ^ 1) * 32 + want - 32)
    pick = jnp.where(ids == want, 1.0, 0.0).astype(jnp.bfloat16)
    for k, coefs in enumerate((sol, res)):
        parts = lax.dot_general(pick, split3(combine(coefs)), NT, preferred_element_type=F32)
        both = parts[:, :64] + (parts[:, 64:128] + parts[:, 128:192])
        mine_ref[k] = both[:32]
        other_ref[k] = both[32:]


def call(kernel, outs, n_in, scratch=(), us=2.0, hbm=0, grant=8):
    return pl.pallas_call(
        kernel,
        out_shape=[jax.ShapeDtypeStruct(s, d) for s, d in outs],
        in_specs=[VMEM] * (n_in - hbm)
        + [pl.BlockSpec(memory_space=pl.ANY)] * hbm,
        out_specs=[VMEM] * len(outs),
        scratch_shapes=list(scratch),
        compiler_params=pltpu.CompilerParams(vmem_limit_bytes=grant * 1024 * 1024),
        cost_estimate=pl.CostEstimate(flops=int(us * 1e9), bytes_accessed=1 << 18, transcendentals=0),
    )


def shifted(block, distance):
    sections = lax.axis_size("sec")
    return lax.ppermute(block, "sec", [(i, (i + distance) % sections) for i in range(sections)])


def swapped(block):
    return lax.ppermute(block, "tile", [(i, i ^ 1) for i in range(8)])


def dealt(block, step):
    return lax.ppermute(block, "tile", [(i, (i + 2 * step) % 8) for i in range(8)])


def on_device(
    ov_first, ov_second, match_count, cell_first, cell_second, frac_first, frac_second, target, stiffness
):
    tile = lax.axis_index("tile")
    core = tile % 2
    sections = lax.axis_size("sec")
    dma = pltpu.SemaphoreType.DMA
    packed = call(
        functools.partial(pack_kernel, sections=sections),
        [((264, 128), F32)],
        9,
        [
            pltpu.VMEM((3, 1, 128), jnp.int32),
            pltpu.VMEM((1, 32), F32),
            pltpu.VMEM((2, 32, 128), jnp.int32),
            dma((12,)),
        ],
        hbm=9,
        grant=60,
    )(
        ov_first.reshape(1, 128),
        ov_second.reshape(1, 128),
        match_count.reshape(1, 128),
        cell_first,
        cell_second,
        frac_first,
        frac_second,
        target,
        stiffness.reshape(1, 32),
    )[0]
    far = [dealt(packed, step) for step in (2, 1, 3)]
    near = swapped(packed)
    field = ((64, 256), F32)
    bf16 = jnp.bfloat16
    groups = []
    sums = ()
    for blocks in BLOCKS:
        if not groups:
            datas = (packed, near)
        elif len(groups) == 1:
            far, sums = lax.optimization_barrier((far, sums))
            far_other = swapped(jnp.stack(far))
            datas = far
        else:
            datas = [far_other[k] for k in range(3)]
        outs = call(
            functools.partial(tables_kernel, blocks=blocks, add=len(sums) > 0),
            [
                ((blocks, 2, 8, 32, 128), F32),
                ((blocks, 2, 8, 32, 128), F32),
                ((blocks, 2, 32, 128), F32),
                ((blocks, 2, 32, 128), jnp.int32),
                ((blocks, 32, 128), F32),
                ((256, 128 * blocks), bf16),
                ((512, 128 * blocks), bf16),
                field,
                field,
                ((1, 256), F32),
            ],
            blocks + len(sums),
            us=0.4 * blocks,
        )(*datas, *sums)
        groups.append(outs[:7])
        sums = tuple(outs[7:])
    own, down, stiff = sums
    parts = [x for g in groups for x in (g[0], g[1], g[4], g[6])]
    send, keep = call(stencil_kernel, [((3, 64, 256), F32), ((2, 64, 256), F32)], 13, us=4.0)(down, *parts)
    above = shifted(send, -1)
    raw = shifted(own, 1)
    fields = [own - above[0]]
    mine = keep + above[1:]
    other = swapped(mine)
    tables = []
    for wx, wy, fx, col, live, ohf, ohs in groups:
        tables += [ohf, ohs, wx, wy, fx, col, live]
    for k in range(ITERS):
        v = fields[-1]
        sent = down
        part, down, gap = call(up_kernel, [field, field, ((8, 32, 128), F32)], 22)(v, *tables)
        above = shifted(down, -1)
        partial = call(functools.partial(down_kernel, back=k > 0), [field], 30)(
            v, raw, sent, fields[max(k - 1, 0)], part, gap, mine, other, stiff, *tables
        )[0]
        if k < ITERS - 1:
            raw = shifted(partial, 1)
        fields.append(partial - above)
    row = call(dots_kernel, [((1, 128), F32)], 4, us=1.0)(*fields[:4])[0]
    row = call(last_kernel, [((1, 128), F32)], 6, us=1.0)(row, *fields)[0]
    row = row + jnp.roll(swapped(row), 32, 1)
    gram = lax.all_to_all(jnp.broadcast_to(row, (32, 128)), "sec", 0, 0, tiled=True)
    mine, other = call(finish_kernel, [((2, 32, 64), F32), ((2, 32, 64), F32)], 6)(gram, *fields)
    other = swapped(other)
    first = jnp.where(core == 0, mine, other)
    last = jnp.where(core == 0, other, mine)
    out = jnp.concatenate([first, last], 2)[:, :, None, :]
    return (out[0], out[1])


def solution(mesh):
    in_specs = (
        P(("sec", "tile")),
        P(("sec", "tile")),
        P(("sec", "tile")),
        P(None, ("sec", "tile")),
        P(None, ("sec", "tile")),
        P(None, None, ("sec", "tile")),
        P(None, None, ("sec", "tile")),
        P(None, None, ("sec", "tile")),
        P("tile", "sec"),
    )
    out_specs = (P("tile", "sec", None), P("tile", "sec", None))
    return jax.shard_map(
        on_device, mesh=mesh, in_specs=in_specs, out_specs=out_specs, check_vma=False
    )
```

```python
import functools

import jax
import jax.numpy as jnp
from jax import lax
from jax.experimental import pallas as pl
from jax.experimental.pallas import tpu as pltpu
from jax.sharding import PartitionSpec as P

ITERS = 4
DAMPING = 0.5
SHIFT = 10.0
SCALE = 1.0 / 128.0
BACK = 25.0 / 16384.0
PAIRS = [(i, j) for i in range(5) for j in range(i, 5) if (i, j) != (4, 4)]
VMEM = pl.BlockSpec(memory_space=pltpu.VMEM)
F32 = jnp.float32
NT = (((1,), (1,)), ((), ()))


def split3(x):
    a = x.astype(jnp.bfloat16)
    rest = x - a.astype(F32)
    b = rest.astype(jnp.bfloat16)
    c = (rest - b.astype(F32)).astype(jnp.bfloat16)
    return jnp.concatenate([a, b, c], 0)


def merge3(x):
    n = x.shape[0] // 3
    return x[:n] + (x[n : 2 * n] + x[2 * n :])


def sublane_ids():
    return lax.broadcasted_iota(jnp.int32, (8, 128), 0)


def fold_rows(parts):
    sub = sublane_ids()
    low = sub < 4
    half = [
        jnp.where(low, parts[p], parts[p + 4])
        + pltpu.roll(jnp.where(low, parts[p + 4], parts[p]), 4, 0)
        for p in range(4)
    ]
    two = (sub & 2) != 0
    quarter = [
        jnp.where(two, half[p + 2] + pltpu.roll(half[p + 2], 2, 0), half[p] + pltpu.roll(half[p], 6, 0))
        for p in range(2)
    ]
    one = (sub & 1) != 0
    return jnp.where(
        one, quarter[1] + pltpu.roll(quarter[1], 1, 0), quarter[0] + pltpu.roll(quarter[0], 7, 0)
    )


def spread_rows(tops, sides):
    rows = []
    for q in range(8):
        parts = []
        for p in range(8):
            acc = tops[q][0] * sides[p][0]
            for group in range(1, 4):
                acc = acc + tops[q][group] * sides[p][group]
            parts.append(acc)
        rows.append(fold_rows(parts))
    return jnp.concatenate(rows, 0)


def sample_block(rows, wy_ref, fx_ref, col_ref, blk, side):
    out = []
    for group in range(4):
        ms = slice(8 * group, 8 * group + 8)
        col = col_ref[blk, side, ms, :]
        nxt = col + 1
        fx = fx_ref[blk, side, ms, :]
        acc = None
        for q in range(8):
            row = rows[8 * q : 8 * q + 8]
            left = jnp.take_along_axis(row, col, axis=0, mode="promise_in_bounds")
            right = jnp.take_along_axis(row, nxt, axis=0, mode="promise_in_bounds")
            term = wy_ref[blk, side, q, ms, :] * (left + fx * (right - left))
            acc = term if acc is None else acc + term
        out.append(acc)
    return out


def load_table(ref, blk, side):
    return [[ref[blk, side, p, 8 * g : 8 * g + 8, :] for g in range(4)] for p in range(8)]


def lanes_of(blk):
    return pl.ds(pl.multiple_of(blk * 128, 128), 128)


def pack_kernel(
    first_hbm, second_hbm, count_hbm, cell1_hbm, cell2_hbm, frac1_hbm, frac2_hbm, target_hbm, stiff_hbm,
    out_ref, ids_ref, stiff_ref, cell_ref, sem, *, sections
):
    copies = [
        pltpu.make_async_copy(cell1_hbm, cell_ref.at[0], sem.at[0]),
        pltpu.make_async_copy(cell2_hbm, cell_ref.at[1], sem.at[1]),
        pltpu.make_async_copy(first_hbm, ids_ref.at[0], sem.at[2]),
        pltpu.make_async_copy(second_hbm, ids_ref.at[1], sem.at[3]),
        pltpu.make_async_copy(count_hbm, ids_ref.at[2], sem.at[4]),
        pltpu.make_async_copy(stiff_hbm, stiff_ref, sem.at[5]),
    ]
    for k, src in enumerate((frac1_hbm, frac2_hbm, target_hbm)):
        for c in range(2):
            at = 64 + 64 * k + 32 * c
            copies.append(pltpu.make_async_copy(src.at[c], out_ref.at[at : at + 32, :], sem.at[6 + 2 * k + c]))
    for copy in copies:
        copy.start()
    for copy in copies:
        copy.wait()
    out_ref[0:32, :] = cell_ref[0].astype(F32)
    out_ref[32:64, :] = cell_ref[1].astype(F32)
    shift = sections.bit_length() - 1
    first = ids_ref[0] >> shift
    second = ids_ref[1] >> shift
    second = second + jnp.where((ids_ref[1] & (sections - 1)) == lax.axis_index("sec"), 0, 256)
    tile = lax.axis_index("tile")
    stiff = jnp.concatenate([stiff_ref[...], jnp.zeros((1, 96), F32)], 1)
    stiff = pltpu.roll(jnp.broadcast_to(stiff, (8, 128)), 32 * (tile & 3), 1)
    row = sublane_ids()
    tail = jnp.where((row >= 3) & (row - 3 == (tile >> 2)), stiff, 0.0)
    for k, x in enumerate((first, second, ids_ref[2])):
        tail = jnp.where(row == k, jnp.broadcast_to(x.astype(F32), (8, 128)), tail)
    out_ref[256:264, :] = tail


def tables_kernel(*refs, blocks, add):
    datas = refs[:blocks]
    refs = refs[blocks:]
    if add:
        before_own, before_down, before_stiff = refs[:3]
        refs = refs[3:]
    wx_ref, wy_ref, fx_ref, col_ref, live_ref, ohf_ref, ohs_ref, own_ref, down_ref, stiff_ref = refs
    comp = lax.axis_index("tile") & 1
    columns = [[], []]
    for blk, data_ref in enumerate(datas):
        lanes = slice(128 * blk, 128 * blk + 128)
        count = data_ref[258, :][None, :]
        goal = []
        for group in range(4):
            ms = slice(8 * group, 8 * group + 8)
            slot = (sublane_ids() + 8 * group).astype(F32)
            live = slot < count
            live_ref[blk, ms, :] = jnp.where(live, SCALE, 0.0)
            at = pl.multiple_of(192 + 32 * comp + 8 * group, 8)
            goal.append(jnp.where(live, data_ref[pl.ds(at, 8), :], 0.0))
        first = data_ref[256, :][None, :].astype(jnp.int32)
        second = data_ref[257, :][None, :].astype(jnp.int32)
        ids = lax.broadcasted_iota(jnp.int32, (256, 128), 0)
        ohf_ref[:, lanes] = jnp.where(ids == first, 1.0, 0.0).astype(jnp.bfloat16)
        ohs_ref[0:256, lanes] = jnp.where(ids == second, 1.0, 0.0).astype(jnp.bfloat16)
        ohs_ref[256:512, lanes] = jnp.where(ids + 256 == second, 1.0, 0.0).astype(jnp.bfloat16)
        for side in range(2):
            for group in range(4):
                ms = slice(8 * group, 8 * group + 8)
                at = 32 * side + 8 * group
                cell = data_ref[at : at + 8, :].astype(jnp.int32)
                base = 64 + 64 * side + 8 * group
                fx = data_ref[base : base + 8, :]
                fy = data_ref[base + 32 : base + 40, :]
                row = (cell * 37) >> 8
                col = cell - 7 * row
                fx_ref[blk, side, ms, :] = fx
                col_ref[blk, side, ms, :] = col
                for k in range(8):
                    wx_ref[blk, side, k, ms, :] = jnp.where(
                        col == k, 1.0 - fx, jnp.where(col == k - 1, fx, 0.0)
                    )
                    wy_ref[blk, side, k, ms, :] = jnp.where(
                        row == k, 1.0 - fy, jnp.where(row == k - 1, fy, 0.0)
                    )
            tops = load_table(wy_ref, blk, side)
            tops = [[tops[q][g] * goal[g] for g in range(4)] for q in range(8)]
            columns[side].append(spread_rows(tops, load_table(wx_ref, blk, side)))
    spreads = [jnp.concatenate(c, 1) for c in columns]
    at_first = merge3(lax.dot_general(split3(spreads[0]), ohf_ref[...], NT, preferred_element_type=F32))
    at_second = merge3(lax.dot_general(split3(spreads[1]), ohs_ref[...], NT, preferred_element_type=F32))
    own = at_first - at_second[:, :256]
    down = at_second[:, 256:]
    stiff = jnp.concatenate(
        [sum(data_ref[row : row + 1, :] for data_ref in datas) for row in (259, 260)], 1
    )
    if add:
        own = own + before_own[...]
        down = down + before_down[...]
        stiff = stiff + before_stiff[...]
    own_ref[...] = own
    down_ref[...] = down
    stiff_ref[...] = stiff


def stencil_kernel(*refs):
    step = lax.axis_index("tile") & 1
    send_ref, keep_ref = refs[4 * len(BLOCKS) :]
    zero = [jnp.zeros((8, 128), F32)] * 4
    terms = [[], []]
    for h, blocks in enumerate(BLOCKS):
        wx_ref, wy_ref, live_ref = refs[4 * h : 4 * h + 3]
        columns = [[], []]
        for blk in range(blocks):
            live = [live_ref[blk, 8 * g : 8 * g + 8, :] for g in range(4)]
            wy = load_table(wy_ref, blk, 1) + [zero]
            tops = [
                [wy[q][g] * jnp.where(step == 0, wy[q][g], wy[q + 1][g]) * live[g] for g in range(4)]
                for q in range(8)
            ]
            wx = load_table(wx_ref, blk, 1) + [zero]
            for kind in range(2):
                sides = [[wx[p][g] * wx[p + kind][g] for g in range(4)] for p in range(8)]
                columns[kind].append(spread_rows(tops, sides))
        for kind in range(2):
            terms[kind].append(split3(jnp.concatenate(columns[kind], 1)))
    for kind in range(2):
        both = scatter(terms[kind], refs[3 : 4 * len(BLOCKS) : 4])
        keep_ref[kind] = both[:, :256]
        send_ref[kind] = both[:, 256:]


def scatter(terms, hots):
    total = None
    for parts, hot in zip(terms, hots):
        term = lax.dot_general(parts, hot[...], NT, preferred_element_type=F32)
        total = term if total is None else total + term
    return merge3(total)


BLOCKS = (2, 4, 2)
AT = (0, 2, 6)


def passed(parts, hot_in, hot_out, tables, side_in, side_out, scale):
    terms = []
    for h, blocks in enumerate(BLOCKS):
        wx_ref, wy_ref, fx_ref, col_ref = tables[h][2:6]
        columns = []
        for start in range(0, blocks, 2):
            stop = min(start + 2, blocks)
            rows = merge3(jnp.dot(parts, hot_in[h][:, 128 * start : 128 * stop], preferred_element_type=F32))
            for blk in range(start, stop):
                at = 128 * (blk - start)
                got = sample_block(rows[:, at : at + 128], wy_ref, fx_ref, col_ref, blk, side_in)
                gap = scale(h, blk, got)
                tops = load_table(wy_ref, blk, side_out)
                tops = [[tops[q][g] * gap[g] for g in range(4)] for q in range(8)]
                columns.append(spread_rows(tops, load_table(wx_ref, blk, side_out)))
        terms.append(split3(jnp.concatenate(columns, 1)))
    return scatter(terms, hot_out)


def up_kernel(v_ref, *refs):
    tables = [refs[7 * h : 7 * h + 7] for h in range(len(BLOCKS))]
    own_ref, down_ref, gap_ref = refs[7 * len(BLOCKS) :]

    def scale(h, blk, got):
        gap = []
        for g in range(4):
            ms = slice(8 * g, 8 * g + 8)
            gap.append(got[g] * tables[h][6][blk, ms, :])
            gap_ref[blk + AT[h], ms, :] = gap[g]
        return gap

    forces = passed(split3(v_ref[...]), [t[0] for t in tables], [t[1] for t in tables], tables, 0, 1, scale)
    own_ref[...] = forces[:, :256]
    down_ref[...] = forces[:, 256:]


def up(x, d):
    return pltpu.roll(x, 64 - d, 0)


def dn(x, d):
    return pltpu.roll(x, d, 0)


def banded(v, mine_ref, other_ref):
    first = (lax.axis_index("tile") & 1) == 0
    band = [jnp.where(first, mine_ref[k], other_ref[k]) for k in range(2)]
    band += [jnp.where(first, other_ref[k], mine_ref[k]) for k in range(2)]
    total = band[0] * v
    total = total + band[1] * up(v, 1) + dn(band[1] * v, 1)
    total = total + band[2] * up(v, 8) + dn(band[2] * v, 8)
    total = total + band[3] * up(v, 9) + dn(band[3] * v, 9)
    return total + dn(band[3] * up(v, 8), 1) + dn(band[3] * up(v, 1), 8)


def band_kernel(part_ref, v_ref, mine_ref, other_ref, out_ref):
    out_ref[...] = part_ref[...] + banded(v_ref[...], mine_ref, other_ref)


def down_kernel(
    v_ref, raw_ref, sent_ref, part_ref, gap_ref, stiff_ref, *refs, back
):
    if back:
        prev_ref, mine_ref, other_ref = refs[:3]
        refs = refs[3:]
    tables = [refs[7 * h : 7 * h + 7] for h in range(len(BLOCKS))]
    (out_ref,) = refs[7 * len(BLOCKS) :]
    v = v_ref[...]
    parts = jnp.concatenate([split3(v), split3(raw_ref[...] - sent_ref[...])], 1)

    def scale(h, blk, got):
        return [
            gap_ref[blk + AT[h], 8 * g : 8 * g + 8, :] - got[g] * tables[h][6][blk, 8 * g : 8 * g + 8, :]
            for g in range(4)
        ]

    forces = passed(parts, [t[1] for t in tables], [t[0] for t in tables], tables, 1, 0, scale)
    node = lax.broadcasted_iota(jnp.int32, (64, 256), 0)
    right = jnp.where((node & 7) < 7, up(v, 1) - v, 0.0)
    below = jnp.where(node < 56, up(v, 8) - v, 0.0)
    bend = (dn(right, 1) - right) + (dn(below, 8) - below)
    total = forces - part_ref[...] + (stiff_ref[...] * SCALE) * bend + ((DAMPING - SHIFT) * SCALE) * v
    if back:
        total = total + banded(v, mine_ref, other_ref)
        total = total - BACK * prev_ref[...]
    out_ref[...] = total


def two_sum(a, b):
    s = a + b
    t = s - a
    return s, (a - (s - t)) + (b - t)


def halves(a):
    c = 4097.0 * a
    high = c - (c - a)
    return high, a - high


def two_prod(a, b):
    p = a * b
    ah, al = halves(a)
    bh, bl = halves(b)
    return p, ((ah * bh - p) + ah * bl + al * bh) + al * bl


def quick(a, b):
    s = a + b
    return s, b - (s - a)


def dd_add(x, y):
    s, e = two_sum(x[0], y[0])
    return quick(s, e + (x[1] + y[1]))


def dd_mul(x, y):
    p, e = two_prod(x[0], y[0])
    return quick(p, e + (x[0] * y[1] + x[1] * y[0]))


def dd_neg(x):
    return (-x[0], -x[1])


def dd_div(x, y):
    q = x[0] / y[0]
    rest = dd_add(x, dd_neg(dd_mul(y, (q, jnp.zeros_like(q)))))
    return quick(q, rest[0] / y[0])


def dots(fields, pairs):
    sub = lax.broadcasted_iota(jnp.int32, (16, 128), 0)
    lane = lax.broadcasted_iota(jnp.int32, (16, 128), 1)
    high = jnp.zeros((16, 128), F32)
    low = jnp.zeros((16, 128), F32)
    for i, j in pairs:
        acc = two_prod(fields[i], fields[j])
        acc = dd_add((acc[0][:, :128], acc[1][:, :128]), (acc[0][:, 128:], acc[1][:, 128:]))
        n = 64
        while n > 8:
            n //= 2
            acc = dd_add((acc[0][:n], acc[1][:n]), (acc[0][n:], acc[1][n:]))
        for d in (4, 2, 1):
            acc = dd_add(acc, (pltpu.roll(acc[0], d, 0), pltpu.roll(acc[1], d, 0)))
        wide = [jnp.concatenate([a, a], 0) for a in acc]
        here = sub == PAIRS.index((i, j))
        high = jnp.where(here, wide[0], high)
        low = jnp.where(here, wide[1], low)
    acc = (high, low)
    for d in (64, 32, 16, 8, 4, 2, 1):
        acc = dd_add(acc, (pltpu.roll(acc[0], d, 1), pltpu.roll(acc[1], d, 1)))
    row = jnp.where(lane == sub, acc[0], 0.0) + jnp.where(lane == sub + 16, acc[1], 0.0)
    return jnp.sum(row, 0, keepdims=True)


def dots_kernel(v0, v1, v2, v3, out_ref):
    out_ref[...] = dots([r[...] for r in (v0, v1, v2, v3)], [p for p in PAIRS if p[1] < 4])


def last_kernel(row_ref, v0, v1, v2, v3, v4, out_ref, slice_ref):
    fields = [r[...] for r in (v0, v1, v2, v3, v4)]
    y = lax.axis_index("tile") >> 1
    for k in range(3):
        sides = []
        for m in (2 * k, 2 * k + 1):
            if m < 5:
                x = jnp.where(y >= 2, fields[m][:, 128:], fields[m][:, :128])
                sides.append((x, pltpu.roll(x, 64, 1)))
            else:
                sides.append((jnp.zeros((64, 128), F32),) * 2)
        left = jnp.where((y & 1) == 0, sides[0][0], sides[0][1])
        right = jnp.where((y & 1) == 0, sides[1][1], sides[1][0])
        lane = lax.broadcasted_iota(jnp.int32, (64, 128), 1)
        slice_ref[k] = jnp.where(lane < 64, left, right)
    out_ref[...] = row_ref[...] + dots(fields, [p for p in PAIRS if p[1] == 4])


def finish_kernel(gram_ref, slice_ref, mine_ref, other_ref):
    rows = gram_ref[...]
    acc = dd_add((rows, pltpu.roll(rows, 112, 1)), (pltpu.roll(rows, 96, 1), pltpu.roll(rows, 80, 1)))
    n = 32
    while n > 8:
        n //= 2
        acc = dd_add((acc[0][:n], acc[1][:n]), (acc[0][n:], acc[1][n:]))
    for d in (4, 2, 1):
        acc = dd_add(acc, (pltpu.roll(acc[0], d, 0), pltpu.roll(acc[1], d, 0)))
    gram = {}
    for k, (i, j) in enumerate(PAIRS):
        pair = tuple(jnp.broadcast_to(a[:, k : k + 1], (8, 128)) for a in acc)
        gram[(i, j)] = pair
        gram[(j, i)] = pair
    zero = jnp.zeros((8, 128), F32)
    const = lambda c: (jnp.full((8, 128), c, F32), zero)

    def tree(terms):
        while len(terms) > 1:
            terms = [dd_add(*terms[k : k + 2]) if k + 1 < len(terms) else terms[k] for k in range(0, len(terms), 2)]
        return terms[0]

    def form(a, b):
        return tree([dd_mul(bj, tree([dd_mul(ai, gram[(i, j)]) for i, ai in enumerate(a)])) for j, bj in enumerate(b)])

    def apply(p):
        out = [const(0.0) for _ in range(len(p) + 1)]
        for k, c in enumerate(p):
            out[k + 1] = dd_add(out[k + 1], (c[0] * 128.0, c[1] * 128.0))
            out[k] = dd_add(out[k], dd_mul(c, const(SHIFT)))
            if k >= 1:
                out[k - 1] = dd_add(out[k - 1], dd_mul(c, const(BACK * 128.0)))
        return out

    def axpy(a, x, y):
        out = []
        for k in range(max(len(x), len(y))):
            if k >= len(x):
                out.append(y[k])
            elif k >= len(y):
                out.append(dd_mul(a, x[k]))
            else:
                out.append(dd_add(y[k], dd_mul(a, x[k])))
        return out

    res = [const(1.0)]
    direc = [const(1.0)]
    sol = []
    norm = gram[(0, 0)]
    for it in range(ITERS):
        image = apply(direc)
        step = dd_div(norm, form(direc, image))
        sol = axpy(step, direc, sol)
        res = axpy(dd_neg(step), image, res)
        if it < ITERS - 1:
            new = form(res, res)
            direc = axpy(dd_div(new, norm), direc, res)
            norm = new
    lane = lax.broadcasted_iota(jnp.int32, (64, 128), 1)

    def combine(coefs):
        total = jnp.zeros((64, 128), F32)
        flat = [c[0][0:1, 0:1] for c in coefs] + [jnp.zeros((1, 1), F32)] * (6 - len(coefs))
        for k in range(3):
            total = total + jnp.where(lane < 64, flat[2 * k], flat[2 * k + 1]) * slice_ref[k]
        return total + pltpu.roll(total, 64, 1)

    core = lax.axis_index("tile") & 1
    want = lax.broadcasted_iota(jnp.int32, (64, 128), 0)
    want = jnp.where(want < 32, want + 32 * core, want - 32 * core)
    pick = jnp.where(lane == want, 1.0, 0.0).astype(jnp.bfloat16)
    for k, coefs in enumerate((sol, res)):
        parts = lax.dot_general(pick, split3(combine(coefs)), NT, preferred_element_type=F32)
        both = parts[:, :64] + (parts[:, 64:128] + parts[:, 128:192])
        mine_ref[k] = both[:32]
        other_ref[k] = both[32:]


def call(kernel, outs, n_in, scratch=(), us=2.0, hbm=0, grant=8):
    return pl.pallas_call(
        kernel,
        out_shape=[jax.ShapeDtypeStruct(s, d) for s, d in outs],
        in_specs=[VMEM] * (n_in - hbm)
        + [pl.BlockSpec(memory_space=pl.ANY)] * hbm,
        out_specs=[VMEM] * len(outs),
        scratch_shapes=list(scratch),
        compiler_params=pltpu.CompilerParams(vmem_limit_bytes=grant * 1024 * 1024),
        cost_estimate=pl.CostEstimate(flops=int(us * 1e9), bytes_accessed=1 << 18, transcendentals=0),
    )


ROW = 4
CHIPS = 4


def seat(section, y, sections):
    row, col = divmod(section, ROW)
    col = col if row % 2 == 0 else ROW - 1 - col
    row = row if y % 2 == 0 else sections // ROW - 1 - row
    return row * ROW + col


def shifted(block, distance):
    sections = lax.axis_size("sec")
    route = []
    for section in range(sections):
        there = (section + distance) % sections
        crosses = (section < sections // 2) != (there < sections // 2)
        for y in range(CHIPS):
            to = y ^ 1 if crosses else y
            for core in range(2):
                route.append(
                    (seat(section, y, sections) * 8 + 2 * y + core, seat(there, to, sections) * 8 + 2 * to + core)
                )
    return lax.ppermute(block, ("sec", "tile"), route)


def swapped(block):
    return lax.ppermute(block, "tile", [(i, i ^ 1) for i in range(8)])


def dealt(block, step):
    sections = lax.axis_size("sec")
    route = []
    for section in range(sections):
        for y in range(CHIPS):
            to = (y + step) % CHIPS
            for core in range(2):
                route.append((section * 8 + 2 * y + core, seat(section, to, sections) * 8 + 2 * to + core))
    return lax.ppermute(block, ("sec", "tile"), route)


def returned(block):
    sections = lax.axis_size("sec")
    route = []
    for section in range(sections):
        for tile in range(2 * CHIPS):
            route.append((seat(section, tile // 2, sections) * 8 + tile, section * 8 + tile))
    return lax.ppermute(block, ("sec", "tile"), route)


def on_device(
    ov_first, ov_second, match_count, cell_first, cell_second, frac_first, frac_second, target, stiffness
):
    tile = lax.axis_index("tile")
    core = tile % 2
    sections = lax.axis_size("sec")
    dma = pltpu.SemaphoreType.DMA
    packed = call(
        functools.partial(pack_kernel, sections=sections),
        [((264, 128), F32)],
        9,
        [
            pltpu.VMEM((3, 1, 128), jnp.int32),
            pltpu.VMEM((1, 32), F32),
            pltpu.VMEM((2, 32, 128), jnp.int32),
            dma((12,)),
        ],
        hbm=9,
        grant=60,
    )(
        ov_first.reshape(1, 128),
        ov_second.reshape(1, 128),
        match_count.reshape(1, 128),
        cell_first,
        cell_second,
        frac_first,
        frac_second,
        target,
        stiffness.reshape(1, 32),
    )[0]
    far = [dealt(packed, step) for step in (0, 3, 1, 2)]
    field = ((64, 256), F32)
    bf16 = jnp.bfloat16
    groups = []
    sums = ()
    for k, blocks in enumerate(BLOCKS):
        if k == 0:
            datas = far[:2]
            near = [swapped(x) for x in datas]
        elif k == 1:
            late, sums = lax.optimization_barrier((far[2:], sums))
            datas = near + late
            near = [swapped(x) for x in late]
        else:
            datas = near
        outs = call(
            functools.partial(tables_kernel, blocks=blocks, add=len(sums) > 0),
            [
                ((blocks, 2, 8, 32, 128), F32),
                ((blocks, 2, 8, 32, 128), F32),
                ((blocks, 2, 32, 128), F32),
                ((blocks, 2, 32, 128), jnp.int32),
                ((blocks, 32, 128), F32),
                ((256, 128 * blocks), bf16),
                ((512, 128 * blocks), bf16),
                field,
                field,
                ((1, 256), F32),
            ],
            blocks + len(sums),
            us=0.4 * blocks,
        )(*datas, *sums)
        groups.append(outs[:7])
        sums = tuple(outs[7:])
    own, down, stiff = sums
    parts = [x for g in groups for x in (g[0], g[1], g[4], g[6])]
    above = shifted(down, -1)
    raw = shifted(own, 1)
    send, keep = call(stencil_kernel, [((2, 64, 256), F32)] * 2, len(parts), us=4.0)(*parts)
    above, send = lax.optimization_barrier((above, send))
    got = shifted(send, -1)
    fields = [own - above]
    tables = []
    for wx, wy, fx, col, live, ohf, ohs in groups:
        tables += [ohf, ohs, wx, wy, fx, col, live]
    for k in range(ITERS):
        v = fields[-1]
        sent = down
        part, down, gap = call(up_kernel, [field, field, ((8, 32, 128), F32)], 1 + len(tables))(v, *tables)
        above = shifted(down, -1)
        more = (fields[k - 1], mine, other) if k else ()
        partial = call(functools.partial(down_kernel, back=k > 0), [field], 6 + len(more) + len(tables))(
            v, raw, sent, part, gap, stiff, *more, *tables
        )[0]
        if k == 0:
            mine = keep + got
            other = swapped(mine)
            partial = call(band_kernel, [field], 4, us=0.3)(partial, v, mine, other)[0]
        if k < ITERS - 1:
            raw = shifted(partial, 1)
        fields.append(partial - above)
    row = call(dots_kernel, [((1, 128), F32)], 4, us=1.0)(*fields[:4])[0]
    row, slices = call(last_kernel, [((1, 128), F32), ((3, 64, 128), F32)], 6, us=1.0)(row, *fields)
    slices = returned(slices)
    row = row + jnp.roll(swapped(row), 32, 1)
    gram = lax.all_to_all(jnp.broadcast_to(row, (32, 128)), "sec", 0, 0, tiled=True)
    mine, other = call(finish_kernel, [((2, 32, 64), F32), ((2, 32, 64), F32)], 2)(gram, slices)
    other = swapped(other)
    first = jnp.where(core == 0, mine, other)
    last = jnp.where(core == 0, other, mine)
    out = jnp.concatenate([first, last], 2)[:, :, None, :]
    return (out[0], out[1])


def solution(mesh):
    in_specs = (
        P(("sec", "tile")),
        P(("sec", "tile")),
        P(("sec", "tile")),
        P(None, ("sec", "tile")),
        P(None, ("sec", "tile")),
        P(None, None, ("sec", "tile")),
        P(None, None, ("sec", "tile")),
        P(None, None, ("sec", "tile")),
        P("tile", "sec"),
    )
    out_specs = (P("tile", "sec", None), P("tile", "sec", None))
    return jax.shard_map(
        on_device, mesh=mesh, in_specs=in_specs, out_specs=out_specs, check_vma=False
    )
```

```python
import functools

import jax
import jax.numpy as jnp
from jax import lax
from jax.experimental import pallas as pl
from jax.experimental.pallas import tpu as pltpu
from jax.sharding import PartitionSpec as P

ITERS = 4
DAMPING = 0.5
SHIFT = 10.0
SCALE = 1.0 / 128.0
BACK = 25.0 / 16384.0
PAIRS = [(i, j) for i in range(5) for j in range(i, 5) if (i, j) != (4, 4)]
VMEM = pl.BlockSpec(memory_space=pltpu.VMEM)
F32 = jnp.float32
NT = (((1,), (1,)), ((), ()))


def split3(x):
    a = x.astype(jnp.bfloat16)
    rest = x - a.astype(F32)
    b = rest.astype(jnp.bfloat16)
    c = (rest - b.astype(F32)).astype(jnp.bfloat16)
    return jnp.concatenate([a, b, c], 0)


def merge3(x):
    n = x.shape[0] // 3
    return x[:n] + (x[n : 2 * n] + x[2 * n :])


def sublane_ids():
    return lax.broadcasted_iota(jnp.int32, (8, 128), 0)


def fold_rows(parts):
    sub = sublane_ids()
    low = sub < 4
    half = [
        jnp.where(low, parts[p], parts[p + 4])
        + pltpu.roll(jnp.where(low, parts[p + 4], parts[p]), 4, 0)
        for p in range(4)
    ]
    two = (sub & 2) != 0
    quarter = [
        jnp.where(two, half[p + 2] + pltpu.roll(half[p + 2], 2, 0), half[p] + pltpu.roll(half[p], 6, 0))
        for p in range(2)
    ]
    one = (sub & 1) != 0
    return jnp.where(
        one, quarter[1] + pltpu.roll(quarter[1], 1, 0), quarter[0] + pltpu.roll(quarter[0], 7, 0)
    )


def spread_rows(tops, sides):
    rows = []
    for q in range(8):
        parts = []
        for p in range(8):
            acc = tops[q][0] * sides[p][0]
            for group in range(1, 4):
                acc = acc + tops[q][group] * sides[p][group]
            parts.append(acc)
        rows.append(fold_rows(parts))
    return jnp.concatenate(rows, 0)


def sample_block(rows, wy_ref, fx_ref, col_ref, blk, side):
    out = []
    for group in range(4):
        ms = slice(8 * group, 8 * group + 8)
        col = col_ref[blk, side, ms, :]
        nxt = col + 1
        fx = fx_ref[blk, side, ms, :]
        acc = None
        for q in range(8):
            row = rows[8 * q : 8 * q + 8]
            left = jnp.take_along_axis(row, col, axis=0, mode="promise_in_bounds")
            right = jnp.take_along_axis(row, nxt, axis=0, mode="promise_in_bounds")
            term = wy_ref[blk, side, q, ms, :] * (left + fx * (right - left))
            acc = term if acc is None else acc + term
        out.append(acc)
    return out


def load_table(ref, blk, side):
    return [[ref[blk, side, p, 8 * g : 8 * g + 8, :] for g in range(4)] for p in range(8)]


def lanes_of(blk):
    return pl.ds(pl.multiple_of(blk * 128, 128), 128)


def pack_kernel(
    first_hbm, second_hbm, count_hbm, cell1_hbm, cell2_hbm, frac1_hbm, frac2_hbm, target_hbm, stiff_hbm,
    out_ref, ids_ref, stiff_ref, cell_ref, sem, *, sections
):
    copies = [
        pltpu.make_async_copy(cell1_hbm, cell_ref.at[0], sem.at[0]),
        pltpu.make_async_copy(cell2_hbm, cell_ref.at[1], sem.at[1]),
        pltpu.make_async_copy(first_hbm, ids_ref.at[0], sem.at[2]),
        pltpu.make_async_copy(second_hbm, ids_ref.at[1], sem.at[3]),
        pltpu.make_async_copy(count_hbm, ids_ref.at[2], sem.at[4]),
        pltpu.make_async_copy(stiff_hbm, stiff_ref, sem.at[5]),
    ]
    for k, src in enumerate((frac1_hbm, frac2_hbm, target_hbm)):
        for c in range(2):
            at = 64 + 64 * k + 32 * c
            copies.append(pltpu.make_async_copy(src.at[c], out_ref.at[at : at + 32, :], sem.at[6 + 2 * k + c]))
    for copy in copies:
        copy.start()
    for copy in copies:
        copy.wait()
    out_ref[0:32, :] = cell_ref[0].astype(F32)
    out_ref[32:64, :] = cell_ref[1].astype(F32)
    shift = sections.bit_length() - 1
    first = ids_ref[0] >> shift
    second = ids_ref[1] >> shift
    second = second + jnp.where((ids_ref[1] & (sections - 1)) == lax.axis_index("sec"), 0, 256)
    tile = lax.axis_index("tile")
    stiff = jnp.concatenate([stiff_ref[...], jnp.zeros((1, 96), F32)], 1)
    stiff = pltpu.roll(jnp.broadcast_to(stiff, (8, 128)), 32 * (tile & 3), 1)
    row = sublane_ids()
    tail = jnp.where((row >= 3) & (row - 3 == (tile >> 2)), stiff, 0.0)
    for k, x in enumerate((first, second, ids_ref[2])):
        tail = jnp.where(row == k, jnp.broadcast_to(x.astype(F32), (8, 128)), tail)
    out_ref[256:264, :] = tail


def tables_kernel(*refs, blocks, add):
    datas = refs[:blocks]
    refs = refs[blocks:]
    if add:
        before_own, before_down, before_stiff = refs[:3]
        refs = refs[3:]
    wx_ref, wy_ref, fx_ref, col_ref, live_ref, ohf_ref, ohs_ref, own_ref, down_ref, stiff_ref = refs
    comp = lax.axis_index("tile") & 1
    columns = [[], []]
    for blk, data_ref in enumerate(datas):
        lanes = slice(128 * blk, 128 * blk + 128)
        count = data_ref[258, :][None, :]
        goal = []
        for group in range(4):
            ms = slice(8 * group, 8 * group + 8)
            slot = (sublane_ids() + 8 * group).astype(F32)
            live = slot < count
            live_ref[blk, ms, :] = jnp.where(live, SCALE, 0.0)
            at = pl.multiple_of(192 + 32 * comp + 8 * group, 8)
            goal.append(jnp.where(live, data_ref[pl.ds(at, 8), :], 0.0))
        first = data_ref[256, :][None, :].astype(jnp.int32)
        second = data_ref[257, :][None, :].astype(jnp.int32)
        ids = lax.broadcasted_iota(jnp.int32, (256, 128), 0)
        ohf_ref[:, lanes] = jnp.where(ids == first, 1.0, 0.0).astype(jnp.bfloat16)
        ohs_ref[0:256, lanes] = jnp.where(ids == second, 1.0, 0.0).astype(jnp.bfloat16)
        ohs_ref[256:512, lanes] = jnp.where(ids + 256 == second, 1.0, 0.0).astype(jnp.bfloat16)
        for side in range(2):
            for group in range(4):
                ms = slice(8 * group, 8 * group + 8)
                at = 32 * side + 8 * group
                cell = data_ref[at : at + 8, :].astype(jnp.int32)
                base = 64 + 64 * side + 8 * group
                fx = data_ref[base : base + 8, :]
                fy = data_ref[base + 32 : base + 40, :]
                row = (cell * 37) >> 8
                col = cell - 7 * row
                fx_ref[blk, side, ms, :] = fx
                col_ref[blk, side, ms, :] = col
                for k in range(8):
                    wx_ref[blk, side, k, ms, :] = jnp.where(
                        col == k, 1.0 - fx, jnp.where(col == k - 1, fx, 0.0)
                    )
                    wy_ref[blk, side, k, ms, :] = jnp.where(
                        row == k, 1.0 - fy, jnp.where(row == k - 1, fy, 0.0)
                    )
            tops = load_table(wy_ref, blk, side)
            tops = [[tops[q][g] * goal[g] for g in range(4)] for q in range(8)]
            columns[side].append(spread_rows(tops, load_table(wx_ref, blk, side)))
    spreads = [jnp.concatenate(c, 1) for c in columns]
    at_first = merge3(lax.dot_general(split3(spreads[0]), ohf_ref[...], NT, preferred_element_type=F32))
    at_second = merge3(lax.dot_general(split3(spreads[1]), ohs_ref[...], NT, preferred_element_type=F32))
    own = at_first - at_second[:, :256]
    down = at_second[:, 256:]
    stiff = jnp.concatenate(
        [sum(data_ref[row : row + 1, :] for data_ref in datas) for row in (259, 260)], 1
    )
    if add:
        own = own + before_own[...]
        down = down + before_down[...]
        stiff = stiff + before_stiff[...]
    own_ref[...] = own
    down_ref[...] = down
    stiff_ref[...] = stiff


def stencil_kernel(*refs):
    step = lax.axis_index("tile") & 1
    send_ref, keep_ref = refs[4 * len(BLOCKS) :]
    zero = [jnp.zeros((8, 128), F32)] * 4
    terms = [[], []]
    for h, blocks in enumerate(BLOCKS):
        wx_ref, wy_ref, live_ref = refs[4 * h : 4 * h + 3]
        columns = [[], []]
        for blk in range(blocks):
            live = [live_ref[blk, 8 * g : 8 * g + 8, :] for g in range(4)]
            wy = load_table(wy_ref, blk, 1) + [zero]
            tops = [
                [wy[q][g] * jnp.where(step == 0, wy[q][g], wy[q + 1][g]) * live[g] for g in range(4)]
                for q in range(8)
            ]
            wx = load_table(wx_ref, blk, 1) + [zero]
            for kind in range(2):
                sides = [[wx[p][g] * wx[p + kind][g] for g in range(4)] for p in range(8)]
                columns[kind].append(spread_rows(tops, sides))
        for kind in range(2):
            terms[kind].append(split3(jnp.concatenate(columns[kind], 1)))
    for kind in range(2):
        both = scatter(terms[kind], refs[3 : 4 * len(BLOCKS) : 4])
        keep_ref[kind] = both[:, :256]
        send_ref[kind] = both[:, 256:]


def scatter(terms, hots):
    total = None
    for parts, hot in zip(terms, hots):
        term = lax.dot_general(parts, hot[...], NT, preferred_element_type=F32)
        total = term if total is None else total + term
    return merge3(total)


BLOCKS = (2, 4, 2)
AT = (0, 2, 6)


def passed(parts, hot_in, hot_out, tables, side_in, side_out, scale):
    terms = []
    for h, blocks in enumerate(BLOCKS):
        wx_ref, wy_ref, fx_ref, col_ref = tables[h][2:6]
        columns = []
        for start in range(0, blocks, 2):
            stop = min(start + 2, blocks)
            rows = merge3(jnp.dot(parts, hot_in[h][:, 128 * start : 128 * stop], preferred_element_type=F32))
            for blk in range(start, stop):
                at = 128 * (blk - start)
                got = sample_block(rows[:, at : at + 128], wy_ref, fx_ref, col_ref, blk, side_in)
                gap = scale(h, blk, got)
                tops = load_table(wy_ref, blk, side_out)
                tops = [[tops[q][g] * gap[g] for g in range(4)] for q in range(8)]
                columns.append(spread_rows(tops, load_table(wx_ref, blk, side_out)))
        terms.append(split3(jnp.concatenate(columns, 1)))
    return scatter(terms, hot_out)


def up_kernel(v_ref, *refs):
    tables = [refs[7 * h : 7 * h + 7] for h in range(len(BLOCKS))]
    own_ref, down_ref, gap_ref = refs[7 * len(BLOCKS) :]

    def scale(h, blk, got):
        gap = []
        for g in range(4):
            ms = slice(8 * g, 8 * g + 8)
            gap.append(got[g] * tables[h][6][blk, ms, :])
            gap_ref[blk + AT[h], ms, :] = gap[g]
        return gap

    forces = passed(split3(v_ref[...]), [t[0] for t in tables], [t[1] for t in tables], tables, 0, 1, scale)
    own_ref[...] = forces[:, :256]
    down_ref[...] = forces[:, 256:]


def up(x, d):
    return pltpu.roll(x, 64 - d, 0)


def dn(x, d):
    return pltpu.roll(x, d, 0)


def banded(v, mine_ref, other_ref):
    first = (lax.axis_index("tile") & 1) == 0
    band = [jnp.where(first, mine_ref[k], other_ref[k]) for k in range(2)]
    band += [jnp.where(first, other_ref[k], mine_ref[k]) for k in range(2)]
    total = band[0] * v
    total = total + band[1] * up(v, 1) + dn(band[1] * v, 1)
    total = total + band[2] * up(v, 8) + dn(band[2] * v, 8)
    total = total + band[3] * up(v, 9) + dn(band[3] * v, 9)
    return total + dn(band[3] * up(v, 8), 1) + dn(band[3] * up(v, 1), 8)


def band_kernel(part_ref, v_ref, mine_ref, other_ref, out_ref):
    out_ref[...] = part_ref[...] + banded(v_ref[...], mine_ref, other_ref)


def down_kernel(
    v_ref, raw_ref, sent_ref, part_ref, gap_ref, stiff_ref, *refs, back
):
    if back:
        prev_ref, mine_ref, other_ref = refs[:3]
        refs = refs[3:]
    tables = [refs[7 * h : 7 * h + 7] for h in range(len(BLOCKS))]
    (out_ref,) = refs[7 * len(BLOCKS) :]
    v = v_ref[...]
    parts = jnp.concatenate([split3(v), split3(raw_ref[...] - sent_ref[...])], 1)

    def scale(h, blk, got):
        return [
            gap_ref[blk + AT[h], 8 * g : 8 * g + 8, :] - got[g] * tables[h][6][blk, 8 * g : 8 * g + 8, :]
            for g in range(4)
        ]

    forces = passed(parts, [t[1] for t in tables], [t[0] for t in tables], tables, 1, 0, scale)
    node = lax.broadcasted_iota(jnp.int32, (64, 256), 0)
    right = jnp.where((node & 7) < 7, up(v, 1) - v, 0.0)
    below = jnp.where(node < 56, up(v, 8) - v, 0.0)
    bend = (dn(right, 1) - right) + (dn(below, 8) - below)
    total = forces - part_ref[...] + (stiff_ref[...] * SCALE) * bend + ((DAMPING - SHIFT) * SCALE) * v
    if back:
        total = total + banded(v, mine_ref, other_ref)
        total = total - BACK * prev_ref[...]
    out_ref[...] = total


def two_sum(a, b):
    s = a + b
    t = s - a
    return s, (a - (s - t)) + (b - t)


def halves(a):
    c = 4097.0 * a
    high = c - (c - a)
    return high, a - high


def two_prod(a, b):
    return split_prod(a, b, halves(a), halves(b))


def split_prod(a, b, a_halves, b_halves):
    p = a * b
    ah, al = a_halves
    bh, bl = b_halves
    return p, ((ah * bh - p) + ah * bl + al * bh) + al * bl


def quick(a, b):
    s = a + b
    return s, b - (s - a)


def dd_add(x, y):
    s, e = two_sum(x[0], y[0])
    return quick(s, e + (x[1] + y[1]))


def dd_mul(x, y):
    p, e = two_prod(x[0], y[0])
    return quick(p, e + (x[0] * y[1] + x[1] * y[0]))


def dd_neg(x):
    return (-x[0], -x[1])


def dd_div(x, y):
    q = x[0] / y[0]
    rest = dd_add(x, dd_neg(dd_mul(y, (q, jnp.zeros_like(q)))))
    return quick(q, rest[0] / y[0])


def dots(fields, pairs):
    sub = lax.broadcasted_iota(jnp.int32, (16, 128), 0)
    lane = lax.broadcasted_iota(jnp.int32, (16, 128), 1)
    high = jnp.zeros((16, 128), F32)
    low = jnp.zeros((16, 128), F32)
    cut = [halves(f) for f in fields]
    for i, j in pairs:
        acc = split_prod(fields[i], fields[j], cut[i], cut[j])
        acc = dd_add((acc[0][:, :128], acc[1][:, :128]), (acc[0][:, 128:], acc[1][:, 128:]))
        n = 64
        while n > 8:
            n //= 2
            acc = dd_add((acc[0][:n], acc[1][:n]), (acc[0][n:], acc[1][n:]))
        for d in (4, 2, 1):
            acc = dd_add(acc, (pltpu.roll(acc[0], d, 0), pltpu.roll(acc[1], d, 0)))
        wide = [jnp.concatenate([a, a], 0) for a in acc]
        here = sub == PAIRS.index((i, j))
        high = jnp.where(here, wide[0], high)
        low = jnp.where(here, wide[1], low)
    acc = (high, low)
    for d in (64, 32, 16, 8, 4, 2, 1):
        acc = dd_add(acc, (pltpu.roll(acc[0], d, 1), pltpu.roll(acc[1], d, 1)))
    row = jnp.where(lane == sub, acc[0], 0.0) + jnp.where(lane == sub + 16, acc[1], 0.0)
    return jnp.sum(row, 0, keepdims=True)


def dots_kernel(v0, v1, v2, v3, out_ref):
    out_ref[...] = dots([r[...] for r in (v0, v1, v2, v3)], [p for p in PAIRS if p[1] < 4])


def last_kernel(row_ref, v0, v1, v2, v3, v4, out_ref, slice_ref):
    fields = [r[...] for r in (v0, v1, v2, v3, v4)]
    y = lax.axis_index("tile") >> 1
    for k in range(3):
        sides = []
        for m in (2 * k, 2 * k + 1):
            if m < 5:
                x = jnp.where(y >= 2, fields[m][:, 128:], fields[m][:, :128])
                sides.append((x, pltpu.roll(x, 64, 1)))
            else:
                sides.append((jnp.zeros((64, 128), F32),) * 2)
        left = jnp.where((y & 1) == 0, sides[0][0], sides[0][1])
        right = jnp.where((y & 1) == 0, sides[1][1], sides[1][0])
        lane = lax.broadcasted_iota(jnp.int32, (64, 128), 1)
        slice_ref[k] = jnp.where(lane < 64, left, right)
    out_ref[...] = row_ref[...] + dots(fields, [p for p in PAIRS if p[1] == 4])


def finish_kernel(gram_ref, slice_ref, mine_ref, other_ref):
    rows = gram_ref[...]
    acc = dd_add((rows, pltpu.roll(rows, 112, 1)), (pltpu.roll(rows, 96, 1), pltpu.roll(rows, 80, 1)))
    n = 32
    while n > 8:
        n //= 2
        acc = dd_add((acc[0][:n], acc[1][:n]), (acc[0][n:], acc[1][n:]))
    for d in (4, 2, 1):
        acc = dd_add(acc, (pltpu.roll(acc[0], d, 0), pltpu.roll(acc[1], d, 0)))
    gram = {}
    for k, (i, j) in enumerate(PAIRS):
        pair = tuple(jnp.broadcast_to(a[:, k : k + 1], (8, 128)) for a in acc)
        gram[(i, j)] = pair
        gram[(j, i)] = pair
    zero = jnp.zeros((8, 128), F32)
    const = lambda c: (jnp.full((8, 128), c, F32), zero)

    def tree(terms):
        while len(terms) > 1:
            terms = [dd_add(*terms[k : k + 2]) if k + 1 < len(terms) else terms[k] for k in range(0, len(terms), 2)]
        return terms[0]

    def form(a, b):
        return tree([dd_mul(bj, tree([dd_mul(ai, gram[(i, j)]) for i, ai in enumerate(a)])) for j, bj in enumerate(b)])

    def apply(p):
        out = [const(0.0) for _ in range(len(p) + 1)]
        for k, c in enumerate(p):
            out[k + 1] = dd_add(out[k + 1], (c[0] * 128.0, c[1] * 128.0))
            out[k] = dd_add(out[k], dd_mul(c, const(SHIFT)))
            if k >= 1:
                out[k - 1] = dd_add(out[k - 1], dd_mul(c, const(BACK * 128.0)))
        return out

    def axpy(a, x, y):
        out = []
        for k in range(max(len(x), len(y))):
            if k >= len(x):
                out.append(y[k])
            elif k >= len(y):
                out.append(dd_mul(a, x[k]))
            else:
                out.append(dd_add(y[k], dd_mul(a, x[k])))
        return out

    res = [const(1.0)]
    direc = [const(1.0)]
    sol = []
    norm = gram[(0, 0)]
    for it in range(ITERS):
        image = apply(direc)
        step = dd_div(norm, form(direc, image))
        sol = axpy(step, direc, sol)
        res = axpy(dd_neg(step), image, res)
        if it < ITERS - 1:
            new = form(res, res)
            direc = axpy(dd_div(new, norm), direc, res)
            norm = new
    lane = lax.broadcasted_iota(jnp.int32, (64, 128), 1)

    def combine(coefs):
        total = jnp.zeros((64, 128), F32)
        flat = [c[0][0:1, 0:1] for c in coefs] + [jnp.zeros((1, 1), F32)] * (6 - len(coefs))
        for k in range(3):
            total = total + jnp.where(lane < 64, flat[2 * k], flat[2 * k + 1]) * slice_ref[k]
        return total + pltpu.roll(total, 64, 1)

    core = lax.axis_index("tile") & 1
    want = lax.broadcasted_iota(jnp.int32, (64, 128), 0)
    want = jnp.where(want < 32, want + 32 * core, want - 32 * core)
    pick = jnp.where(lane == want, 1.0, 0.0).astype(jnp.bfloat16)
    for k, coefs in enumerate((sol, res)):
        parts = lax.dot_general(pick, split3(combine(coefs)), NT, preferred_element_type=F32)
        both = parts[:, :64] + (parts[:, 64:128] + parts[:, 128:192])
        mine_ref[k] = both[:32]
        other_ref[k] = both[32:]


def call(kernel, outs, n_in, scratch=(), us=2.0, hbm=0, grant=8):
    return pl.pallas_call(
        kernel,
        out_shape=[jax.ShapeDtypeStruct(s, d) for s, d in outs],
        in_specs=[VMEM] * (n_in - hbm)
        + [pl.BlockSpec(memory_space=pl.ANY)] * hbm,
        out_specs=[VMEM] * len(outs),
        scratch_shapes=list(scratch),
        compiler_params=pltpu.CompilerParams(vmem_limit_bytes=grant * 1024 * 1024),
        cost_estimate=pl.CostEstimate(flops=int(us * 1e9), bytes_accessed=1 << 18, transcendentals=0),
    )


ROW = 4
CHIPS = 4


def seat(section, y, sections):
    row, col = divmod(section, ROW)
    col = col if row % 2 == 0 else ROW - 1 - col
    row = row if y % 2 == 0 else sections // ROW - 1 - row
    return row * ROW + col


def shifted(block, distance):
    sections = lax.axis_size("sec")
    route = []
    for section in range(sections):
        there = (section + distance) % sections
        crosses = (section < sections // 2) != (there < sections // 2)
        for y in range(CHIPS):
            to = y ^ 1 if crosses else y
            for core in range(2):
                route.append(
                    (seat(section, y, sections) * 8 + 2 * y + core, seat(there, to, sections) * 8 + 2 * to + core)
                )
    return lax.ppermute(block, ("sec", "tile"), route)


def swapped(block):
    return lax.ppermute(block, "tile", [(i, i ^ 1) for i in range(8)])


def dealt(block, step):
    sections = lax.axis_size("sec")
    route = []
    for section in range(sections):
        for y in range(CHIPS):
            to = (y + step) % CHIPS
            for core in range(2):
                route.append((section * 8 + 2 * y + core, seat(section, to, sections) * 8 + 2 * to + core))
    return lax.ppermute(block, ("sec", "tile"), route)


def returned(block):
    sections = lax.axis_size("sec")
    route = []
    for section in range(sections):
        for tile in range(2 * CHIPS):
            route.append((seat(section, tile // 2, sections) * 8 + tile, section * 8 + tile))
    return lax.ppermute(block, ("sec", "tile"), route)


def on_device(
    ov_first, ov_second, match_count, cell_first, cell_second, frac_first, frac_second, target, stiffness
):
    tile = lax.axis_index("tile")
    core = tile % 2
    sections = lax.axis_size("sec")
    dma = pltpu.SemaphoreType.DMA
    packed = call(
        functools.partial(pack_kernel, sections=sections),
        [((264, 128), F32)],
        9,
        [
            pltpu.VMEM((3, 1, 128), jnp.int32),
            pltpu.VMEM((1, 32), F32),
            pltpu.VMEM((2, 32, 128), jnp.int32),
            dma((12,)),
        ],
        hbm=9,
        grant=60,
    )(
        ov_first.reshape(1, 128),
        ov_second.reshape(1, 128),
        match_count.reshape(1, 128),
        cell_first,
        cell_second,
        frac_first,
        frac_second,
        target,
        stiffness.reshape(1, 32),
    )[0]
    far = [dealt(packed, step) for step in (3, 2, 1, 0)]
    field = ((64, 256), F32)
    bf16 = jnp.bfloat16
    groups = []
    sums = ()
    for k, blocks in enumerate(BLOCKS):
        if k == 0:
            datas = far[:2]
            near = [swapped(x) for x in datas]
        elif k == 1:
            late, sums = lax.optimization_barrier((far[2:], sums))
            datas = near + late
            near = [swapped(x) for x in late]
        else:
            datas = near
        outs = call(
            functools.partial(tables_kernel, blocks=blocks, add=len(sums) > 0),
            [
                ((blocks, 2, 8, 32, 128), F32),
                ((blocks, 2, 8, 32, 128), F32),
                ((blocks, 2, 32, 128), F32),
                ((blocks, 2, 32, 128), jnp.int32),
                ((blocks, 32, 128), F32),
                ((256, 128 * blocks), bf16),
                ((512, 128 * blocks), bf16),
                field,
                field,
                ((1, 256), F32),
            ],
            blocks + len(sums),
            us=0.4 * blocks,
        )(*datas, *sums)
        groups.append(outs[:7])
        sums = tuple(outs[7:])
    own, down, stiff = sums
    parts = [x for g in groups for x in (g[0], g[1], g[4], g[6])]
    above = shifted(down, -1)
    raw = shifted(own, 1)
    send, keep = call(stencil_kernel, [((2, 64, 256), F32)] * 2, len(parts), us=4.0)(*parts)
    above, send = lax.optimization_barrier((above, send))
    got = shifted(send, -1)
    fields = [own - above]
    tables = []
    for wx, wy, fx, col, live, ohf, ohs in groups:
        tables += [ohf, ohs, wx, wy, fx, col, live]
    for k in range(ITERS):
        v = fields[-1]
        sent = down
        part, down, gap = call(up_kernel, [field, field, ((8, 32, 128), F32)], 1 + len(tables))(v, *tables)
        above = shifted(down, -1)
        more = (fields[k - 1], mine, other) if k else ()
        partial = call(functools.partial(down_kernel, back=k > 0), [field], 6 + len(more) + len(tables))(
            v, raw, sent, part, gap, stiff, *more, *tables
        )[0]
        if k == 0:
            mine = keep + got
            other = swapped(mine)
            partial = call(band_kernel, [field], 4, us=0.3)(partial, v, mine, other)[0]
        if k < ITERS - 1:
            raw = shifted(partial, 1)
        fields.append(partial - above)
    row = call(dots_kernel, [((1, 128), F32)], 4, us=1.0)(*fields[:4])[0]
    row, slices = call(last_kernel, [((1, 128), F32), ((3, 64, 128), F32)], 6, us=1.0)(row, *fields)
    slices = returned(slices)
    row = row + jnp.roll(swapped(row), 32, 1)
    gram = lax.all_to_all(jnp.broadcast_to(row, (32, 128)), "sec", 0, 0, tiled=True)
    mine, other = call(finish_kernel, [((2, 32, 64), F32), ((2, 32, 64), F32)], 2)(gram, slices)
    other = swapped(other)
    first = jnp.where(core == 0, mine, other)
    last = jnp.where(core == 0, other, mine)
    out = jnp.concatenate([first, last], 2)[:, :, None, :]
    return (out[0], out[1])


def solution(mesh):
    in_specs = (
        P(("sec", "tile")),
        P(("sec", "tile")),
        P(("sec", "tile")),
        P(None, ("sec", "tile")),
        P(None, ("sec", "tile")),
        P(None, None, ("sec", "tile")),
        P(None, None, ("sec", "tile")),
        P(None, None, ("sec", "tile")),
        P("tile", "sec"),
    )
    out_specs = (P("tile", "sec", None), P("tile", "sec", None))
    return jax.shard_map(
        on_device, mesh=mesh, in_specs=in_specs, out_specs=out_specs, check_vma=False
    )
```

```python
import functools

import jax
import jax.numpy as jnp
from jax import lax
from jax.experimental import pallas as pl
from jax.experimental.pallas import tpu as pltpu
from jax.sharding import PartitionSpec as P

ITERS = 4
DAMPING = 0.5
SHIFT = 10.0
SCALE = 1.0 / 128.0
BACK = 25.0 / 16384.0
PAIRS = [(i, j) for i in range(5) for j in range(i, 5) if (i, j) != (4, 4)]
VMEM = pl.BlockSpec(memory_space=pltpu.VMEM)
F32 = jnp.float32
NT = (((1,), (1,)), ((), ()))


def split3(x):
    a = x.astype(jnp.bfloat16)
    rest = x - a.astype(F32)
    b = rest.astype(jnp.bfloat16)
    c = (rest - b.astype(F32)).astype(jnp.bfloat16)
    return jnp.concatenate([a, b, c], 0)


def merge3(x):
    n = x.shape[0] // 3
    return x[:n] + (x[n : 2 * n] + x[2 * n :])


def sublane_ids():
    return lax.broadcasted_iota(jnp.int32, (8, 128), 0)


def fold_rows(parts):
    sub = sublane_ids()
    low = sub < 4
    half = [
        jnp.where(low, parts[p], parts[p + 4])
        + pltpu.roll(jnp.where(low, parts[p + 4], parts[p]), 4, 0)
        for p in range(4)
    ]
    two = (sub & 2) != 0
    quarter = [
        jnp.where(two, half[p + 2] + pltpu.roll(half[p + 2], 2, 0), half[p] + pltpu.roll(half[p], 6, 0))
        for p in range(2)
    ]
    one = (sub & 1) != 0
    return jnp.where(
        one, quarter[1] + pltpu.roll(quarter[1], 1, 0), quarter[0] + pltpu.roll(quarter[0], 7, 0)
    )


def spread_rows(tops, sides):
    rows = []
    for q in range(8):
        parts = []
        for p in range(8):
            acc = tops[q][0] * sides[p][0]
            for group in range(1, 4):
                acc = acc + tops[q][group] * sides[p][group]
            parts.append(acc)
        rows.append(fold_rows(parts))
    return jnp.concatenate(rows, 0)


def sample_block(rows, wy_ref, fx_ref, col_ref, blk, side):
    out = []
    for group in range(4):
        ms = slice(8 * group, 8 * group + 8)
        col = col_ref[blk, side, ms, :]
        nxt = col + 1
        fx = fx_ref[blk, side, ms, :]
        acc = None
        for q in range(8):
            row = rows[8 * q : 8 * q + 8]
            left = jnp.take_along_axis(row, col, axis=0, mode="promise_in_bounds")
            right = jnp.take_along_axis(row, nxt, axis=0, mode="promise_in_bounds")
            term = wy_ref[blk, side, q, ms, :] * (left + fx * (right - left))
            acc = term if acc is None else acc + term
        out.append(acc)
    return out


def load_table(ref, blk, side):
    return [[ref[blk, side, p, 8 * g : 8 * g + 8, :] for g in range(4)] for p in range(8)]


def lanes_of(blk):
    return pl.ds(pl.multiple_of(blk * 128, 128), 128)


def pack_kernel(
    first_hbm, second_hbm, count_hbm, cell1_hbm, cell2_hbm, frac1_hbm, frac2_hbm, target_hbm, stiff_hbm,
    out_ref, ids_ref, stiff_ref, cell_ref, sem, *, sections
):
    copies = [
        pltpu.make_async_copy(cell1_hbm, cell_ref.at[0], sem.at[0]),
        pltpu.make_async_copy(cell2_hbm, cell_ref.at[1], sem.at[1]),
        pltpu.make_async_copy(first_hbm, ids_ref.at[0], sem.at[2]),
        pltpu.make_async_copy(second_hbm, ids_ref.at[1], sem.at[3]),
        pltpu.make_async_copy(count_hbm, ids_ref.at[2], sem.at[4]),
        pltpu.make_async_copy(stiff_hbm, stiff_ref, sem.at[5]),
    ]
    for k, src in enumerate((frac1_hbm, frac2_hbm, target_hbm)):
        for c in range(2):
            at = 64 + 64 * k + 32 * c
            copies.append(pltpu.make_async_copy(src.at[c], out_ref.at[at : at + 32, :], sem.at[6 + 2 * k + c]))
    for copy in copies:
        copy.start()
    for copy in copies:
        copy.wait()
    out_ref[0:32, :] = cell_ref[0].astype(F32)
    out_ref[32:64, :] = cell_ref[1].astype(F32)
    shift = sections.bit_length() - 1
    first = ids_ref[0] >> shift
    second = ids_ref[1] >> shift
    second = second + jnp.where((ids_ref[1] & (sections - 1)) == lax.axis_index("sec"), 0, 256)
    tile = lax.axis_index("tile")
    stiff = jnp.concatenate([stiff_ref[...], jnp.zeros((1, 96), F32)], 1)
    stiff = pltpu.roll(jnp.broadcast_to(stiff, (8, 128)), 32 * (tile & 3), 1)
    row = sublane_ids()
    tail = jnp.where((row >= 3) & (row - 3 == (tile >> 2)), stiff, 0.0)
    for k, x in enumerate((first, second, ids_ref[2])):
        tail = jnp.where(row == k, jnp.broadcast_to(x.astype(F32), (8, 128)), tail)
    out_ref[256:264, :] = tail


def tables_kernel(*refs, blocks, add):
    datas = refs[:blocks]
    refs = refs[blocks:]
    if add:
        before_own, before_down, before_stiff = refs[:3]
        refs = refs[3:]
    wx_ref, wy_ref, fx_ref, col_ref, live_ref, ohf_ref, ohs_ref, own_ref, down_ref, stiff_ref = refs
    comp = lax.axis_index("tile") & 1
    columns = [[], []]
    for blk, data_ref in enumerate(datas):
        lanes = slice(128 * blk, 128 * blk + 128)
        count = data_ref[258, :][None, :]
        goal = []
        for group in range(4):
            ms = slice(8 * group, 8 * group + 8)
            slot = (sublane_ids() + 8 * group).astype(F32)
            live = slot < count
            live_ref[blk, ms, :] = jnp.where(live, SCALE, 0.0)
            at = pl.multiple_of(192 + 32 * comp + 8 * group, 8)
            goal.append(jnp.where(live, data_ref[pl.ds(at, 8), :], 0.0))
        first = data_ref[256, :][None, :].astype(jnp.int32)
        second = data_ref[257, :][None, :].astype(jnp.int32)
        ids = lax.broadcasted_iota(jnp.int32, (256, 128), 0)
        ohf_ref[:, lanes] = jnp.where(ids == first, 1.0, 0.0).astype(jnp.bfloat16)
        ohs_ref[0:256, lanes] = jnp.where(ids == second, 1.0, 0.0).astype(jnp.bfloat16)
        ohs_ref[256:512, lanes] = jnp.where(ids + 256 == second, 1.0, 0.0).astype(jnp.bfloat16)
        for side in range(2):
            for group in range(4):
                ms = slice(8 * group, 8 * group + 8)
                at = 32 * side + 8 * group
                cell = data_ref[at : at + 8, :].astype(jnp.int32)
                base = 64 + 64 * side + 8 * group
                fx = data_ref[base : base + 8, :]
                fy = data_ref[base + 32 : base + 40, :]
                row = (cell * 37) >> 8
                col = cell - 7 * row
                fx_ref[blk, side, ms, :] = fx
                col_ref[blk, side, ms, :] = col
                for k in range(8):
                    wx_ref[blk, side, k, ms, :] = jnp.where(
                        col == k, 1.0 - fx, jnp.where(col == k - 1, fx, 0.0)
                    )
                    wy_ref[blk, side, k, ms, :] = jnp.where(
                        row == k, 1.0 - fy, jnp.where(row == k - 1, fy, 0.0)
                    )
            tops = load_table(wy_ref, blk, side)
            tops = [[tops[q][g] * goal[g] for g in range(4)] for q in range(8)]
            columns[side].append(spread_rows(tops, load_table(wx_ref, blk, side)))
    spreads = [jnp.concatenate(c, 1) for c in columns]
    at_first = merge3(lax.dot_general(split3(spreads[0]), ohf_ref[...], NT, preferred_element_type=F32))
    at_second = merge3(lax.dot_general(split3(spreads[1]), ohs_ref[...], NT, preferred_element_type=F32))
    own = at_first - at_second[:, :256]
    down = at_second[:, 256:]
    stiff = jnp.concatenate(
        [sum(data_ref[row : row + 1, :] for data_ref in datas) for row in (259, 260)], 1
    )
    if add:
        own = own + before_own[...]
        down = down + before_down[...]
        stiff = stiff + before_stiff[...]
    own_ref[...] = own
    down_ref[...] = down
    stiff_ref[...] = stiff


def stencil_kernel(*refs):
    step = lax.axis_index("tile") & 1
    send_ref, keep_ref = refs[4 * len(BLOCKS) :]
    zero = [jnp.zeros((8, 128), F32)] * 4
    terms = [[], []]
    for h, blocks in enumerate(BLOCKS):
        wx_ref, wy_ref, live_ref = refs[4 * h : 4 * h + 3]
        columns = [[], []]
        for blk in range(blocks):
            live = [live_ref[blk, 8 * g : 8 * g + 8, :] for g in range(4)]
            wy = load_table(wy_ref, blk, 1) + [zero]
            tops = [
                [wy[q][g] * jnp.where(step == 0, wy[q][g], wy[q + 1][g]) * live[g] for g in range(4)]
                for q in range(8)
            ]
            wx = load_table(wx_ref, blk, 1) + [zero]
            for kind in range(2):
                sides = [[wx[p][g] * wx[p + kind][g] for g in range(4)] for p in range(8)]
                columns[kind].append(spread_rows(tops, sides))
        for kind in range(2):
            terms[kind].append(split3(jnp.concatenate(columns[kind], 1)))
    for kind in range(2):
        both = scatter(terms[kind], refs[3 : 4 * len(BLOCKS) : 4])
        keep_ref[kind] = both[:, :256]
        send_ref[kind] = both[:, 256:]


def scatter(terms, hots):
    total = None
    for parts, hot in zip(terms, hots):
        term = lax.dot_general(parts, hot[...], NT, preferred_element_type=F32)
        total = term if total is None else total + term
    return merge3(total)


BLOCKS = (2, 4, 2)
AT = (0, 2, 6)


def passed(parts, hot_in, hot_out, tables, side_in, side_out, scale):
    terms = []
    for h, blocks in enumerate(BLOCKS):
        wx_ref, wy_ref, fx_ref, col_ref = tables[h][2:6]
        columns = []
        for start in range(0, blocks, 2):
            stop = min(start + 2, blocks)
            rows = merge3(jnp.dot(parts, hot_in[h][:, 128 * start : 128 * stop], preferred_element_type=F32))
            for blk in range(start, stop):
                at = 128 * (blk - start)
                got = sample_block(rows[:, at : at + 128], wy_ref, fx_ref, col_ref, blk, side_in)
                gap = scale(h, blk, got)
                tops = load_table(wy_ref, blk, side_out)
                tops = [[tops[q][g] * gap[g] for g in range(4)] for q in range(8)]
                columns.append(spread_rows(tops, load_table(wx_ref, blk, side_out)))
        terms.append(split3(jnp.concatenate(columns, 1)))
    return scatter(terms, hot_out)


def up_kernel(v_ref, *refs):
    tables = [refs[7 * h : 7 * h + 7] for h in range(len(BLOCKS))]
    own_ref, down_ref, gap_ref = refs[7 * len(BLOCKS) :]

    def scale(h, blk, got):
        gap = []
        for g in range(4):
            ms = slice(8 * g, 8 * g + 8)
            gap.append(got[g] * tables[h][6][blk, ms, :])
            gap_ref[blk + AT[h], ms, :] = gap[g]
        return gap

    forces = passed(split3(v_ref[...]), [t[0] for t in tables], [t[1] for t in tables], tables, 0, 1, scale)
    own_ref[...] = forces[:, :256]
    down_ref[...] = forces[:, 256:]


def up(x, d):
    return pltpu.roll(x, 64 - d, 0)


def dn(x, d):
    return pltpu.roll(x, d, 0)


def banded(v, mine_ref, other_ref):
    first = (lax.axis_index("tile") & 1) == 0
    band = [jnp.where(first, mine_ref[k], other_ref[k]) for k in range(2)]
    band += [jnp.where(first, other_ref[k], mine_ref[k]) for k in range(2)]
    total = band[0] * v
    total = total + band[1] * up(v, 1) + dn(band[1] * v, 1)
    total = total + band[2] * up(v, 8) + dn(band[2] * v, 8)
    total = total + band[3] * up(v, 9) + dn(band[3] * v, 9)
    return total + dn(band[3] * up(v, 8), 1) + dn(band[3] * up(v, 1), 8)


def band_kernel(part_ref, v_ref, mine_ref, other_ref, out_ref):
    out_ref[...] = part_ref[...] + banded(v_ref[...], mine_ref, other_ref)


def down_kernel(
    v_ref, raw_ref, sent_ref, part_ref, gap_ref, stiff_ref, *refs, back
):
    if back:
        prev_ref, mine_ref, other_ref = refs[:3]
        refs = refs[3:]
    tables = [refs[7 * h : 7 * h + 7] for h in range(len(BLOCKS))]
    (out_ref,) = refs[7 * len(BLOCKS) :]
    v = v_ref[...]
    parts = jnp.concatenate([split3(v), split3(raw_ref[...] - sent_ref[...])], 1)

    def scale(h, blk, got):
        return [
            gap_ref[blk + AT[h], 8 * g : 8 * g + 8, :] - got[g] * tables[h][6][blk, 8 * g : 8 * g + 8, :]
            for g in range(4)
        ]

    forces = passed(parts, [t[1] for t in tables], [t[0] for t in tables], tables, 1, 0, scale)
    node = lax.broadcasted_iota(jnp.int32, (64, 256), 0)
    right = jnp.where((node & 7) < 7, up(v, 1) - v, 0.0)
    below = jnp.where(node < 56, up(v, 8) - v, 0.0)
    bend = (dn(right, 1) - right) + (dn(below, 8) - below)
    total = forces - part_ref[...] + (stiff_ref[...] * SCALE) * bend + ((DAMPING - SHIFT) * SCALE) * v
    if back:
        total = total + banded(v, mine_ref, other_ref)
        total = total - BACK * prev_ref[...]
    out_ref[...] = total


def two_sum(a, b):
    s = a + b
    t = s - a
    return s, (a - (s - t)) + (b - t)


def halves(a):
    c = 4097.0 * a
    high = c - (c - a)
    return high, a - high


def two_prod(a, b):
    return split_prod(a, b, halves(a), halves(b))


def split_prod(a, b, a_halves, b_halves):
    p = a * b
    ah, al = a_halves
    bh, bl = b_halves
    return p, ((ah * bh - p) + ah * bl + al * bh) + al * bl


def quick(a, b):
    s = a + b
    return s, b - (s - a)


def dd_add(x, y):
    s, e = two_sum(x[0], y[0])
    return quick(s, e + (x[1] + y[1]))


def dd_mul(x, y):
    p, e = two_prod(x[0], y[0])
    return quick(p, e + (x[0] * y[1] + x[1] * y[0]))


def dd_neg(x):
    return (-x[0], -x[1])


def dd_div(x, y):
    q = x[0] / y[0]
    rest = dd_add(x, dd_neg(dd_mul(y, (q, jnp.zeros_like(q)))))
    return quick(q, rest[0] / y[0])


def dots(fields, pairs):
    sub = lax.broadcasted_iota(jnp.int32, (16, 128), 0)
    lane = lax.broadcasted_iota(jnp.int32, (16, 128), 1)
    high = jnp.zeros((16, 128), F32)
    low = jnp.zeros((16, 128), F32)
    cut = [halves(f) for f in fields]
    for i, j in pairs:
        acc = split_prod(fields[i], fields[j], cut[i], cut[j])
        acc = dd_add((acc[0][:, :128], acc[1][:, :128]), (acc[0][:, 128:], acc[1][:, 128:]))
        n = 64
        while n > 8:
            n //= 2
            acc = dd_add((acc[0][:n], acc[1][:n]), (acc[0][n:], acc[1][n:]))
        for d in (4, 2, 1):
            acc = dd_add(acc, (pltpu.roll(acc[0], d, 0), pltpu.roll(acc[1], d, 0)))
        wide = [jnp.concatenate([a, a], 0) for a in acc]
        here = sub == PAIRS.index((i, j))
        high = jnp.where(here, wide[0], high)
        low = jnp.where(here, wide[1], low)
    acc = (high, low)
    for d in (64, 32, 16, 8, 4, 2, 1):
        acc = dd_add(acc, (pltpu.roll(acc[0], d, 1), pltpu.roll(acc[1], d, 1)))
    row = jnp.where(lane == sub, acc[0], 0.0) + jnp.where(lane == sub + 16, acc[1], 0.0)
    return jnp.sum(row, 0, keepdims=True)


def dots_kernel(v0, v1, v2, v3, out_ref):
    out_ref[...] = dots([r[...] for r in (v0, v1, v2, v3)], [p for p in PAIRS if p[1] < 4])


def slice_kernel(v0, v1, v2, v3, v4, even_ref, odd_ref):
    fields = [r[...] for r in (v0, v1, v2, v3, v4)]
    y = lax.axis_index("tile") >> 1
    low = lax.broadcasted_iota(jnp.int32, (64, 128), 1) < 64
    for k in range(3):
        left = jnp.where(y >= 2, fields[2 * k][:, 128:], fields[2 * k][:, :128])
        if k < 2:
            right = jnp.where(y >= 2, fields[2 * k + 1][:, 128:], fields[2 * k + 1][:, :128])
        else:
            right = jnp.zeros((64, 128), F32)
        even_ref[k] = jnp.where(low, left, pltpu.roll(right, 64, 1))
        odd_ref[k] = jnp.where(low, pltpu.roll(left, 64, 1), right)


def last_kernel(row_ref, v0, v1, v2, v3, v4, out_ref):
    out_ref[...] = row_ref[...] + dots([r[...] for r in (v0, v1, v2, v3, v4)], [p for p in PAIRS if p[1] == 4])


def finish_kernel(gram_ref, even_ref, odd_ref, mine_ref, other_ref):
    rows = gram_ref[...]
    acc = dd_add((rows, pltpu.roll(rows, 112, 1)), (pltpu.roll(rows, 96, 1), pltpu.roll(rows, 80, 1)))
    n = 32
    while n > 8:
        n //= 2
        acc = dd_add((acc[0][:n], acc[1][:n]), (acc[0][n:], acc[1][n:]))
    for d in (4, 2, 1):
        acc = dd_add(acc, (pltpu.roll(acc[0], d, 0), pltpu.roll(acc[1], d, 0)))
    gram = {}
    for k, (i, j) in enumerate(PAIRS):
        pair = tuple(jnp.broadcast_to(a[:, k : k + 1], (8, 128)) for a in acc)
        gram[(i, j)] = pair
        gram[(j, i)] = pair
    zero = jnp.zeros((8, 128), F32)
    const = lambda c: (jnp.full((8, 128), c, F32), zero)

    def tree(terms):
        while len(terms) > 1:
            terms = [dd_add(*terms[k : k + 2]) if k + 1 < len(terms) else terms[k] for k in range(0, len(terms), 2)]
        return terms[0]

    def form(a, b):
        return tree([dd_mul(bj, tree([dd_mul(ai, gram[(i, j)]) for i, ai in enumerate(a)])) for j, bj in enumerate(b)])

    def apply(p):
        out = [const(0.0) for _ in range(len(p) + 1)]
        for k, c in enumerate(p):
            out[k + 1] = dd_add(out[k + 1], (c[0] * 128.0, c[1] * 128.0))
            out[k] = dd_add(out[k], dd_mul(c, const(SHIFT)))
            if k >= 1:
                out[k - 1] = dd_add(out[k - 1], dd_mul(c, const(BACK * 128.0)))
        return out

    def axpy(a, x, y):
        out = []
        for k in range(max(len(x), len(y))):
            if k >= len(x):
                out.append(y[k])
            elif k >= len(y):
                out.append(dd_mul(a, x[k]))
            else:
                out.append(dd_add(y[k], dd_mul(a, x[k])))
        return out

    res = [const(1.0)]
    direc = [const(1.0)]
    sol = []
    norm = gram[(0, 0)]
    for it in range(ITERS):
        image = apply(direc)
        step = dd_div(norm, form(direc, image))
        sol = axpy(step, direc, sol)
        res = axpy(dd_neg(step), image, res)
        if it < ITERS - 1:
            new = form(res, res)
            direc = axpy(dd_div(new, norm), direc, res)
            norm = new
    lane = lax.broadcasted_iota(jnp.int32, (64, 128), 1)

    odd = ((lax.axis_index("tile") >> 1) & 1) == 1

    def combine(coefs):
        total = jnp.zeros((64, 128), F32)
        flat = [c[0][0:1, 0:1] for c in coefs] + [jnp.zeros((1, 1), F32)] * (6 - len(coefs))
        for k in range(3):
            total = total + jnp.where(lane < 64, flat[2 * k], flat[2 * k + 1]) * jnp.where(odd, odd_ref[k], even_ref[k])
        return total + pltpu.roll(total, 64, 1)

    core = lax.axis_index("tile") & 1
    want = lax.broadcasted_iota(jnp.int32, (64, 128), 0)
    want = jnp.where(want < 32, want + 32 * core, want - 32 * core)
    pick = jnp.where(lane == want, 1.0, 0.0).astype(jnp.bfloat16)
    for k, coefs in enumerate((sol, res)):
        parts = lax.dot_general(pick, split3(combine(coefs)), NT, preferred_element_type=F32)
        both = parts[:, :64] + (parts[:, 64:128] + parts[:, 128:192])
        mine_ref[k] = both[:32]
        other_ref[k] = both[32:]


def call(kernel, outs, n_in, scratch=(), us=2.0, hbm=0, grant=8):
    return pl.pallas_call(
        kernel,
        out_shape=[jax.ShapeDtypeStruct(s, d) for s, d in outs],
        in_specs=[VMEM] * (n_in - hbm)
        + [pl.BlockSpec(memory_space=pl.ANY)] * hbm,
        out_specs=[VMEM] * len(outs),
        scratch_shapes=list(scratch),
        compiler_params=pltpu.CompilerParams(vmem_limit_bytes=grant * 1024 * 1024),
        cost_estimate=pl.CostEstimate(flops=int(us * 1e9), bytes_accessed=1 << 18, transcendentals=0),
    )


ROW = 4
CHIPS = 4


def seat(section, y, sections):
    row, col = divmod(section, ROW)
    col = col if row % 2 == 0 else ROW - 1 - col
    row = row if y % 2 == 0 else sections // ROW - 1 - row
    return row * ROW + col


def shifted(block, distance):
    sections = lax.axis_size("sec")
    route = []
    for section in range(sections):
        there = (section + distance) % sections
        crosses = (section < sections // 2) != (there < sections // 2)
        for y in range(CHIPS):
            to = y ^ 1 if crosses else y
            for core in range(2):
                route.append(
                    (seat(section, y, sections) * 8 + 2 * y + core, seat(there, to, sections) * 8 + 2 * to + core)
                )
    return lax.ppermute(block, ("sec", "tile"), route)


def swapped(block):
    return lax.ppermute(block, "tile", [(i, i ^ 1) for i in range(8)])


def dealt(block, step):
    sections = lax.axis_size("sec")
    route = []
    for section in range(sections):
        for y in range(CHIPS):
            to = (y + step) % CHIPS
            for core in range(2):
                route.append((section * 8 + 2 * y + core, seat(section, to, sections) * 8 + 2 * to + core))
    return lax.ppermute(block, ("sec", "tile"), route)


def returned(block, up):
    sections = lax.axis_size("sec")
    route = []
    for section in range(sections):
        for y in range(CHIPS):
            for core in range(2):
                if y % 2 == 0:
                    route.append((seat(section, y, sections) * 8 + 2 * y + core, section * 8 + 2 * (y + up) + core))
                else:
                    route.append((section * 8 + 2 * y + core, section * 8 + 2 * (y - up) + core))
    return lax.ppermute(block, ("sec", "tile"), route)


def on_device(
    ov_first, ov_second, match_count, cell_first, cell_second, frac_first, frac_second, target, stiffness
):
    tile = lax.axis_index("tile")
    core = tile % 2
    sections = lax.axis_size("sec")
    dma = pltpu.SemaphoreType.DMA
    packed = call(
        functools.partial(pack_kernel, sections=sections),
        [((264, 128), F32)],
        9,
        [
            pltpu.VMEM((3, 1, 128), jnp.int32),
            pltpu.VMEM((1, 32), F32),
            pltpu.VMEM((2, 32, 128), jnp.int32),
            dma((12,)),
        ],
        hbm=9,
        grant=60,
    )(
        ov_first.reshape(1, 128),
        ov_second.reshape(1, 128),
        match_count.reshape(1, 128),
        cell_first,
        cell_second,
        frac_first,
        frac_second,
        target,
        stiffness.reshape(1, 32),
    )[0]
    far = [dealt(packed, step) for step in (3, 2, 1, 0)]
    field = ((64, 256), F32)
    bf16 = jnp.bfloat16
    groups = []
    sums = ()
    for k, blocks in enumerate(BLOCKS):
        if k == 0:
            datas = far[:2]
            near = [swapped(x) for x in datas]
        elif k == 1:
            late, sums = lax.optimization_barrier((far[2:], sums))
            datas = near + late
            near = [swapped(x) for x in late]
        else:
            datas = near
        outs = call(
            functools.partial(tables_kernel, blocks=blocks, add=len(sums) > 0),
            [
                ((blocks, 2, 8, 32, 128), F32),
                ((blocks, 2, 8, 32, 128), F32),
                ((blocks, 2, 32, 128), F32),
                ((blocks, 2, 32, 128), jnp.int32),
                ((blocks, 32, 128), F32),
                ((256, 128 * blocks), bf16),
                ((512, 128 * blocks), bf16),
                field,
                field,
                ((1, 256), F32),
            ],
            blocks + len(sums),
            us=0.4 * blocks,
        )(*datas, *sums)
        groups.append(outs[:7])
        sums = tuple(outs[7:])
    own, down, stiff = sums
    parts = [x for g in groups for x in (g[0], g[1], g[4], g[6])]
    above = shifted(down, -1)
    raw = shifted(own, 1)
    send, keep = call(stencil_kernel, [((2, 64, 256), F32)] * 2, len(parts), us=4.0)(*parts)
    above, send = lax.optimization_barrier((above, send))
    got = shifted(send, -1)
    fields = [own - above]
    tables = []
    for wx, wy, fx, col, live, ohf, ohs in groups:
        tables += [ohf, ohs, wx, wy, fx, col, live]
    for k in range(ITERS):
        v = fields[-1]
        sent = down
        part, down, gap = call(up_kernel, [field, field, ((8, 32, 128), F32)], 1 + len(tables))(v, *tables)
        above = shifted(down, -1)
        more = (fields[k - 1], mine, other) if k else ()
        partial = call(functools.partial(down_kernel, back=k > 0), [field], 6 + len(more) + len(tables))(
            v, raw, sent, part, gap, stiff, *more, *tables
        )[0]
        if k == 0:
            mine = keep + got
            other = swapped(mine)
            partial = call(band_kernel, [field], 4, us=0.3)(partial, v, mine, other)[0]
        if k < ITERS - 1:
            raw = shifted(partial, 1)
        fields.append(partial - above)
    row = call(dots_kernel, [((1, 128), F32)], 4, us=1.0)(*fields[:4])[0]
    even, odd = call(slice_kernel, [((3, 64, 128), F32)] * 2, 5, us=0.1)(*fields)
    even = returned(even, 0)
    odd = returned(odd, 1)
    row = call(last_kernel, [((1, 128), F32)], 6, us=1.0)(row, *fields)[0]
    row = row + jnp.roll(swapped(row), 32, 1)
    gram = lax.all_to_all(jnp.broadcast_to(row, (32, 128)), "sec", 0, 0, tiled=True)
    mine, other = call(finish_kernel, [((2, 32, 64), F32), ((2, 32, 64), F32)], 3)(gram, even, odd)
    other = swapped(other)
    first = jnp.where(core == 0, mine, other)
    last = jnp.where(core == 0, other, mine)
    out = jnp.concatenate([first, last], 2)[:, :, None, :]
    return (out[0], out[1])


def solution(mesh):
    in_specs = (
        P(("sec", "tile")),
        P(("sec", "tile")),
        P(("sec", "tile")),
        P(None, ("sec", "tile")),
        P(None, ("sec", "tile")),
        P(None, None, ("sec", "tile")),
        P(None, None, ("sec", "tile")),
        P(None, None, ("sec", "tile")),
        P("tile", "sec"),
    )
    out_specs = (P("tile", "sec", None), P("tile", "sec", None))
    return jax.shard_map(
        on_device, mesh=mesh, in_specs=in_specs, out_specs=out_specs, check_vma=False
    )
```

```python
import functools

import jax
import jax.numpy as jnp
from jax import lax
from jax.experimental import pallas as pl
from jax.experimental.pallas import tpu as pltpu
from jax.sharding import PartitionSpec as P

ITERS = 4
DAMPING = 0.5
SHIFT = 10.0
SCALE = 1.0 / 128.0
BACK = 25.0 / 16384.0
PAIRS = [(i, j) for i in range(5) for j in range(i, 5) if (i, j) != (4, 4)]
VMEM = pl.BlockSpec(memory_space=pltpu.VMEM)
F32 = jnp.float32
NT = (((1,), (1,)), ((), ()))


def split3(x):
    a = x.astype(jnp.bfloat16)
    rest = x - a.astype(F32)
    b = rest.astype(jnp.bfloat16)
    c = (rest - b.astype(F32)).astype(jnp.bfloat16)
    return jnp.concatenate([a, b, c], 0)


def merge3(x):
    n = x.shape[0] // 3
    return x[:n] + (x[n : 2 * n] + x[2 * n :])


def sublane_ids():
    return lax.broadcasted_iota(jnp.int32, (8, 128), 0)


def fold_rows(parts):
    sub = sublane_ids()
    low = sub < 4
    half = [
        jnp.where(low, parts[p], parts[p + 4])
        + pltpu.roll(jnp.where(low, parts[p + 4], parts[p]), 4, 0)
        for p in range(4)
    ]
    two = (sub & 2) != 0
    quarter = [
        jnp.where(two, half[p + 2] + pltpu.roll(half[p + 2], 2, 0), half[p] + pltpu.roll(half[p], 6, 0))
        for p in range(2)
    ]
    one = (sub & 1) != 0
    return jnp.where(
        one, quarter[1] + pltpu.roll(quarter[1], 1, 0), quarter[0] + pltpu.roll(quarter[0], 7, 0)
    )


def spread_rows(tops, sides):
    rows = []
    for q in range(8):
        parts = []
        for p in range(8):
            acc = tops[q][0] * sides[p][0]
            for group in range(1, 4):
                acc = acc + tops[q][group] * sides[p][group]
            parts.append(acc)
        rows.append(fold_rows(parts))
    return jnp.concatenate(rows, 0)


def sample_block(rows, wy_ref, fx_ref, col_ref, blk, side):
    out = []
    for group in range(4):
        ms = slice(8 * group, 8 * group + 8)
        col = col_ref[blk, side, ms, :]
        nxt = col + 1
        fx = fx_ref[blk, side, ms, :]
        acc = None
        for q in range(8):
            row = rows[q]
            left = jnp.take_along_axis(row, col, axis=0, mode="promise_in_bounds")
            right = jnp.take_along_axis(row, nxt, axis=0, mode="promise_in_bounds")
            term = wy_ref[blk, side, q, ms, :] * (left + fx * (right - left))
            acc = term if acc is None else acc + term
        out.append(acc)
    return out


def load_table(ref, blk, side):
    return [[ref[blk, side, p, 8 * g : 8 * g + 8, :] for g in range(4)] for p in range(8)]


def lanes_of(blk):
    return pl.ds(pl.multiple_of(blk * 128, 128), 128)


def pack_kernel(
    first_hbm, second_hbm, count_hbm, cell1_hbm, cell2_hbm, frac1_hbm, frac2_hbm, target_hbm, stiff_hbm,
    out_ref, ids_ref, stiff_ref, cell_ref, sem, *, sections
):
    copies = [
        pltpu.make_async_copy(cell1_hbm, cell_ref.at[0], sem.at[0]),
        pltpu.make_async_copy(cell2_hbm, cell_ref.at[1], sem.at[1]),
        pltpu.make_async_copy(first_hbm, ids_ref.at[0], sem.at[2]),
        pltpu.make_async_copy(second_hbm, ids_ref.at[1], sem.at[3]),
        pltpu.make_async_copy(count_hbm, ids_ref.at[2], sem.at[4]),
        pltpu.make_async_copy(stiff_hbm, stiff_ref, sem.at[5]),
    ]
    for k, src in enumerate((frac1_hbm, frac2_hbm, target_hbm)):
        for c in range(2):
            at = 64 + 64 * k + 32 * c
            copies.append(pltpu.make_async_copy(src.at[c], out_ref.at[at : at + 32, :], sem.at[6 + 2 * k + c]))
    for copy in copies:
        copy.start()
    for copy in copies:
        copy.wait()
    out_ref[0:32, :] = cell_ref[0].astype(F32)
    out_ref[32:64, :] = cell_ref[1].astype(F32)
    shift = sections.bit_length() - 1
    first = ids_ref[0] >> shift
    second = ids_ref[1] >> shift
    second = second + jnp.where((ids_ref[1] & (sections - 1)) == lax.axis_index("sec"), 0, 256)
    tile = lax.axis_index("tile")
    stiff = jnp.concatenate([stiff_ref[...], jnp.zeros((1, 96), F32)], 1)
    stiff = pltpu.roll(jnp.broadcast_to(stiff, (8, 128)), 32 * (tile & 3), 1)
    row = sublane_ids()
    tail = jnp.where((row >= 3) & (row - 3 == (tile >> 2)), stiff, 0.0)
    for k, x in enumerate((first, second, ids_ref[2])):
        tail = jnp.where(row == k, jnp.broadcast_to(x.astype(F32), (8, 128)), tail)
    out_ref[256:264, :] = tail


def tables_kernel(*refs, blocks, add):
    datas = refs[:blocks]
    refs = refs[blocks:]
    if add:
        before_own, before_down, before_stiff = refs[:3]
        refs = refs[3:]
    wx_ref, wy_ref, fx_ref, col_ref, live_ref, ohf_ref, ohs_ref, ids_ref, own_ref, down_ref, stiff_ref = refs
    comp = lax.axis_index("tile") & 1
    columns = [[], []]
    for blk, data_ref in enumerate(datas):
        lanes = slice(128 * blk, 128 * blk + 128)
        count = data_ref[258, :][None, :]
        goal = []
        for group in range(4):
            ms = slice(8 * group, 8 * group + 8)
            slot = (sublane_ids() + 8 * group).astype(F32)
            live = slot < count
            live_ref[blk, ms, :] = jnp.where(live, SCALE, 0.0)
            at = pl.multiple_of(192 + 32 * comp + 8 * group, 8)
            goal.append(jnp.where(live, data_ref[pl.ds(at, 8), :], 0.0))
        first = data_ref[256, :][None, :].astype(jnp.int32)
        second = data_ref[257, :][None, :].astype(jnp.int32)
        ids_ref[blk, 0] = jnp.broadcast_to(first, (8, 128))
        ids_ref[blk, 1] = jnp.broadcast_to(second, (8, 128))
        ids = lax.broadcasted_iota(jnp.int32, (256, 128), 0)
        ohf_ref[:, lanes] = jnp.where(ids == first, 1.0, 0.0).astype(jnp.bfloat16)
        ohs_ref[0:256, lanes] = jnp.where(ids == second, 1.0, 0.0).astype(jnp.bfloat16)
        ohs_ref[256:512, lanes] = jnp.where(ids + 256 == second, 1.0, 0.0).astype(jnp.bfloat16)
        for side in range(2):
            for group in range(4):
                ms = slice(8 * group, 8 * group + 8)
                at = 32 * side + 8 * group
                cell = data_ref[at : at + 8, :].astype(jnp.int32)
                base = 64 + 64 * side + 8 * group
                fx = data_ref[base : base + 8, :]
                fy = data_ref[base + 32 : base + 40, :]
                row = (cell * 37) >> 8
                col = cell - 7 * row
                fx_ref[blk, side, ms, :] = fx
                col_ref[blk, side, ms, :] = col
                for k in range(8):
                    wx_ref[blk, side, k, ms, :] = jnp.where(
                        col == k, 1.0 - fx, jnp.where(col == k - 1, fx, 0.0)
                    )
                    wy_ref[blk, side, k, ms, :] = jnp.where(
                        row == k, 1.0 - fy, jnp.where(row == k - 1, fy, 0.0)
                    )
            tops = load_table(wy_ref, blk, side)
            tops = [[tops[q][g] * goal[g] for g in range(4)] for q in range(8)]
            columns[side].append(spread_rows(tops, load_table(wx_ref, blk, side)))
    spreads = [jnp.concatenate(c, 1) for c in columns]
    at_first = merge3(lax.dot_general(split3(spreads[0]), ohf_ref[...], NT, preferred_element_type=F32))
    at_second = merge3(lax.dot_general(split3(spreads[1]), ohs_ref[...], NT, preferred_element_type=F32))
    own = at_first - at_second[:, :256]
    down = at_second[:, 256:]
    stiff = jnp.concatenate(
        [sum(data_ref[row : row + 1, :] for data_ref in datas) for row in (259, 260)], 1
    )
    if add:
        own = own + before_own[...]
        down = down + before_down[...]
        stiff = stiff + before_stiff[...]
    own_ref[...] = own
    down_ref[...] = down
    stiff_ref[...] = stiff


def stencil_kernel(*refs):
    step = lax.axis_index("tile") & 1
    send_ref, keep_ref = refs[4 * len(BLOCKS) :]
    zero = [jnp.zeros((8, 128), F32)] * 4
    terms = [[], []]
    for h, blocks in enumerate(BLOCKS):
        wx_ref, wy_ref, live_ref = refs[4 * h : 4 * h + 3]
        columns = [[], []]
        for blk in range(blocks):
            live = [live_ref[blk, 8 * g : 8 * g + 8, :] for g in range(4)]
            wy = load_table(wy_ref, blk, 1) + [zero]
            tops = [
                [wy[q][g] * jnp.where(step == 0, wy[q][g], wy[q + 1][g]) * live[g] for g in range(4)]
                for q in range(8)
            ]
            wx = load_table(wx_ref, blk, 1) + [zero]
            for kind in range(2):
                sides = [[wx[p][g] * wx[p + kind][g] for g in range(4)] for p in range(8)]
                columns[kind].append(spread_rows(tops, sides))
        for kind in range(2):
            terms[kind].append(split3(jnp.concatenate(columns[kind], 1)))
    for kind in range(2):
        both = scatter(terms[kind], refs[3 : 4 * len(BLOCKS) : 4])
        keep_ref[kind] = both[:, :256]
        send_ref[kind] = both[:, 256:]


def scatter(terms, hots):
    total = None
    for parts, hot in zip(terms, hots):
        term = lax.dot_general(parts, hot[...], NT, preferred_element_type=F32)
        total = term if total is None else total + term
    return merge3(total)


BLOCKS = (2, 4, 2)
AT = (0, 2, 6)


def columns_of(fields, ids):
    place = ids & 127
    half = ids >> 7
    rows = []
    for q in range(8):
        out = None
        for k in range(2 * len(fields)):
            part = fields[k // 2][8 * q : 8 * q + 8, 128 * (k % 2) : 128 * (k % 2) + 128]
            got = jnp.take_along_axis(part, place, axis=1, mode="promise_in_bounds")
            out = got if out is None else jnp.where(half == k, got, out)
        rows.append(out)
    return rows


def passed(fields, hot_out, tables, side_in, side_out, scale):
    terms = []
    for h, blocks in enumerate(BLOCKS):
        wx_ref, wy_ref, fx_ref, col_ref, _, ids_ref = tables[h][2:8]
        columns = []
        for blk in range(blocks):
            rows = columns_of(fields, ids_ref[blk, side_in])
            got = sample_block(rows, wy_ref, fx_ref, col_ref, blk, side_in)
            gap = scale(h, blk, got)
            tops = load_table(wy_ref, blk, side_out)
            tops = [[tops[q][g] * gap[g] for g in range(4)] for q in range(8)]
            columns.append(spread_rows(tops, load_table(wx_ref, blk, side_out)))
        terms.append(split3(jnp.concatenate(columns, 1)))
    return scatter(terms, hot_out)


def up_kernel(v_ref, *refs):
    tables = [refs[8 * h : 8 * h + 8] for h in range(len(BLOCKS))]
    own_ref, down_ref, gap_ref = refs[8 * len(BLOCKS) :]

    def scale(h, blk, got):
        gap = []
        for g in range(4):
            ms = slice(8 * g, 8 * g + 8)
            gap.append(got[g] * tables[h][6][blk, ms, :])
            gap_ref[blk + AT[h], ms, :] = gap[g]
        return gap

    forces = passed([v_ref[...]], [t[1] for t in tables], tables, 0, 1, scale)
    own_ref[...] = forces[:, :256]
    down_ref[...] = forces[:, 256:]


def up(x, d):
    return pltpu.roll(x, 64 - d, 0)


def dn(x, d):
    return pltpu.roll(x, d, 0)


def banded(v, mine_ref, other_ref):
    first = (lax.axis_index("tile") & 1) == 0
    band = [jnp.where(first, mine_ref[k], other_ref[k]) for k in range(2)]
    band += [jnp.where(first, other_ref[k], mine_ref[k]) for k in range(2)]
    total = band[0] * v
    total = total + band[1] * up(v, 1) + dn(band[1] * v, 1)
    total = total + band[2] * up(v, 8) + dn(band[2] * v, 8)
    total = total + band[3] * up(v, 9) + dn(band[3] * v, 9)
    return total + dn(band[3] * up(v, 8), 1) + dn(band[3] * up(v, 1), 8)


def band_kernel(part_ref, v_ref, mine_ref, other_ref, out_ref):
    out_ref[...] = part_ref[...] + banded(v_ref[...], mine_ref, other_ref)


def down_kernel(
    v_ref, raw_ref, sent_ref, part_ref, gap_ref, stiff_ref, *refs, back
):
    if back:
        prev_ref, mine_ref, other_ref = refs[:3]
        refs = refs[3:]
    tables = [refs[8 * h : 8 * h + 8] for h in range(len(BLOCKS))]
    (out_ref,) = refs[8 * len(BLOCKS) :]
    v = v_ref[...]
    below_v = raw_ref[...] - sent_ref[...]

    def scale(h, blk, got):
        return [
            gap_ref[blk + AT[h], 8 * g : 8 * g + 8, :] - got[g] * tables[h][6][blk, 8 * g : 8 * g + 8, :]
            for g in range(4)
        ]

    forces = passed([v, below_v], [t[0] for t in tables], tables, 1, 0, scale)
    node = lax.broadcasted_iota(jnp.int32, (64, 256), 0)
    right = jnp.where((node & 7) < 7, up(v, 1) - v, 0.0)
    below = jnp.where(node < 56, up(v, 8) - v, 0.0)
    bend = (dn(right, 1) - right) + (dn(below, 8) - below)
    total = forces - part_ref[...] + (stiff_ref[...] * SCALE) * bend + ((DAMPING - SHIFT) * SCALE) * v
    if back:
        total = total + banded(v, mine_ref, other_ref)
        total = total - BACK * prev_ref[...]
    out_ref[...] = total


def two_sum(a, b):
    s = a + b
    t = s - a
    return s, (a - (s - t)) + (b - t)


def halves(a):
    c = 4097.0 * a
    high = c - (c - a)
    return high, a - high


def two_prod(a, b):
    return split_prod(a, b, halves(a), halves(b))


def split_prod(a, b, a_halves, b_halves):
    p = a * b
    ah, al = a_halves
    bh, bl = b_halves
    return p, ((ah * bh - p) + ah * bl + al * bh) + al * bl


def quick(a, b):
    s = a + b
    return s, b - (s - a)


def dd_add(x, y):
    s, e = two_sum(x[0], y[0])
    return quick(s, e + (x[1] + y[1]))


def dd_mul(x, y):
    p, e = two_prod(x[0], y[0])
    return quick(p, e + (x[0] * y[1] + x[1] * y[0]))


def dd_neg(x):
    return (-x[0], -x[1])


def dd_div(x, y):
    q = x[0] / y[0]
    rest = dd_add(x, dd_neg(dd_mul(y, (q, jnp.zeros_like(q)))))
    return quick(q, rest[0] / y[0])


def dots(fields, pairs):
    sub = lax.broadcasted_iota(jnp.int32, (16, 128), 0)
    high = jnp.zeros((16, 128), F32)
    low = jnp.zeros((16, 128), F32)
    cut = [halves(f) for f in fields]
    for i, j in pairs:
        acc = split_prod(fields[i], fields[j], cut[i], cut[j])
        acc = dd_add((acc[0][:, :128], acc[1][:, :128]), (acc[0][:, 128:], acc[1][:, 128:]))
        n = 64
        while n > 8:
            n //= 2
            acc = dd_add((acc[0][:n], acc[1][:n]), (acc[0][n:], acc[1][n:]))
        for d in (4, 2, 1):
            acc = dd_add(acc, (pltpu.roll(acc[0], d, 0), pltpu.roll(acc[1], d, 0)))
        wide = [jnp.concatenate([a, a], 0) for a in acc]
        here = sub == PAIRS.index((i, j))
        high = jnp.where(here, wide[0], high)
        low = jnp.where(here, wide[1], low)
    return high, low


def dots_kernel(v0, v1, v2, v3, high_ref, low_ref):
    high, low = dots([r[...] for r in (v0, v1, v2, v3)], [p for p in PAIRS if p[1] < 4])
    high_ref[...] = high
    low_ref[...] = low


def slice_kernel(v0, v1, v2, v3, v4, even_ref, odd_ref):
    fields = [r[...] for r in (v0, v1, v2, v3, v4)]
    y = lax.axis_index("tile") >> 1
    low = lax.broadcasted_iota(jnp.int32, (64, 128), 1) < 64
    for k in range(3):
        left = jnp.where(y >= 2, fields[2 * k][:, 128:], fields[2 * k][:, :128])
        if k < 2:
            right = jnp.where(y >= 2, fields[2 * k + 1][:, 128:], fields[2 * k + 1][:, :128])
        else:
            right = jnp.zeros((64, 128), F32)
        even_ref[k] = jnp.where(low, left, pltpu.roll(right, 64, 1))
        odd_ref[k] = jnp.where(low, pltpu.roll(left, 64, 1), right)


def last_kernel(high_ref, low_ref, v0, v1, v2, v3, v4, out_ref):
    sub = lax.broadcasted_iota(jnp.int32, (16, 128), 0)
    lane = lax.broadcasted_iota(jnp.int32, (16, 128), 1)
    high, low = dots([r[...] for r in (v0, v1, v2, v3, v4)], [p for p in PAIRS if p[1] == 4])
    acc = (high + high_ref[...], low + low_ref[...])
    for d in (64, 32, 16, 8, 4, 2, 1):
        acc = dd_add(acc, (pltpu.roll(acc[0], d, 1), pltpu.roll(acc[1], d, 1)))
    row = jnp.where(lane == sub, acc[0], 0.0) + jnp.where(lane == sub + 16, acc[1], 0.0)
    out_ref[...] = jnp.sum(row, 0, keepdims=True)


def finish_kernel(gram_ref, even_ref, odd_ref, mine_ref, other_ref):
    rows = gram_ref[...]
    acc = dd_add((rows, pltpu.roll(rows, 112, 1)), (pltpu.roll(rows, 96, 1), pltpu.roll(rows, 80, 1)))
    n = 32
    while n > 8:
        n //= 2
        acc = dd_add((acc[0][:n], acc[1][:n]), (acc[0][n:], acc[1][n:]))
    for d in (4, 2, 1):
        acc = dd_add(acc, (pltpu.roll(acc[0], d, 0), pltpu.roll(acc[1], d, 0)))
    gram = {}
    for k, (i, j) in enumerate(PAIRS):
        pair = tuple(jnp.broadcast_to(a[:, k : k + 1], (8, 128)) for a in acc)
        gram[(i, j)] = pair
        gram[(j, i)] = pair
    zero = jnp.zeros((8, 128), F32)
    const = lambda c: (jnp.full((8, 128), c, F32), zero)

    def tree(terms):
        while len(terms) > 1:
            terms = [dd_add(*terms[k : k + 2]) if k + 1 < len(terms) else terms[k] for k in range(0, len(terms), 2)]
        return terms[0]

    def form(a, b):
        return tree([dd_mul(bj, tree([dd_mul(ai, gram[(i, j)]) for i, ai in enumerate(a)])) for j, bj in enumerate(b)])

    def apply(p):
        out = [const(0.0) for _ in range(len(p) + 1)]
        for k, c in enumerate(p):
            out[k + 1] = dd_add(out[k + 1], (c[0] * 128.0, c[1] * 128.0))
            out[k] = dd_add(out[k], dd_mul(c, const(SHIFT)))
            if k >= 1:
                out[k - 1] = dd_add(out[k - 1], dd_mul(c, const(BACK * 128.0)))
        return out

    def axpy(a, x, y):
        out = []
        for k in range(max(len(x), len(y))):
            if k >= len(x):
                out.append(y[k])
            elif k >= len(y):
                out.append(dd_mul(a, x[k]))
            else:
                out.append(dd_add(y[k], dd_mul(a, x[k])))
        return out

    res = [const(1.0)]
    direc = [const(1.0)]
    sol = []
    norm = gram[(0, 0)]
    for it in range(ITERS):
        image = apply(direc)
        step = dd_div(norm, form(direc, image))
        sol = axpy(step, direc, sol)
        res = axpy(dd_neg(step), image, res)
        if it < ITERS - 1:
            new = form(res, res)
            direc = axpy(dd_div(new, norm), direc, res)
            norm = new
    lane = lax.broadcasted_iota(jnp.int32, (64, 128), 1)

    odd = ((lax.axis_index("tile") >> 1) & 1) == 1

    def combine(coefs):
        total = jnp.zeros((64, 128), F32)
        flat = [c[0][0:1, 0:1] for c in coefs] + [jnp.zeros((1, 1), F32)] * (6 - len(coefs))
        for k in range(3):
            total = total + jnp.where(lane < 64, flat[2 * k], flat[2 * k + 1]) * jnp.where(odd, odd_ref[k], even_ref[k])
        return total + pltpu.roll(total, 64, 1)

    core = lax.axis_index("tile") & 1
    want = lax.broadcasted_iota(jnp.int32, (64, 128), 0)
    want = jnp.where(want < 32, want + 32 * core, want - 32 * core)
    pick = jnp.where(lane == want, 1.0, 0.0).astype(jnp.bfloat16)
    for k, coefs in enumerate((sol, res)):
        parts = lax.dot_general(pick, split3(combine(coefs)), NT, preferred_element_type=F32)
        both = parts[:, :64] + (parts[:, 64:128] + parts[:, 128:192])
        mine_ref[k] = both[:32]
        other_ref[k] = both[32:]


def call(kernel, outs, n_in, scratch=(), us=2.0, hbm=0, grant=8):
    return pl.pallas_call(
        kernel,
        out_shape=[jax.ShapeDtypeStruct(s, d) for s, d in outs],
        in_specs=[VMEM] * (n_in - hbm)
        + [pl.BlockSpec(memory_space=pl.ANY)] * hbm,
        out_specs=[VMEM] * len(outs),
        scratch_shapes=list(scratch),
        compiler_params=pltpu.CompilerParams(vmem_limit_bytes=grant * 1024 * 1024),
        cost_estimate=pl.CostEstimate(flops=int(us * 1e9), bytes_accessed=1 << 18, transcendentals=0),
    )


ROW = 4
CHIPS = 4


def seat(section, y, sections):
    row, col = divmod(section, ROW)
    col = col if row % 2 == 0 else ROW - 1 - col
    row = row if y % 2 == 0 else sections // ROW - 1 - row
    return row * ROW + col


def shifted(block, distance):
    sections = lax.axis_size("sec")
    route = []
    for section in range(sections):
        there = (section + distance) % sections
        crosses = (section < sections // 2) != (there < sections // 2)
        for y in range(CHIPS):
            to = y ^ 1 if crosses else y
            for core in range(2):
                route.append(
                    (seat(section, y, sections) * 8 + 2 * y + core, seat(there, to, sections) * 8 + 2 * to + core)
                )
    return lax.ppermute(block, ("sec", "tile"), route)


def swapped(block):
    return lax.ppermute(block, "tile", [(i, i ^ 1) for i in range(8)])


def dealt(block, step):
    sections = lax.axis_size("sec")
    route = []
    for section in range(sections):
        for y in range(CHIPS):
            to = (y + step) % CHIPS
            for core in range(2):
                route.append((section * 8 + 2 * y + core, seat(section, to, sections) * 8 + 2 * to + core))
    return lax.ppermute(block, ("sec", "tile"), route)


def returned(block, up):
    sections = lax.axis_size("sec")
    route = []
    for section in range(sections):
        for y in range(CHIPS):
            for core in range(2):
                if y % 2 == 0:
                    route.append((seat(section, y, sections) * 8 + 2 * y + core, section * 8 + 2 * (y + up) + core))
                else:
                    route.append((section * 8 + 2 * y + core, section * 8 + 2 * (y - up) + core))
    return lax.ppermute(block, ("sec", "tile"), route)


def on_device(
    ov_first, ov_second, match_count, cell_first, cell_second, frac_first, frac_second, target, stiffness
):
    tile = lax.axis_index("tile")
    core = tile % 2
    sections = lax.axis_size("sec")
    dma = pltpu.SemaphoreType.DMA
    packed = call(
        functools.partial(pack_kernel, sections=sections),
        [((264, 128), F32)],
        9,
        [
            pltpu.VMEM((3, 1, 128), jnp.int32),
            pltpu.VMEM((1, 32), F32),
            pltpu.VMEM((2, 32, 128), jnp.int32),
            dma((12,)),
        ],
        hbm=9,
        grant=60,
    )(
        ov_first.reshape(1, 128),
        ov_second.reshape(1, 128),
        match_count.reshape(1, 128),
        cell_first,
        cell_second,
        frac_first,
        frac_second,
        target,
        stiffness.reshape(1, 32),
    )[0]
    far = [dealt(packed, step) for step in (3, 2, 1, 0)]
    field = ((64, 256), F32)
    bf16 = jnp.bfloat16
    groups = []
    sums = ()
    for k, blocks in enumerate(BLOCKS):
        if k == 0:
            datas = far[:2]
            near = [swapped(x) for x in datas]
        elif k == 1:
            late, sums = lax.optimization_barrier((far[2:], sums))
            datas = near + late
            near = [swapped(x) for x in late]
        else:
            datas = near
        outs = call(
            functools.partial(tables_kernel, blocks=blocks, add=len(sums) > 0),
            [
                ((blocks, 2, 8, 32, 128), F32),
                ((blocks, 2, 8, 32, 128), F32),
                ((blocks, 2, 32, 128), F32),
                ((blocks, 2, 32, 128), jnp.int32),
                ((blocks, 32, 128), F32),
                ((256, 128 * blocks), bf16),
                ((512, 128 * blocks), bf16),
                ((blocks, 2, 8, 128), jnp.int32),
                field,
                field,
                ((1, 256), F32),
            ],
            blocks + len(sums),
            us=0.4 * blocks,
        )(*datas, *sums)
        groups.append(outs[:8])
        sums = tuple(outs[8:])
    own, down, stiff = sums
    parts = [x for g in groups for x in (g[0], g[1], g[4], g[6])]
    above = shifted(down, -1)
    raw = shifted(own, 1)
    send, keep = call(stencil_kernel, [((2, 64, 256), F32)] * 2, len(parts), us=4.0)(*parts)
    above, send = lax.optimization_barrier((above, send))
    got = shifted(send, -1)
    fields = [own - above]
    tables = []
    for wx, wy, fx, col, live, ohf, ohs, ids in groups:
        tables += [ohf, ohs, wx, wy, fx, col, live, ids]
    for k in range(ITERS):
        v = fields[-1]
        sent = down
        part, down, gap = call(up_kernel, [field, field, ((8, 32, 128), F32)], 1 + len(tables))(v, *tables)
        above = shifted(down, -1)
        more = (fields[k - 1], mine, other) if k else ()
        partial = call(functools.partial(down_kernel, back=k > 0), [field], 6 + len(more) + len(tables))(
            v, raw, sent, part, gap, stiff, *more, *tables
        )[0]
        if k == 0:
            mine = keep + got
            other = swapped(mine)
            partial = call(band_kernel, [field], 4, us=0.3)(partial, v, mine, other)[0]
        if k < ITERS - 1:
            raw = shifted(partial, 1)
        fields.append(partial - above)
    begun = call(dots_kernel, [((16, 128), F32)] * 2, 4, us=1.0)(*fields[:4])
    even, odd = call(slice_kernel, [((3, 64, 128), F32)] * 2, 5, us=0.1)(*fields)
    even = returned(even, 0)
    odd = returned(odd, 1)
    row = call(last_kernel, [((1, 128), F32)], 7, us=1.0)(*begun, *fields)[0]
    row = row + jnp.roll(swapped(row), 32, 1)
    gram = lax.all_to_all(jnp.broadcast_to(row, (32, 128)), "sec", 0, 0, tiled=True)
    mine, other = call(finish_kernel, [((2, 32, 64), F32), ((2, 32, 64), F32)], 3)(gram, even, odd)
    other = swapped(other)
    first = jnp.where(core == 0, mine, other)
    last = jnp.where(core == 0, other, mine)
    out = jnp.concatenate([first, last], 2)[:, :, None, :]
    return (out[0], out[1])


def solution(mesh):
    in_specs = (
        P(("sec", "tile")),
        P(("sec", "tile")),
        P(("sec", "tile")),
        P(None, ("sec", "tile")),
        P(None, ("sec", "tile")),
        P(None, None, ("sec", "tile")),
        P(None, None, ("sec", "tile")),
        P(None, None, ("sec", "tile")),
        P("tile", "sec"),
    )
    out_specs = (P("tile", "sec", None), P("tile", "sec", None))
    return jax.shard_map(
        on_device, mesh=mesh, in_specs=in_specs, out_specs=out_specs, check_vma=False
    )
```
